32 devices in a mesh: grp: 2 (over y), batch: 8 (over z, x), tensor: 2 (over core).
Axes of the slice: x: 2, y: 2, z: 4, core: 2. Of those that a mesh axis runs over, the one named last changes fastest.
Arguments:
- init_cache: bfloat16 [16, 2, 64, 3072], P(('grp', 'batch'), None, None, 'tensor'), parts along dimension 0, may hold values from -6 to 6
- memory: bfloat16 [16, 2, 64, 3072], P(('grp', 'batch'), None, None, 'tensor'), parts along dimension 0, may hold values from -6 to 6
- queries: bfloat16 [1, 16, 2, 3072], P(None, ('grp', 'batch'), None, 'tensor'), parts along dimension 1, may hold values from -600 to 600
- new_kv: bfloat16 [1, 16, 2, 3072], P(None, ('grp', 'batch'), None, 'tensor'), parts along dimension 1, may hold values from -6 to 6
- residual: bfloat16 [1, 16, 6144], P(None, 'grp', 'batch'), parts along dimension 1, may hold values from -6 to 6
- out_weight: bfloat16 [2, 3072, 6144], P(None, 'tensor', 'batch'), may hold values from -0.078125 to 0.078125
- up_weight: bfloat16 [6144, 24576], P(None, ('batch', 'tensor')), may hold values from -0.078125 to 0.078125
- down_weight: bfloat16 [24576, 6144], P('batch', 'tensor'), may hold values from -0.0390625 to 0.0390625
- parents: int32 [1, 16], P(None, 'grp'), parts along dimension 1, may hold values from 0 to 7
- lengths: int32 [2], P('grp'), parts along dimension 0, may hold values from 1 to 63
Outputs:
- hidden: bfloat16 [1, 16, 6144], P(None, 'grp', 'batch'), parts along dimension 1
- ffn_out: bfloat16 [1, 16, 6144], P(None, ('grp', 'batch'), 'tensor'), parts along dimension 1
- final_cache: bfloat16 [16, 2, 64, 3072], P(('grp', 'batch'), None, None, 'tensor'), parts along dimension 0
The draws below stay inside these ranges and needn't reach their ends.
There are 2 independent parts, one for each index of `grp`. The reference program is written for one: setup_inputs(seed, part) draws one part's arguments, and reference() takes and returns one part's arrays. A program takes and returns all parts, laid end to end along the dimension named above; an argument that names none is the same for every part. Nothing has to cross between parts.
Inputs may be any that keep to these rules, and one draw needn't show every extreme that they name: parents[s, b + r] is the beam of request r whose cache beam b continues at step s.
All inputs are finite; a program needn't handle non-finite values.
Results may differ from the reference program's by a relative error of at most 0.006.
Values may be sent and summed in bfloat16 or wider, within the bound.
No kernel may reach another device: no remote copies, remote signals or barrier semaphores. Data moves between devices by JAX's collectives and lax.ppermute only.
A program may use at most 128 MiB of HBM per device.

```python
import math
import jax
import jax.numpy as jnp
from jax import lax

D = 6144
HEADS = 24
HD = 128
FF = 24576
BEAMS = 8
STEPS = 1
CACHE = 64
FB = 64
HF = 3072
ROWS = 8
REQ = 1


def draw_queries(key, part):
    base = jax.random.truncated_normal(key, -6.0, 6.0, (STEPS, ROWS, 2, HF), jnp.float32)
    return base.astype(jnp.bfloat16)


def with_ends(result, stream_key, least, largest):
    longest = result.shape.index(max(result.shape))
    spots = []
    for shift in (0, 1):
        where = [jax.random.randint(jax.random.fold_in(stream_key, axis), (), 0, length) for axis, length in enumerate(result.shape)]
        where[longest] = (where[longest] + shift) % result.shape[longest]
        spots.append(tuple(where))
    return result.at[spots[0]].set(least).at[spots[1]].set(largest)


def block_scale(stream_key, dims, split, least, largest):
    level, own = 1.0, jax.random.fold_in(stream_key, 6)
    for dim, parts in split:
        draws = jnp.exp(jax.random.uniform(jax.random.fold_in(own, dim), (parts,), jnp.float32, least / len(split), largest / len(split)))
        level = level * jnp.repeat(draws, dims[dim] // parts).reshape([-1 if axis == dim else 1 for axis in range(len(dims))])
    return level


def scatter_about(rng, dims, deviation, most, shards=(), kind=jnp.bfloat16):
    drawn = deviation * jax.random.normal(rng, dims, jnp.float32)
    if shards:
        drawn = drawn * block_scale(rng, dims, shards, -0.22, 0.18)
    return jnp.clip(drawn, -most, most).astype(kind)


def setup_inputs(seed: int = 0, part: int = 0) -> dict:
    key_list = jax.random.split(jax.random.key(seed), 11)
    part_splits = jax.random.split(jax.random.fold_in(key_list[10], part), 11)
    init_cache = scatter_about(part_splits[0], (ROWS, 2, CACHE, HF), 1.0, 6.0, ((0, 8), (3, 2)))
    memory = scatter_about(part_splits[1], (ROWS, 2, FB, HF), 1.0, 6.0, ((0, 8), (3, 2)))
    queries = draw_queries(jax.random.fold_in(jax.random.fold_in(key_list[10], part), 71), part)
    new_kv = scatter_about(part_splits[3], (STEPS, ROWS, 2, HF), 1.0, 6.0, ((1, 8), (3, 2)))
    residual = scatter_about(part_splits[4], (STEPS, ROWS, D), 1.0, 6.0, ((2, 8),))
    out_weight = scatter_about(key_list[5], (2, HF, D), (2 * HF) ** -0.5, 0.078125, ((1, 2), (2, 8)))
    up_weight = scatter_about(key_list[6], (D, FF), D ** -0.5, 0.078125, ((1, 16),))
    down_weight = scatter_about(key_list[7], (FF, D), FF ** -0.5, 0.0390625, ((0, 8), (1, 2)))
    parents = with_ends(jax.random.randint(part_splits[8], (STEPS, ROWS), 0, BEAMS), jax.random.fold_in(part_splits[8], 1), 0, BEAMS - 1).astype(jnp.int32)
    lengths = jax.random.randint(part_splits[9], (REQ,), 1, CACHE - STEPS + 1).astype(jnp.int32)
    return {"init_cache": init_cache, "memory": memory, "queries": queries, "new_kv": new_kv, "residual": residual, "out_weight": out_weight, "up_weight": up_weight, "down_weight": down_weight, "parents": parents, "lengths": lengths}


def reference(init_cache, memory, queries, new_kv, residual, out_weight, up_weight, down_weight, parents, lengths):
    highest = lax.Precision.HIGHEST
    row_request = jnp.arange(ROWS, dtype=jnp.int32) % REQ
    slots = jnp.arange(CACHE, dtype=jnp.int32)
    row_length = lengths[row_request]
    mem = memory.astype(jnp.float32).reshape(BEAMS, REQ, 2, FB, HEADS, HD)
    mem_keys = mem[:, :, 0].transpose(1, 0, 2, 3, 4).reshape(REQ, BEAMS * FB, HEADS, HD)
    mem_values = mem[:, :, 1].transpose(1, 0, 2, 3, 4).reshape(REQ, BEAMS * FB, HEADS, HD)
    cache = init_cache
    hidden_list = []
    ffn_list = []
    for step in range(STEPS):
        source = (parents[step] * REQ + row_request).astype(jnp.int32)
        cache = cache[source]
        write = slots[None, :] == (row_length + step)[:, None]
        cache = jnp.where(write[:, None, :, None], new_kv[step][:, :, None, :], cache)
        query_all = queries[step].astype(jnp.float32)
        self_query = query_all[:, 0].reshape(ROWS, HEADS, HD)
        keys = cache[:, 0].astype(jnp.float32).reshape(ROWS, CACHE, HEADS, HD)
        values = cache[:, 1].astype(jnp.float32).reshape(ROWS, CACHE, HEADS, HD)
        scores = jnp.einsum('rhd,rchd->rhc', self_query, keys, precision=highest) / math.sqrt(HD)
        valid = (slots[None, :] <= (row_length + step)[:, None])[:, None, :]
        masked = jnp.where(valid, scores, -1e+30)
        peak = lax.optimization_barrier(jnp.max(masked, axis=-1, keepdims=True))
        weights = jnp.where(valid, jnp.exp(masked - peak), 0.0)
        total = lax.optimization_barrier(jnp.sum(weights, axis=-1))
        weighted = jnp.einsum('rhc,rchd->rhd', weights, values, precision=highest)
        self_out = (weighted / total[..., None]).reshape(ROWS, HF).astype(jnp.bfloat16)
        cross_query = query_all[:, 1].reshape(BEAMS, REQ, HEADS, HD)
        scores = jnp.einsum('brhd,rfhd->brhf', cross_query, mem_keys, precision=highest) / math.sqrt(HD)
        peak = lax.optimization_barrier(jnp.max(scores, axis=-1, keepdims=True))
        weights = jnp.exp(scores - peak)
        total = lax.optimization_barrier(jnp.sum(weights, axis=-1))
        weighted = jnp.einsum('brhf,rfhd->brhd', weights, mem_values, precision=highest)
        cross_out = (weighted / total[..., None]).reshape(ROWS, HF).astype(jnp.bfloat16)
        attended = jnp.stack([self_out, cross_out], axis=1).reshape(ROWS, 2 * HF)
        projected = jnp.dot(attended, out_weight.reshape(2 * HF, D), preferred_element_type=jnp.float32)
        hidden = (residual[step].astype(jnp.float32) + projected).astype(jnp.bfloat16)
        pre_act = jnp.dot(hidden, up_weight, preferred_element_type=jnp.float32)
        activation = jax.nn.gelu(pre_act, approximate=False).astype(jnp.bfloat16)
        ffn_row = jnp.dot(activation, down_weight, preferred_element_type=jnp.float32).astype(jnp.bfloat16)
        hidden_list.append(hidden)
        ffn_list.append(ffn_row)
    return (jnp.stack(hidden_list), jnp.stack(ffn_list), cache)
```

```python
import math

import jax
import jax.numpy as jnp
from jax import lax
from jax.sharding import PartitionSpec as P

HD = 128
BEAMS = 8
LOW = -1e30


def body(
    init_cache,
    memory,
    queries,
    new_kv,
    residual,
    out_weight,
    up_weight,
    down_weight,
    parents,
    lengths,
):
    devices = lax.axis_size("batch")
    stride = devices // BEAMS
    position = lax.axis_index("batch")
    own_beam = position // stride
    request = position % stride
    width = queries.shape[-1]
    heads = width // HD
    cache_len = init_cache.shape[2]
    rows = parents.shape[1]
    groups = None
    if stride > 1:
        groups = [[b * stride + r for b in range(BEAMS)] for r in range(stride)]

    def swap(value):
        return lax.all_to_all(value, "batch", 0, 0, axis_index_groups=groups, tiled=True)

    def swap_all(value):
        return lax.all_to_all(value, "batch", 0, 0, tiled=True)

    def gather_all(value):
        return swap_all(jnp.broadcast_to(value[None], (devices,) + value.shape))

    request_ids = jnp.arange(stride, dtype=jnp.int32)
    length = jnp.sum(jnp.where(request_ids == request, lengths, 0))
    grouped = parents.reshape(BEAMS, stride)
    parent = jnp.sum(jnp.where(request_ids[None, :] == request, grouped, 0), axis=1)
    slots = jnp.arange(cache_len, dtype=jnp.int32)
    scale = 1.0 / math.sqrt(HD)

    own_query = queries[0, 0]
    query = swap(jnp.broadcast_to(own_query[None], (BEAMS, 2, width)))
    query = query.reshape(BEAMS, 2, heads, HD)

    def partial(q, kv, valid):
        keys = kv[0].reshape(-1, heads, HD)
        values = kv[1].reshape(-1, heads, HD)
        scores = jnp.einsum("nhd,chd->nhc", q, keys, preferred_element_type=jnp.float32) * scale
        if valid is not None:
            scores = jnp.where(valid[:, None, :], scores, LOW)
        peak = jnp.max(scores, axis=-1)
        weights = jnp.exp(scores - peak[..., None])
        if valid is not None:
            weights = jnp.where(valid[:, None, :], weights, 0.0)
        total = jnp.sum(weights, axis=-1)
        high = weights.astype(jnp.bfloat16)
        low = (weights - high.astype(jnp.float32)).astype(jnp.bfloat16)
        both = jnp.einsum(
            "nhc,chd->nhd", jnp.concatenate([high, low]), values, preferred_element_type=jnp.float32
        )
        return both[:BEAMS] + both[BEAMS:], peak, total

    valid = (slots < length)[None, :] & (parent == own_beam)[:, None]
    ws, ps, ts = partial(query[:, 0], init_cache[0], valid)
    wc, pc, tc = partial(query[:, 1], memory[0], None)
    packed = jnp.concatenate(
        [
            ws.reshape(BEAMS, width),
            wc.reshape(BEAMS, width),
            ps,
            pc,
            ts,
            tc,
        ],
        axis=1,
    )
    got = swap(packed)
    both = 2 * heads
    weighted = got[:, : 2 * width].reshape(BEAMS, both, HD)
    peaks = got[:, 2 * width : 2 * width + both]
    totals = got[:, 2 * width + both :]

    new_score = jnp.sum(
        own_query[0].astype(jnp.float32).reshape(heads, HD)
        * new_kv[0, 0, 0].astype(jnp.float32).reshape(heads, HD),
        axis=1,
    ) * scale
    new_peak = jnp.concatenate([new_score, jnp.full((heads,), LOW, jnp.float32)])
    new_total = jnp.concatenate([jnp.ones((heads,), jnp.float32), jnp.zeros((heads,), jnp.float32)])
    new_value = jnp.concatenate(
        [new_kv[0, 0, 1].astype(jnp.float32), jnp.zeros((width,), jnp.float32)]
    ).reshape(both, HD)
    top = jnp.maximum(jnp.max(peaks, axis=0), new_peak)
    factors = jnp.exp(peaks - top[None])
    new_factor = jnp.exp(new_peak - top) * new_total
    denom = jnp.sum(totals * factors, axis=0) + new_factor
    numer = jnp.sum(weighted * factors[..., None], axis=0) + new_value * new_factor[:, None]
    attended = (numer / denom[:, None]).astype(jnp.bfloat16).reshape(2 * width)

    projected = lax.psum(
        jnp.dot(
            gather_all(attended),
            out_weight.reshape(2 * width, -1),
            preferred_element_type=jnp.float32,
        ),
        "tensor",
    )
    hidden = (residual[0].astype(jnp.float32) + projected).astype(jnp.bfloat16)
    wide = jnp.swapaxes(gather_all(hidden), 0, 1).reshape(rows, -1)
    pre_act = jnp.dot(wide, up_weight, preferred_element_type=jnp.float32)
    activation = jax.nn.gelu(pre_act, approximate=False).astype(jnp.bfloat16)
    joined = lax.all_gather(activation, "tensor", axis=1, tiled=True)
    part = jnp.dot(joined, down_weight, preferred_element_type=jnp.float32)
    ffn_row = jnp.sum(swap_all(part), axis=0, keepdims=True).astype(jnp.bfloat16)

    pieces = init_cache.reshape(BEAMS, 2 * cache_len // BEAMS, width)
    mine = swap(pieces)
    chosen = jnp.stack([lax.dynamic_index_in_dim(mine, parent[b], 0, False) for b in range(BEAMS)])
    cache = swap(chosen).reshape(2, cache_len, width)
    cache = jnp.where((slots == length)[None, :, None], new_kv[0, 0][:, None, :], cache)
    return (hidden[None], ffn_row[None], cache[None])


def solution(mesh):
    placed = (
        P(("grp", "batch"), None, None, "tensor"),
        P(("grp", "batch"), None, None, "tensor"),
        P(None, ("grp", "batch"), None, "tensor"),
        P(None, ("grp", "batch"), None, "tensor"),
        P(None, "grp", "batch"),
        P(None, "tensor", "batch"),
        P(None, ("batch", "tensor")),
        P("batch", "tensor"),
        P(None, "grp"),
        P("grp"),
    )
    return jax.shard_map(
        body,
        mesh=mesh,
        in_specs=placed,
        out_specs=(
            P(None, "grp", "batch"),
            P(None, ("grp", "batch"), "tensor"),
            P(("grp", "batch"), None, None, "tensor"),
        ),
        check_vma=False,
    )
```

```python
import math

import jax
import jax.numpy as jnp
from jax import lax
from jax.experimental import pallas as pl
from jax.experimental.pallas import tpu as pltpu
from jax.sharding import PartitionSpec as P

HD = 128
BEAMS = 8
LOW = -1e30


def doubling(value, position, first, last):
    total = lax.axis_size("batch")
    buffer = value[None]
    bit = first
    while bit < last:
        pairs = [(i, i ^ bit) for i in range(total)]
        other = lax.ppermute(buffer, "batch", pairs)
        upper = (position // bit) % 2 == 1
        buffer = jnp.concatenate([jnp.where(upper, other, buffer), jnp.where(upper, buffer, other)])
        bit *= 2
    return buffer


def place_kernel(parent_ref, length_ref, row_ref, new_ref, out_ref):
    slots = lax.broadcasted_iota(jnp.int32, row_ref.shape[2:], 0)
    for kind in range(2):
        old = row_ref[0, kind]
        new = jnp.broadcast_to(new_ref[kind : kind + 1, :], old.shape)
        out_ref[kind] = jnp.where(slots == length_ref[0], new, old)


def place(gathered, new_kv, parent, length):
    _, kinds, positions, width = gathered.shape
    return pl.pallas_call(
        place_kernel,
        out_shape=jax.ShapeDtypeStruct((kinds, positions, width), gathered.dtype),
        grid_spec=pltpu.PrefetchScalarGridSpec(
            num_scalar_prefetch=2,
            grid=(1,),
            in_specs=[
                pl.BlockSpec((1, kinds, positions, width), lambda i, p, n: (p[0], 0, 0, 0)),
                pl.BlockSpec((kinds, width), lambda i, p, n: (0, 0)),
            ],
            out_specs=pl.BlockSpec((kinds, positions, width), lambda i, p, n: (0, 0, 0)),
        ),
        compiler_params=pltpu.CompilerParams(vmem_limit_bytes=8 * 1024 * 1024),
    )(parent, length, gathered, new_kv)


def body(
    init_cache,
    memory,
    queries,
    new_kv,
    residual,
    out_weight,
    up_weight,
    down_weight,
    parents,
    lengths,
):
    devices = lax.axis_size("batch")
    stride = devices // BEAMS
    position = lax.axis_index("batch")
    own_beam = position // stride
    request = position % stride
    width = queries.shape[-1]
    heads = width // HD
    cache_len = init_cache.shape[2]
    rows = parents.shape[1]
    groups = None
    if stride > 1:
        groups = [[b * stride + r for b in range(BEAMS)] for r in range(stride)]

    def swap(value):
        return lax.all_to_all(value, "batch", 0, 0, axis_index_groups=groups, tiled=True)

    def swap_all(value):
        return lax.all_to_all(value, "batch", 0, 0, tiled=True)

    def gather_all(value):
        return doubling(value, position, 1, devices)

    request_ids = jnp.arange(stride, dtype=jnp.int32)
    length = jnp.sum(jnp.where(request_ids == request, lengths, 0))
    grouped = parents.reshape(BEAMS, stride)
    parent = jnp.sum(jnp.where(request_ids[None, :] == request, grouped, 0), axis=1)
    slots = jnp.arange(cache_len, dtype=jnp.int32)
    scale = 1.0 / math.sqrt(HD)

    own_query = queries[0, 0]
    query = doubling(own_query, position, stride, devices)
    query = query.reshape(BEAMS, 2, heads, HD)

    def partial(q, kv, valid):
        keys = kv[0].reshape(-1, heads, HD)
        values = kv[1].reshape(-1, heads, HD)
        scores = jnp.einsum("nhd,chd->nhc", q, keys, preferred_element_type=jnp.float32) * scale
        if valid is not None:
            scores = jnp.where(valid[:, None, :], scores, LOW)
        peak = jnp.max(scores, axis=-1)
        weights = jnp.exp(scores - peak[..., None])
        if valid is not None:
            weights = jnp.where(valid[:, None, :], weights, 0.0)
        total = jnp.sum(weights, axis=-1)
        high = weights.astype(jnp.bfloat16)
        low = (weights - high.astype(jnp.float32)).astype(jnp.bfloat16)
        both = jnp.einsum(
            "nhc,chd->nhd", jnp.concatenate([high, low]), values, preferred_element_type=jnp.float32
        )
        return both[:BEAMS] + both[BEAMS:], peak, total

    valid = (slots < length)[None, :] & (parent == own_beam)[:, None]
    ws, ps, ts = partial(query[:, 0], init_cache[0], valid)
    wc, pc, tc = partial(query[:, 1], memory[0], None)
    packed = jnp.concatenate(
        [
            ws.reshape(BEAMS, width),
            wc.reshape(BEAMS, width),
            ps,
            pc,
            ts,
            tc,
        ],
        axis=1,
    )
    got = swap(packed)
    both = 2 * heads
    weighted = got[:, : 2 * width].reshape(BEAMS, both, HD)
    peaks = got[:, 2 * width : 2 * width + both]
    totals = got[:, 2 * width + both :]

    new_score = jnp.sum(
        own_query[0].astype(jnp.float32).reshape(heads, HD)
        * new_kv[0, 0, 0].astype(jnp.float32).reshape(heads, HD),
        axis=1,
    ) * scale
    new_peak = jnp.concatenate([new_score, jnp.full((heads,), LOW, jnp.float32)])
    new_total = jnp.concatenate([jnp.ones((heads,), jnp.float32), jnp.zeros((heads,), jnp.float32)])
    new_value = jnp.concatenate(
        [new_kv[0, 0, 1].astype(jnp.float32), jnp.zeros((width,), jnp.float32)]
    ).reshape(both, HD)
    top = jnp.maximum(jnp.max(peaks, axis=0), new_peak)
    factors = jnp.exp(peaks - top[None])
    new_factor = jnp.exp(new_peak - top) * new_total
    denom = jnp.sum(totals * factors, axis=0) + new_factor
    numer = jnp.sum(weighted * factors[..., None], axis=0) + new_value * new_factor[:, None]
    attended = (numer / denom[:, None]).astype(jnp.bfloat16).reshape(2 * width)

    projected = lax.psum(
        jnp.dot(
            gather_all(attended),
            out_weight.reshape(2 * width, -1),
            preferred_element_type=jnp.float32,
        ),
        "tensor",
    )
    hidden = (residual[0].astype(jnp.float32) + projected).astype(jnp.bfloat16)
    wide = jnp.swapaxes(gather_all(hidden), 0, 1).reshape(rows, -1)
    pre_act = jnp.dot(wide, up_weight, preferred_element_type=jnp.float32)
    activation = jax.nn.gelu(pre_act, approximate=False).astype(jnp.bfloat16)
    joined = lax.all_gather(activation, "tensor", axis=1, tiled=True)
    part = jnp.dot(joined, down_weight, preferred_element_type=jnp.float32)
    ffn_row = jnp.sum(swap_all(part), axis=0, keepdims=True).astype(jnp.bfloat16)

    gathered = lax.all_gather(init_cache[0], "batch", axis_index_groups=groups)
    parent_own = jnp.sum(jnp.where(jnp.arange(BEAMS) == own_beam, parent, 0))
    cache = place(gathered, new_kv[0, 0], parent_own[None], length[None])
    return (hidden[None], ffn_row[None], cache[None])


def solution(mesh):
    placed = (
        P(("grp", "batch"), None, None, "tensor"),
        P(("grp", "batch"), None, None, "tensor"),
        P(None, ("grp", "batch"), None, "tensor"),
        P(None, ("grp", "batch"), None, "tensor"),
        P(None, "grp", "batch"),
        P(None, "tensor", "batch"),
        P(None, ("batch", "tensor")),
        P("batch", "tensor"),
        P(None, "grp"),
        P("grp"),
    )
    return jax.shard_map(
        body,
        mesh=mesh,
        in_specs=placed,
        out_specs=(
            P(None, "grp", "batch"),
            P(None, ("grp", "batch"), "tensor"),
            P(("grp", "batch"), None, None, "tensor"),
        ),
        check_vma=False,
    )
```

```python
import functools
import math

import jax
import jax.numpy as jnp
from jax import lax
from jax.experimental import pallas as pl
from jax.experimental.pallas import tpu as pltpu
from jax.sharding import PartitionSpec as P

HD = 128
LANES = 128
SLOT = 16
BEAMS = 8
LOW = -1e30
MIB = 1024 * 1024
RESIDENT = True

VM = pl.BlockSpec(memory_space=pltpu.VMEM)
SM = pl.BlockSpec(memory_space=pltpu.SMEM)


def xor_permute(value, axis, bit):
    total = lax.axis_size(axis)
    return lax.ppermute(value, axis, [(i, i ^ bit) for i in range(total)])


def doubling(buffer, first, last):
    bit = first
    while bit < last:
        buffer = jnp.concatenate([buffer, xor_permute(buffer, "batch", bit)])
        bit *= 2
    return buffer


def call(kernel, out, *args, specs=None, vmem=8, flops=0, moved=0):
    return pl.pallas_call(
        kernel,
        out_shape=out,
        in_specs=specs or [VM] * len(args),
        out_specs=jax.tree.map(lambda _: VM, out),
        compiler_params=pltpu.CompilerParams(vmem_limit_bytes=vmem * MIB),
        cost_estimate=pl.CostEstimate(flops=flops, bytes_accessed=moved, transcendentals=0),
    )(*args)


def split3(value):
    high = value.astype(jnp.bfloat16).astype(jnp.float32)
    rest = value - high
    middle = rest.astype(jnp.bfloat16).astype(jnp.float32)
    return high, middle, rest - middle


def export(num_ref, state_ref, pay_ref, peaks, totals):
    heads = num_ref.shape[1] // HD
    inverse = jnp.where(totals > 0.0, 1.0 / jnp.where(totals > 0.0, totals, 1.0), 0.0)
    for h in range(heads):
        cols = slice(h * HD, (h + 1) * HD)
        pay_ref[:, cols] = (num_ref[:, cols] * inverse[:, h : h + 1]).astype(jnp.bfloat16)
    state_ref[:, :LANES] = peaks
    state_ref[:, LANES:] = totals
    group = lax.broadcasted_iota(jnp.int32, peaks.shape, 1) // SLOT
    extra = jnp.zeros_like(peaks)
    for g, part in enumerate(split3(peaks) + split3(totals)):
        extra = jnp.where(group == g, pltpu.roll(part, g * SLOT, 1) if g else part, extra)
    pay_ref[:, heads * HD :] = extra.astype(jnp.bfloat16)


def attend_kernel(stride, query_ref, cache_ref, memory_ref, new_ref, parents_ref, lengths_ref, num_ref, state_ref, pay_ref):
    position = lax.axis_index("batch")
    own, request = position // stride, lax.rem(position, stride)
    length = lengths_ref[request]
    rows, width = query_ref.shape
    heads = width // HD
    past = cache_ref.shape[1]
    span = past + memory_ref.shape[1]

    to = lax.broadcasted_iota(jnp.int32, (rows, rows), 0)
    source = lax.broadcasted_iota(jnp.int32, (rows, rows), 1)
    beam = jnp.bitwise_xor(source // 2, own)
    order = jnp.where(to == (source % 2) * BEAMS + beam, 1.0, 0.0).astype(jnp.bfloat16)

    row = lax.broadcasted_iota(jnp.int32, (rows, span), 0)
    slot = lax.broadcasted_iota(jnp.int32, (rows, span), 1)
    parent = jnp.zeros_like(row)
    for b in range(BEAMS):
        parent = jnp.where(row == b, parents_ref[0, b * stride + request], parent)
    in_past = ((slot < length) & (parent == own)) | ((slot == length) & (row == own))
    valid = jnp.where(row < BEAMS, jnp.where(in_past, 1, 0), jnp.where(slot >= past, 1, 0)) == 1
    fresh = lax.broadcasted_iota(jnp.int32, (past, HD), 0) == length
    lane = lax.broadcasted_iota(jnp.int32, (rows, LANES), 1)
    peaks = jnp.zeros((rows, LANES), jnp.float32)
    totals = jnp.zeros((rows, LANES), jnp.float32)

    def block(kind, cols):
        old = cache_ref[kind, :, cols].astype(jnp.float32)
        new = new_ref[kind : kind + 1, cols].astype(jnp.float32)
        merged = jnp.where(fresh, new, old).astype(jnp.bfloat16)
        return jnp.concatenate([merged, memory_ref[kind, :, cols]])

    for h in range(heads):
        cols = slice(h * HD, (h + 1) * HD)
        query = jnp.dot(order, query_ref[:, cols], preferred_element_type=jnp.float32).astype(jnp.bfloat16)
        scores = lax.dot_general(
            query, block(0, cols), (((1,), (1,)), ((), ())), preferred_element_type=jnp.float32
        ) * (1.0 / math.sqrt(HD))
        scores = jnp.where(valid, scores, LOW)
        peak = jnp.max(scores, axis=1, keepdims=True)
        weights = jnp.where(valid, jnp.exp(scores - peak), 0.0)
        total = jnp.sum(weights, axis=1, keepdims=True)
        high = weights.astype(jnp.bfloat16)
        low = (weights - high.astype(jnp.float32)).astype(jnp.bfloat16)
        values = block(1, cols)
        num_ref[:, cols] = jnp.dot(high, values, preferred_element_type=jnp.float32) + jnp.dot(
            low, values, preferred_element_type=jnp.float32
        )
        peaks = jnp.where(lane == h, peak, peaks)
        totals = jnp.where(lane == h, total, totals)
    export(num_ref, state_ref, pay_ref, peaks, totals)


def combine(num_ref, state_ref, pay_ref, out_ref):
    heads = num_ref.shape[1] // HD
    extra = pay_ref[:, heads * HD :].astype(jnp.float32)
    summed = extra + pltpu.roll(extra, LANES - SLOT, 1) + pltpu.roll(extra, LANES - 2 * SLOT, 1)
    other_total = pltpu.roll(summed, LANES - 3 * SLOT, 1)
    lane = lax.broadcasted_iota(jnp.int32, extra.shape, 1)
    used = lane < SLOT
    other_peak = jnp.where(used, summed, 0.0)
    other_total = jnp.where(used, other_total, 0.0)
    own_peak, own_total = state_ref[:, :LANES], state_ref[:, LANES:]
    peaks = jnp.maximum(own_peak, other_peak)
    own_factor = jnp.exp(own_peak - peaks)
    other_factor = jnp.exp(other_peak - peaks) * other_total
    totals = own_total * own_factor + other_factor
    for h in range(heads):
        cols = slice(h * HD, (h + 1) * HD)
        other = pay_ref[:, cols].astype(jnp.float32)
        out_ref[:, cols] = num_ref[:, cols] * own_factor[:, h : h + 1] + other * other_factor[:, h : h + 1]
    return peaks, totals


def merge_kernel(num_ref, state_ref, pay_ref, num_out, state_out, pay_out):
    peaks, totals = combine(num_ref, state_ref, pay_ref, num_out)
    export(num_out, state_out, pay_out, peaks, totals)


def finish_kernel(num_ref, state_ref, pay_ref, out_ref, num):
    _, totals = combine(num_ref, state_ref, pay_ref, num)
    for h in range(num.shape[1] // HD):
        cols = slice(h * HD, (h + 1) * HD)
        out_ref[:, cols] = (num[:, cols] / totals[:, h : h + 1]).astype(jnp.bfloat16)


def finish(num, state, pay):
    return pl.pallas_call(
        finish_kernel,
        out_shape=jax.ShapeDtypeStruct(num.shape, jnp.bfloat16),
        in_specs=[VM] * 3,
        out_specs=VM,
        scratch_shapes=[pltpu.VMEM(num.shape, jnp.float32)],
        compiler_params=pltpu.CompilerParams(vmem_limit_bytes=8 * MIB),
    )(num, state, pay)


def project_kernel(attended_ref, weight_ref, out_ref):
    rows = out_ref.shape[0]
    first = jnp.dot(attended_ref[...], weight_ref[0], preferred_element_type=jnp.float32)
    second = jnp.dot(attended_ref[...], weight_ref[1], preferred_element_type=jnp.float32)
    out_ref[...] = first[:rows] + second[rows:]


def add_kernel(own_ref, other_ref, residual_ref, out_ref):
    total = residual_ref[...].astype(jnp.float32) + (own_ref[...] + other_ref[...])
    out_ref[...] = total.astype(jnp.bfloat16)


def up_kernel(hidden_ref, weight_ref, out_ref):
    blocks, rows, depth = hidden_ref.shape
    position = lax.axis_index("batch")

    def step(j, total):
        start = pl.multiple_of(jnp.bitwise_xor(position, j) * depth, depth)
        return total + jnp.dot(
            hidden_ref[j], weight_ref[pl.ds(start, depth), :], preferred_element_type=jnp.float32
        )

    total = lax.fori_loop(0, blocks, step, jnp.zeros(out_ref.shape, jnp.float32), unroll=blocks <= 8)
    out_ref[...] = (0.5 * total * (1.0 + lax.erf(total * math.sqrt(0.5)))).astype(jnp.bfloat16)


def reorder(activation):
    rows = activation.shape[0]
    position = lax.axis_index("batch")
    to = lax.broadcasted_iota(jnp.int32, (rows, rows), 0)
    source = lax.broadcasted_iota(jnp.int32, (rows, rows), 1)
    reverse = jnp.zeros_like(to)
    bits = rows.bit_length() - 1
    for k in range(bits):
        reverse = reverse + ((to >> k) % 2) * (1 << (bits - 1 - k))
    order = jnp.where(source == jnp.bitwise_xor(reverse, position), 1.0, 0.0).astype(jnp.bfloat16)
    return jnp.dot(order, activation, preferred_element_type=jnp.float32).astype(jnp.bfloat16)


def down_kernel(mine, act_ref, weight_ref, *rest):
    depth = act_ref.shape[1]
    side = lax.axis_index("tensor")
    start = pl.multiple_of((side if mine else 1 - side) * depth, depth)
    part = jnp.dot(
        reorder(act_ref[...]), weight_ref[pl.ds(start, depth), :], preferred_element_type=jnp.float32
    )
    if mine:
        rest[0][...] = part
        return
    before, keep_ref, send_ref = rest
    total = before[...] + part
    half = total.shape[0] // 2
    keep_ref[...] = total[:half]
    send_ref[...] = total[half:]


def place_kernel(parent_ref, length_ref, row_ref, new_ref, out_ref):
    slots = lax.broadcasted_iota(jnp.int32, row_ref.shape[2:], 0)
    for kind in range(2):
        old = row_ref[0, kind]
        new = jnp.broadcast_to(new_ref[kind : kind + 1, :], old.shape)
        out_ref[kind] = jnp.where(slots == length_ref[0], new, old)


def place(gathered, new_kv, parent, length):
    _, kinds, positions, width = gathered.shape
    return pl.pallas_call(
        place_kernel,
        out_shape=jax.ShapeDtypeStruct((kinds, positions, width), gathered.dtype),
        grid_spec=pltpu.PrefetchScalarGridSpec(
            num_scalar_prefetch=2,
            grid=(1,),
            in_specs=[
                pl.BlockSpec((1, kinds, positions, width), lambda i, p, n: (p[0], 0, 0, 0)),
                pl.BlockSpec((kinds, width), lambda i, p, n: (0, 0)),
            ],
            out_specs=pl.BlockSpec((kinds, positions, width), lambda i, p, n: (0, 0, 0)),
        ),
        compiler_params=pltpu.CompilerParams(vmem_limit_bytes=8 * MIB),
    )(parent, length, gathered, new_kv)


def body(
    init_cache,
    memory,
    queries,
    new_kv,
    residual,
    out_weight,
    up_weight,
    down_weight,
    parents,
    lengths,
):
    devices = lax.axis_size("batch")
    stride = devices // BEAMS
    position = lax.axis_index("batch")
    own_beam = position // stride
    request = position % stride
    width = queries.shape[-1]
    rows = parents.shape[1]
    columns = out_weight.shape[2]
    hidden_units = up_weight.shape[1]
    out_columns = down_weight.shape[1]
    groups = None
    if stride > 1:
        groups = [[b * stride + r for b in range(BEAMS)] for r in range(stride)]
    f32, bf16 = jnp.float32, jnp.bfloat16
    shape = jax.ShapeDtypeStruct

    if RESIDENT:
        out_weight, up_weight, down_weight = (
            pltpu.with_memory_space_constraint(w, pltpu.VMEM) for w in (out_weight, up_weight, down_weight)
        )

    query = doubling(queries[0, 0], stride, devices)
    state_shapes = (
        shape((2 * BEAMS, width), f32),
        shape((2 * BEAMS, 2 * LANES), f32),
        shape((2 * BEAMS, width + LANES), bf16),
    )
    num, state, pay = call(
        functools.partial(attend_kernel, stride),
        state_shapes,
        query,
        init_cache[0],
        memory[0],
        new_kv[0, 0],
        parents,
        lengths,
        specs=[VM] * 4 + [SM] * 2,
    )
    bit = stride
    while 2 * bit < devices:
        num, state, pay = call(merge_kernel, state_shapes, num, state, xor_permute(pay, "batch", bit))
        bit *= 2
    attended = finish(num, state, xor_permute(pay, "batch", bit))
    if stride > 1:
        stacked = doubling(attended[None], 1, stride)
        wanted = jnp.bitwise_xor(jnp.arange(stride, dtype=jnp.int32), request)
        stacked = stacked[wanted].reshape(stride, 2, BEAMS, width)
        attended = stacked.transpose(1, 2, 0, 3).reshape(2 * rows, width)

    partial = call(project_kernel, shape((rows, columns), f32), attended, out_weight)
    other = xor_permute(partial, "tensor", 1)
    hidden = call(add_kernel, shape((rows, columns), bf16), partial, other, residual[0])
    wide = doubling(hidden[None], 1, devices)
    activation = call(up_kernel, shape((rows, hidden_units), bf16), wide, up_weight)
    arrived = xor_permute(activation, "tensor", 1)
    before = call(
        functools.partial(down_kernel, True), shape((rows, out_columns), f32), activation, down_weight
    )
    keep, send = call(
        functools.partial(down_kernel, False),
        (shape((rows // 2, out_columns), f32),) * 2,
        arrived,
        down_weight,
        before,
    )
    bit = 1
    while True:
        total = keep + xor_permute(send, "batch", bit)
        bit *= 2
        if bit == devices:
            break
        half = total.shape[0] // 2
        keep, send = total[:half], total[half:]
    ffn_row = total.astype(bf16)

    gathered = lax.all_gather(init_cache[0], "batch", axis_index_groups=groups)
    grouped = parents.reshape(BEAMS, stride)
    here = (jnp.arange(BEAMS)[:, None] == own_beam) & (jnp.arange(stride)[None] == request)
    parent_own = jnp.sum(jnp.where(here, grouped, 0))
    length = jnp.sum(jnp.where(jnp.arange(stride) == request, lengths, 0))
    cache = place(gathered, new_kv[0, 0], parent_own[None], length[None])
    return (hidden[None], ffn_row[None], cache[None])


def solution(mesh):
    placed = (
        P(("grp", "batch"), None, None, "tensor"),
        P(("grp", "batch"), None, None, "tensor"),
        P(None, ("grp", "batch"), None, "tensor"),
        P(None, ("grp", "batch"), None, "tensor"),
        P(None, "grp", "batch"),
        P(None, "tensor", "batch"),
        P(None, ("batch", "tensor")),
        P("batch", "tensor"),
        P(None, "grp"),
        P("grp"),
    )
    return jax.shard_map(
        body,
        mesh=mesh,
        in_specs=placed,
        out_specs=(
            P(None, "grp", "batch"),
            P(None, ("grp", "batch"), "tensor"),
            P(("grp", "batch"), None, None, "tensor"),
        ),
        check_vma=False,
    )
```

```python
import functools
import math

import jax
import jax.numpy as jnp
from jax import lax
from jax.experimental import pallas as pl
from jax.experimental.pallas import tpu as pltpu
from jax.sharding import PartitionSpec as P

HD = 128
LANES = 128
SLOT = 16
BEAMS = 8
LOW = -1e30
MIB = 1024 * 1024

VM = pl.BlockSpec(memory_space=pltpu.VMEM)
SM = pl.BlockSpec(memory_space=pltpu.SMEM)
ANY = pl.BlockSpec(memory_space=pl.ANY)


def xor_permute(value, axis, bit):
    total = lax.axis_size(axis)
    return lax.ppermute(value, axis, [(i, i ^ bit) for i in range(total)])


def reverse(index, size):
    bits = size.bit_length() - 1
    return sum(((index >> k) & 1) << (bits - 1 - k) for k in range(bits))


def doubling(buffer, first, last, work):
    bit = last
    while True:
        bit //= 2
        other = xor_permute(buffer, "batch", bit)
        work(buffer)
        if bit == first:
            return buffer, other
        buffer = jnp.concatenate([buffer, other])


def call(kernel, out, *args, specs=None, vmem=8, flops=0, moved=0):
    return pl.pallas_call(
        kernel,
        out_shape=out,
        in_specs=specs or [VM] * len(args),
        out_specs=jax.tree.map(lambda _: VM, out),
        compiler_params=pltpu.CompilerParams(vmem_limit_bytes=vmem * MIB),
        cost_estimate=pl.CostEstimate(flops=flops, bytes_accessed=moved, transcendentals=0),
    )(*args)


def start_all(copies):
    for copy in copies:
        copy.start()
    for copy in copies:
        copy.wait()


def fetch_kernel(count, *refs):
    sems = refs[-1]
    outs = refs[-1 - count : -1]
    start_all([pltpu.make_async_copy(refs[i], outs[i], sems.at[i]) for i in range(count)])


def fetch(arrays, after):
    count = len(arrays)
    return pl.pallas_call(
        functools.partial(fetch_kernel, count),
        out_shape=[pltpu.VMEM(x.shape, x.dtype) for x in arrays],
        in_specs=[ANY] * (count + 1),
        out_specs=[VM] * count,
        scratch_shapes=[pltpu.SemaphoreType.DMA((count,))],
        compiler_params=pltpu.CompilerParams(vmem_limit_bytes=2 * MIB),
        cost_estimate=pl.CostEstimate(flops=0, bytes_accessed=2 * MIB, transcendentals=0),
    )(*arrays, after)


def fetch_rows_kernel(first, blocks, total, weight_ref, _, out_ref, sems):
    position = lax.axis_index("batch")
    depth = out_ref.shape[0] // blocks
    copies = []
    for k in range(blocks):
        start = pl.multiple_of(jnp.bitwise_xor(position, reverse(first + k, total)) * depth, depth)
        copies.append(
            pltpu.make_async_copy(
                weight_ref.at[pl.ds(start, depth), :], out_ref.at[pl.ds(k * depth, depth), :], sems.at[k]
            )
        )
    start_all(copies)


def fetch_rows(weight, first, blocks, total, after):
    depth = weight.shape[0] // total * blocks
    return pl.pallas_call(
        functools.partial(fetch_rows_kernel, first, blocks, total),
        out_shape=pltpu.VMEM((depth, weight.shape[1]), weight.dtype),
        in_specs=[ANY] * 2,
        out_specs=VM,
        scratch_shapes=[pltpu.SemaphoreType.DMA((blocks,))],
        compiler_params=pltpu.CompilerParams(vmem_limit_bytes=2 * MIB),
        cost_estimate=pl.CostEstimate(flops=0, bytes_accessed=2 * MIB, transcendentals=0),
    )(weight, after)


def split3(value):
    high = value.astype(jnp.bfloat16).astype(jnp.float32)
    rest = value - high
    middle = rest.astype(jnp.bfloat16).astype(jnp.float32)
    return high, middle, rest - middle


def export(num_ref, state_ref, pay_ref, peaks, totals):
    heads = num_ref.shape[1] // HD
    inverse = jnp.where(totals > 0.0, 1.0 / jnp.where(totals > 0.0, totals, 1.0), 0.0)
    for h in range(heads):
        cols = slice(h * HD, (h + 1) * HD)
        pay_ref[:, cols] = (num_ref[:, cols] * inverse[:, h : h + 1]).astype(jnp.bfloat16)
    state_ref[:, :LANES] = peaks
    state_ref[:, LANES:] = totals
    group = lax.broadcasted_iota(jnp.int32, peaks.shape, 1) // SLOT
    extra = jnp.zeros_like(peaks)
    for g, part in enumerate(split3(peaks) + split3(totals)):
        extra = jnp.where(group == g, pltpu.roll(part, g * SLOT, 1) if g else part, extra)
    pay_ref[:, heads * HD :] = extra.astype(jnp.bfloat16)


def attend_kernel(
    stride, near_ref, far_ref, cache_ref, memory_ref, new_ref, parents_ref, lengths_ref, num_ref, state_ref, pay_ref
):
    position = lax.axis_index("batch")
    own, request = position // stride, lax.rem(position, stride)
    length = lengths_ref[request]
    rows, width = num_ref.shape
    heads = width // HD
    past = cache_ref.shape[1]
    span = past + memory_ref.shape[1]
    f32, bf16 = jnp.float32, jnp.bfloat16

    to = lax.broadcasted_iota(jnp.int32, (rows, BEAMS), 0)
    source = lax.broadcasted_iota(jnp.int32, (rows, BEAMS), 1)

    def place_rows(piece_ref, first):
        beam = jnp.bitwise_xor(reverse(first + source // 2, BEAMS), own)
        order = jnp.where(to == (source % 2) * BEAMS + beam, 1.0, 0.0).astype(bf16)
        return jnp.dot(order, piece_ref[...], preferred_element_type=f32)

    query = (place_rows(near_ref, 0) + place_rows(far_ref, BEAMS // 2)).astype(bf16)

    row = lax.broadcasted_iota(jnp.int32, (rows, span), 0)
    slot = lax.broadcasted_iota(jnp.int32, (rows, span), 1)
    parent = jnp.zeros_like(row)
    for b in range(BEAMS):
        parent = jnp.where(row == b, parents_ref[0, b * stride + request], parent)
    in_past = ((slot < length) & (parent == own)) | ((slot == length) & (row == own))
    valid = jnp.where(row < BEAMS, jnp.where(in_past, 1, 0), jnp.where(slot >= past, 1, 0)) == 1
    fresh = lax.broadcasted_iota(jnp.int32, (past, HD), 0) == length
    lane = lax.broadcasted_iota(jnp.int32, (rows, LANES), 1)
    all_cols = [slice(h * HD, (h + 1) * HD) for h in range(heads)]

    def block(kind, cols):
        old = cache_ref[kind, :, cols].astype(f32)
        new = new_ref[kind : kind + 1, cols].astype(f32)
        merged = jnp.where(fresh, new, old).astype(bf16)
        return jnp.concatenate([merged, memory_ref[kind, :, cols]])

    scores = [
        lax.dot_general(
            query[:, cols], block(0, cols), (((1,), (1,)), ((), ())), preferred_element_type=f32
        )
        for cols in all_cols
    ]
    values = [block(1, cols) for cols in all_cols]
    scores = [jnp.where(valid, s * (1.0 / math.sqrt(HD)), LOW) for s in scores]
    tops = [jnp.max(s, axis=1, keepdims=True) for s in scores]
    weights = [jnp.where(valid, jnp.exp(s - t), 0.0) for s, t in zip(scores, tops)]
    sums = [jnp.sum(w, axis=1, keepdims=True) for w in weights]
    highs = [w.astype(bf16) for w in weights]
    lows = [(w - high.astype(f32)).astype(bf16) for w, high in zip(weights, highs)]
    both = [
        jnp.dot(jnp.concatenate([high, low]), v, preferred_element_type=f32)
        for high, low, v in zip(highs, lows, values)
    ]
    peaks = jnp.zeros((rows, LANES), f32)
    totals = jnp.zeros((rows, LANES), f32)
    for h, cols in enumerate(all_cols):
        num_ref[:, cols] = both[h][:rows] + both[h][rows:]
        peaks = jnp.where(lane == h, tops[h], peaks)
        totals = jnp.where(lane == h, sums[h], totals)
    export(num_ref, state_ref, pay_ref, peaks, totals)


def combine(num_ref, state_ref, pay_ref, out_ref):
    heads = num_ref.shape[1] // HD
    extra = pay_ref[:, heads * HD :].astype(jnp.float32)
    summed = extra + pltpu.roll(extra, LANES - SLOT, 1) + pltpu.roll(extra, LANES - 2 * SLOT, 1)
    other_total = pltpu.roll(summed, LANES - 3 * SLOT, 1)
    lane = lax.broadcasted_iota(jnp.int32, extra.shape, 1)
    used = lane < SLOT
    other_peak = jnp.where(used, summed, 0.0)
    other_total = jnp.where(used, other_total, 0.0)
    own_peak, own_total = state_ref[:, :LANES], state_ref[:, LANES:]
    peaks = jnp.maximum(own_peak, other_peak)
    own_factor = jnp.exp(own_peak - peaks)
    other_factor = jnp.exp(other_peak - peaks) * other_total
    totals = own_total * own_factor + other_factor
    for h in range(heads):
        cols = slice(h * HD, (h + 1) * HD)
        other = pay_ref[:, cols].astype(jnp.float32)
        out_ref[:, cols] = num_ref[:, cols] * own_factor[:, h : h + 1] + other * other_factor[:, h : h + 1]
    return peaks, totals


def merge_kernel(num_ref, state_ref, pay_ref, num_out, state_out, pay_out):
    peaks, totals = combine(num_ref, state_ref, pay_ref, num_out)
    export(num_out, state_out, pay_out, peaks, totals)


def finish_kernel(num_ref, state_ref, pay_ref, out_ref, num):
    _, totals = combine(num_ref, state_ref, pay_ref, num)
    for h in range(num.shape[1] // HD):
        cols = slice(h * HD, (h + 1) * HD)
        out_ref[:, cols] = (num[:, cols] / totals[:, h : h + 1]).astype(jnp.bfloat16)


def finish(num, state, pay):
    return pl.pallas_call(
        finish_kernel,
        out_shape=jax.ShapeDtypeStruct(num.shape, jnp.bfloat16),
        in_specs=[VM] * 3,
        out_specs=VM,
        scratch_shapes=[pltpu.VMEM(num.shape, jnp.float32)],
        compiler_params=pltpu.CompilerParams(vmem_limit_bytes=8 * MIB),
    )(num, state, pay)


def project_kernel(attended_ref, first_ref, second_ref, out_ref):
    rows = out_ref.shape[0]
    first = jnp.dot(attended_ref[...], first_ref[0], preferred_element_type=jnp.float32)
    second = jnp.dot(attended_ref[...], second_ref[0], preferred_element_type=jnp.float32)
    out_ref[...] = first[:rows] + second[rows:]


def add_kernel(own_ref, other_ref, residual_ref, out_ref):
    total = residual_ref[0].astype(jnp.float32) + (own_ref[...] + other_ref[...])
    out_ref[0] = total.astype(jnp.bfloat16)


def up_kernel(near_ref, far_ref, *refs):
    chunks, (hidden_ref, out_ref, sem) = refs[:-3], refs[-3:]
    half, _, depth = near_ref.shape
    per = 2 * half // len(chunks)
    copy = pltpu.make_async_copy(near_ref.at[0], hidden_ref, sem)
    copy.start()
    total = jnp.zeros(out_ref.shape, jnp.float32)
    for j in range(2 * half):
        block = near_ref[j] if j < half else far_ref[j - half]
        weight = chunks[j // per][pl.ds(j % per * depth, depth), :]
        total = total + jnp.dot(block, weight, preferred_element_type=jnp.float32)
    out_ref[...] = (0.5 * total * (1.0 + lax.erf(total * math.sqrt(0.5)))).astype(jnp.bfloat16)
    copy.wait()


def up(near, far, chunks, units):
    _, rows, columns = near.shape
    return pl.pallas_call(
        up_kernel,
        out_shape=(
            jax.ShapeDtypeStruct((rows, columns), jnp.bfloat16),
            jax.ShapeDtypeStruct((rows, units), jnp.bfloat16),
        ),
        in_specs=[VM] * (2 + len(chunks)),
        out_specs=(ANY, VM),
        scratch_shapes=[pltpu.SemaphoreType.DMA],
        compiler_params=pltpu.CompilerParams(vmem_limit_bytes=8 * MIB),
    )(near, far, *chunks)


def reorder(activation):
    rows = activation.shape[0]
    position = lax.axis_index("batch")
    to = lax.broadcasted_iota(jnp.int32, (rows, rows), 0)
    source = lax.broadcasted_iota(jnp.int32, (rows, rows), 1)
    order = jnp.where(source == jnp.bitwise_xor(reverse(to, rows), position), 1.0, 0.0).astype(jnp.bfloat16)
    return jnp.dot(order, activation, preferred_element_type=jnp.float32).astype(jnp.bfloat16)


def down_kernel(mine, act_ref, weight_ref, *rest):
    depth = act_ref.shape[1]
    side = lax.axis_index("tensor")
    start = pl.multiple_of((side if mine else 1 - side) * depth, depth)
    part = jnp.dot(
        reorder(act_ref[...]), weight_ref[pl.ds(start, depth), :], preferred_element_type=jnp.float32
    )
    if mine:
        rest[0][...] = part
        return
    before, keep_ref, send_ref = rest
    total = before[...] + part
    half = total.shape[0] // 2
    keep_ref[...] = total[:half]
    send_ref[...] = total[half:]


def ring(devices):
    if devices > BEAMS:
        return list(range(BEAMS))
    return list(range(0, BEAMS, 2)) + list(range(BEAMS - 1, 0, -2))


def place_kernel(stride, order, gathered_ref, new_ref, parents_ref, lengths_ref, out_ref, row, sem):
    position = lax.axis_index("batch")
    request = lax.rem(position, stride)
    parent = parents_ref[0, position]
    place = jnp.int32(0)
    for k, beam in enumerate(order):
        place = jnp.where(parent == beam, k, place)
    place = jnp.where(lax.axis_index("tensor") == 1, BEAMS - 1 - place, place)
    copy = pltpu.make_async_copy(gathered_ref.at[place], row, sem)
    copy.start()
    slots = lax.broadcasted_iota(jnp.int32, row.shape[1:], 0)
    copy.wait()
    for kind in range(2):
        old = row[kind].astype(jnp.float32)
        new = new_ref[kind : kind + 1, :].astype(jnp.float32)
        out_ref[kind] = jnp.where(slots == lengths_ref[request], new, old).astype(jnp.bfloat16)


def place(stride, order, gathered, new_kv, parents, lengths):
    return pl.pallas_call(
        functools.partial(place_kernel, stride, order),
        out_shape=jax.ShapeDtypeStruct(gathered.shape[1:], gathered.dtype),
        in_specs=[pl.BlockSpec(memory_space=pltpu.HBM), VM, SM, SM],
        out_specs=VM,
        scratch_shapes=[pltpu.VMEM(gathered.shape[1:], gathered.dtype), pltpu.SemaphoreType.DMA],
        compiler_params=pltpu.CompilerParams(vmem_limit_bytes=8 * MIB),
    )(gathered, new_kv, parents, lengths)


def body(
    init_cache,
    memory,
    queries,
    new_kv,
    residual,
    out_weight,
    up_weight,
    down_weight,
    parents,
    lengths,
):
    devices = lax.axis_size("batch")
    stride = devices // BEAMS
    position = lax.axis_index("batch")
    request = position % stride
    width = queries.shape[-1]
    rows = parents.shape[1]
    columns = out_weight.shape[2]
    hidden_units = up_weight.shape[1]
    out_columns = down_weight.shape[1]
    f32, bf16 = jnp.float32, jnp.bfloat16
    shape = jax.ShapeDtypeStruct
    down_weight = pltpu.with_memory_space_constraint(down_weight, pltpu.VMEM)
    pieces = 8
    local = {}
    chunks = []

    def load_operands(after):
        sources = (queries[0, 0], init_cache[0], memory[0], new_kv[0, 0], residual)
        local["all"] = fetch(sources, after)

    def load_out(kind):
        def work(after):
            local[kind] = fetch([out_weight[kind : kind + 1]], after)[0]

        return work

    def load_up(after):
        if len(chunks) < pieces:
            per = devices // pieces
            chunks.append(fetch_rows(up_weight, len(chunks) * per, per, devices, after))

    bit = devices // 2
    other = xor_permute(queries[0, 0], "batch", bit)
    load_operands(queries[0, 0])
    query, cache_row, memory_row, new_row, residual_row = local["all"]
    works = [load_out(0), load_out(1)]
    query = jnp.concatenate([query, other])
    query, far = doubling(query, stride, bit, lambda after: works.pop(0)(after))
    state_shapes = (
        shape((2 * BEAMS, width), f32),
        shape((2 * BEAMS, 2 * LANES), f32),
        shape((2 * BEAMS, width + LANES), bf16),
    )
    num, state, pay = call(
        functools.partial(attend_kernel, stride),
        state_shapes,
        query,
        far,
        cache_row,
        memory_row,
        new_row,
        parents,
        lengths,
        specs=[VM] * 5 + [SM] * 2,
    )
    bit = stride
    while True:
        arrived = xor_permute(pay, "batch", bit)
        load_up(pay)
        load_up(pay)
        bit *= 2
        if bit == devices:
            break
        num, state, pay = call(merge_kernel, state_shapes, num, state, arrived)
    attended = finish(num, state, arrived)
    if stride > 1:
        stacked = jnp.concatenate(doubling(attended[None], 1, stride, lambda after: None))
        wanted = reverse(jnp.bitwise_xor(jnp.arange(stride, dtype=jnp.int32), request), stride)
        stacked = stacked[wanted].reshape(stride, 2, BEAMS, width)
        attended = stacked.transpose(1, 2, 0, 3).reshape(2 * rows, width)

    partial = call(project_kernel, shape((rows, columns), f32), attended, local[0], local[1])
    other = xor_permute(partial, "tensor", 1)
    mine = call(add_kernel, pltpu.VMEM((1, rows, columns), bf16), partial, other, residual_row)
    near, far = doubling(mine, 1, devices, load_up)
    while len(chunks) < pieces:
        load_up(near)
    hidden, activation = up(near, far, chunks, hidden_units)
    arrived = xor_permute(activation, "tensor", 1)
    before = call(
        functools.partial(down_kernel, True), shape((rows, out_columns), f32), activation, down_weight
    )
    keep, send = call(
        functools.partial(down_kernel, False),
        (shape((rows // 2, out_columns), f32),) * 2,
        arrived,
        down_weight,
        before,
    )
    bit = 1
    while True:
        total = keep + xor_permute(send, "batch", bit)
        bit *= 2
        if bit == devices:
            break
        half = total.shape[0] // 2
        keep, send = total[:half], total[half:]
    ffn_row = total.astype(bf16)

    order = ring(devices)
    groups = []
    for r in range(stride):
        groups.append([(beam * stride + r) * 2 for beam in order])
        groups.append([(beam * stride + r) * 2 + 1 for beam in reversed(order)])
    gathered = lax.all_gather(init_cache[0], ("batch", "tensor"), axis_index_groups=groups)
    cache = place(stride, order, gathered, new_row, parents, lengths)
    return (hidden[None], ffn_row[None], cache[None])


def solution(mesh):
    placed = (
        P(("grp", "batch"), None, None, "tensor"),
        P(("grp", "batch"), None, None, "tensor"),
        P(None, ("grp", "batch"), None, "tensor"),
        P(None, ("grp", "batch"), None, "tensor"),
        P(None, "grp", "batch"),
        P(None, "tensor", "batch"),
        P(None, ("batch", "tensor")),
        P("batch", "tensor"),
        P(None, "grp"),
        P("grp"),
    )
    return jax.shard_map(
        body,
        mesh=mesh,
        in_specs=placed,
        out_specs=(
            P(None, "grp", "batch"),
            P(None, ("grp", "batch"), "tensor"),
            P(("grp", "batch"), None, None, "tensor"),
        ),
        check_vma=False,
    )
```

```python
import functools
import math

import jax
import jax.numpy as jnp
from jax import lax
from jax.experimental import pallas as pl
from jax.experimental.pallas import tpu as pltpu
from jax.sharding import PartitionSpec as P

HD = 128
LANES = 128
SLOT = 16
BEAMS = 8
LOW = -1e30
MIB = 1024 * 1024
PIECES = 8

VM = pl.BlockSpec(memory_space=pltpu.VMEM)
SM = pl.BlockSpec(memory_space=pltpu.SMEM)
ANY = pl.BlockSpec(memory_space=pl.ANY)


def xor_permute(value, axis, bit):
    total = lax.axis_size(axis)
    return lax.ppermute(value, axis, [(i, i ^ bit) for i in range(total)])


def lead_permute(value, bit):
    pairs = [(2 * i + 1, 2 * (i ^ bit) + 1) for i in range(lax.axis_size("batch"))]
    return lax.ppermute(value, ("batch", "tensor"), pairs)


def hand(value, to):
    pairs = [(2 * i + 1 - to, 2 * i + to) for i in range(lax.axis_size("batch"))]
    return lax.ppermute(value, ("batch", "tensor"), pairs)


def reverse(index, size):
    bits = size.bit_length() - 1
    return sum(((index >> k) & 1) << (bits - 1 - k) for k in range(bits))


def pin(value, loaded):
    return lax.optimization_barrier((value, loaded))


def doubling(buffer, first, last, work, permute=lead_permute):
    bit = last
    while True:
        bit //= 2
        other = permute(buffer, bit)
        other = work(buffer, other)
        if bit == first:
            return buffer, other
        buffer = jnp.concatenate([buffer, other])


def call(kernel, out, *args, specs=None, vmem=8, flops=0, moved=0):
    return pl.pallas_call(
        kernel,
        out_shape=out,
        in_specs=specs or [VM] * len(args),
        out_specs=jax.tree.map(lambda _: VM, out),
        compiler_params=pltpu.CompilerParams(vmem_limit_bytes=vmem * MIB),
        cost_estimate=pl.CostEstimate(flops=flops, bytes_accessed=moved, transcendentals=0),
    )(*args)


def in_hbm(value):
    return pltpu.with_memory_space_constraint(value, pltpu.HBM)


def start_all(copies):
    for copy in copies:
        copy.start()
    for copy in copies:
        copy.wait()


def fetch_kernel(count, *refs):
    sems = refs[-1]
    outs = refs[-1 - count : -1]
    start_all([pltpu.make_async_copy(refs[i], outs[i], sems.at[i]) for i in range(count)])


def fetch(arrays, after):
    count = len(arrays)
    return pl.pallas_call(
        functools.partial(fetch_kernel, count),
        out_shape=[pltpu.VMEM(x.shape, x.dtype) for x in arrays],
        in_specs=[ANY] * (count + 1),
        out_specs=[VM] * count,
        scratch_shapes=[pltpu.SemaphoreType.DMA((count,))],
        compiler_params=pltpu.CompilerParams(vmem_limit_bytes=2 * MIB),
        cost_estimate=pl.CostEstimate(flops=0, bytes_accessed=2 * MIB, transcendentals=0),
    )(*arrays, after)


def fetch_rows_kernel(first, blocks, total, weight_ref, _, out_ref, sems):
    position = lax.axis_index("batch")
    depth = out_ref.shape[0] // blocks
    copies = []
    for k in range(blocks):
        start = pl.multiple_of(jnp.bitwise_xor(position, reverse(first + k, total)) * depth, depth)
        copies.append(
            pltpu.make_async_copy(
                weight_ref.at[pl.ds(start, depth), :], out_ref.at[pl.ds(k * depth, depth), :], sems.at[k]
            )
        )
    start_all(copies)


def fetch_rows(weight, first, blocks, total, after):
    depth = weight.shape[0] // total * blocks
    return pl.pallas_call(
        functools.partial(fetch_rows_kernel, first, blocks, total),
        out_shape=pltpu.VMEM((depth, weight.shape[1]), weight.dtype),
        in_specs=[ANY] * 2,
        out_specs=VM,
        scratch_shapes=[pltpu.SemaphoreType.DMA((blocks,))],
        compiler_params=pltpu.CompilerParams(vmem_limit_bytes=2 * MIB),
        cost_estimate=pl.CostEstimate(flops=0, bytes_accessed=2 * MIB, transcendentals=0),
    )(weight, after)


def split3(value):
    high = value.astype(jnp.bfloat16).astype(jnp.float32)
    rest = value - high
    middle = rest.astype(jnp.bfloat16).astype(jnp.float32)
    return high, middle, rest - middle


def export(num_ref, state_ref, pay_ref, peaks, totals):
    heads = num_ref.shape[1] // HD
    inverse = jnp.where(totals > 0.0, 1.0 / jnp.where(totals > 0.0, totals, 1.0), 0.0)
    for h in range(heads):
        cols = slice(h * HD, (h + 1) * HD)
        pay_ref[:, cols] = (num_ref[:, cols] * inverse[:, h : h + 1]).astype(jnp.bfloat16)
    state_ref[:, :LANES] = peaks
    state_ref[:, LANES:] = totals
    group = lax.broadcasted_iota(jnp.int32, peaks.shape, 1) // SLOT
    extra = jnp.zeros_like(peaks)
    for g, part in enumerate(split3(peaks) + split3(totals)):
        extra = jnp.where(group == g, pltpu.roll(part, g * SLOT, 1) if g else part, extra)
    pay_ref[:, heads * HD :] = extra.astype(jnp.bfloat16)


def attend_kernel(stride, near_ref, far_ref, *refs):
    sides, (parents_ref, lengths_ref, num_ref, state_ref, pay_ref) = refs[:-5], refs[-5:]
    for side in range(2):
        attend_side(
            stride,
            side,
            near_ref,
            far_ref,
            *sides[3 * side : 3 * side + 3],
            parents_ref,
            lengths_ref,
            num_ref.at[side],
            state_ref.at[side],
            pay_ref.at[side],
        )


def attend_side(
    stride,
    side,
    near_ref,
    far_ref,
    cache_ref,
    memory_ref,
    new_ref,
    parents_ref,
    lengths_ref,
    num_ref,
    state_ref,
    pay_ref,
):
    position = lax.axis_index("batch")
    own, request = position // stride, lax.rem(position, stride)
    length = lengths_ref[request]
    rows, width = num_ref.shape
    heads = width // HD
    past = cache_ref.shape[1]
    span = past + memory_ref.shape[1]
    f32, bf16 = jnp.float32, jnp.bfloat16

    to = lax.broadcasted_iota(jnp.int32, (rows, near_ref.shape[0]), 0)
    source = lax.broadcasted_iota(jnp.int32, (rows, near_ref.shape[0]), 1)

    def place_rows(piece_ref, first):
        beam = jnp.bitwise_xor(reverse(first + source // 4, BEAMS), own)
        wanted = jnp.where((source // 2) % 2 == side, (source % 2) * BEAMS + beam, -1)
        order = jnp.where(to == wanted, 1.0, 0.0).astype(bf16)
        return jnp.dot(order, piece_ref[...], preferred_element_type=f32)

    query = (place_rows(near_ref, 0) + place_rows(far_ref, BEAMS // 2)).astype(bf16)

    row = lax.broadcasted_iota(jnp.int32, (rows, span), 0)
    slot = lax.broadcasted_iota(jnp.int32, (rows, span), 1)
    parent = jnp.zeros_like(row)
    for b in range(BEAMS):
        parent = jnp.where(row == b, parents_ref[0, b * stride + request], parent)
    in_past = ((slot < length) & (parent == own)) | ((slot == length) & (row == own))
    valid = jnp.where(row < BEAMS, jnp.where(in_past, 1, 0), jnp.where(slot >= past, 1, 0)) == 1
    fresh = lax.broadcasted_iota(jnp.int32, (past, HD), 0) == length
    lane = lax.broadcasted_iota(jnp.int32, (rows, LANES), 1)
    all_cols = [slice(h * HD, (h + 1) * HD) for h in range(heads)]

    def block(kind, cols):
        old = cache_ref[kind, :, cols].astype(f32)
        new = new_ref[kind : kind + 1, cols].astype(f32)
        merged = jnp.where(fresh, new, old).astype(bf16)
        return jnp.concatenate([merged, memory_ref[kind, :, cols]])

    scores = [
        lax.dot_general(
            query[:, cols], block(0, cols), (((1,), (1,)), ((), ())), preferred_element_type=f32
        )
        for cols in all_cols
    ]
    values = [block(1, cols) for cols in all_cols]
    scores = [jnp.where(valid, s * (1.0 / math.sqrt(HD)), LOW) for s in scores]
    tops = [jnp.max(s, axis=1, keepdims=True) for s in scores]
    weights = [jnp.where(valid, jnp.exp(s - t), 0.0) for s, t in zip(scores, tops)]
    sums = [jnp.sum(w, axis=1, keepdims=True) for w in weights]
    highs = [w.astype(bf16) for w in weights]
    lows = [(w - high.astype(f32)).astype(bf16) for w, high in zip(weights, highs)]
    both = [
        jnp.dot(jnp.concatenate([high, low]), v, preferred_element_type=f32)
        for high, low, v in zip(highs, lows, values)
    ]
    peaks = jnp.zeros((rows, LANES), f32)
    totals = jnp.zeros((rows, LANES), f32)
    for h, cols in enumerate(all_cols):
        num_ref[:, cols] = both[h][:rows] + both[h][rows:]
        peaks = jnp.where(lane == h, tops[h], peaks)
        totals = jnp.where(lane == h, sums[h], totals)
    export(num_ref, state_ref, pay_ref, peaks, totals)


def combine(num_ref, state_ref, pay_ref, out_ref):
    heads = num_ref.shape[1] // HD
    extra = pay_ref[:, heads * HD :].astype(jnp.float32)
    summed = extra + pltpu.roll(extra, LANES - SLOT, 1) + pltpu.roll(extra, LANES - 2 * SLOT, 1)
    other_total = pltpu.roll(summed, LANES - 3 * SLOT, 1)
    lane = lax.broadcasted_iota(jnp.int32, extra.shape, 1)
    used = lane < SLOT
    other_peak = jnp.where(used, summed, 0.0)
    other_total = jnp.where(used, other_total, 0.0)
    own_peak, own_total = state_ref[:, :LANES], state_ref[:, LANES:]
    peaks = jnp.maximum(own_peak, other_peak)
    own_factor = jnp.exp(own_peak - peaks)
    other_factor = jnp.exp(other_peak - peaks) * other_total
    totals = own_total * own_factor + other_factor
    for h in range(heads):
        cols = slice(h * HD, (h + 1) * HD)
        other = pay_ref[:, cols].astype(jnp.float32)
        out_ref[:, cols] = num_ref[:, cols] * own_factor[:, h : h + 1] + other * other_factor[:, h : h + 1]
    return peaks, totals


def merge_kernel(num_ref, state_ref, pay_ref, num_out, state_out, pay_out):
    for side in range(2):
        peaks, totals = combine(num_ref.at[side], state_ref.at[side], pay_ref.at[side], num_out.at[side])
        export(num_out.at[side], state_out.at[side], pay_out.at[side], peaks, totals)


def finish_kernel(num_ref, state_ref, pay_ref, out_ref, num):
    for side in range(2):
        _, totals = combine(num_ref.at[side], state_ref.at[side], pay_ref.at[side], num.at[side])
        for h in range(num.shape[2] // HD):
            cols = slice(h * HD, (h + 1) * HD)
            out_ref[side, :, cols] = (num[side, :, cols] / totals[:, h : h + 1]).astype(jnp.bfloat16)


def finish(num, state, pay):
    return pl.pallas_call(
        finish_kernel,
        out_shape=jax.ShapeDtypeStruct(num.shape, jnp.bfloat16),
        in_specs=[VM] * 3,
        out_specs=VM,
        scratch_shapes=[pltpu.VMEM(num.shape, jnp.float32)],
        compiler_params=pltpu.CompilerParams(vmem_limit_bytes=8 * MIB),
    )(num, state, pay)


def project_kernel(attended_ref, own_ref, other_ref, residual_ref, out_ref):
    rows = out_ref.shape[1]
    total = residual_ref[0].astype(jnp.float32)
    for side, weight_ref in enumerate((own_ref, other_ref)):
        for kind in range(2):
            part = jnp.dot(attended_ref[side], weight_ref[kind], preferred_element_type=jnp.float32)
            total = total + part[kind * rows : (kind + 1) * rows]
    out_ref[0] = total.astype(jnp.bfloat16)


def up_kernel(near_ref, far_ref, near_given_ref, far_given_ref, *refs):
    chunks, (hidden_ref, out_ref, kept, sem) = refs[:-4], refs[-4:]
    lead = lax.axis_index("tensor") == 1
    half, _, depth = near_ref.shape
    per = 2 * half // len(chunks)
    for j in range(half):
        kept[j] = jnp.where(lead, near_ref[j], near_given_ref[j])
        kept[half + j] = jnp.where(lead, far_ref[j], far_given_ref[j])
    copy = pltpu.make_async_copy(kept.at[0], hidden_ref, sem)
    copy.start()
    total = jnp.zeros(out_ref.shape, jnp.float32)
    for j in range(2 * half):
        weight = chunks[j // per][pl.ds(j % per * depth, depth), :]
        total = total + jnp.dot(kept[j], weight, preferred_element_type=jnp.float32)
    out_ref[...] = (0.5 * total * (1.0 + lax.erf(total * math.sqrt(0.5)))).astype(jnp.bfloat16)
    copy.wait()


def up(near, far, near_given, far_given, chunks, units):
    half, rows, columns = near.shape
    return pl.pallas_call(
        up_kernel,
        out_shape=(
            jax.ShapeDtypeStruct((rows, columns), jnp.bfloat16),
            jax.ShapeDtypeStruct((rows, units), jnp.bfloat16),
        ),
        in_specs=[VM] * (4 + len(chunks)),
        out_specs=(ANY, VM),
        scratch_shapes=[pltpu.VMEM((2 * half, rows, columns), jnp.bfloat16), pltpu.SemaphoreType.DMA],
        compiler_params=pltpu.CompilerParams(vmem_limit_bytes=8 * MIB),
    )(near, far, near_given, far_given, *chunks)


def reorder(activation):
    rows = activation.shape[0]
    position = lax.axis_index("batch")
    to = lax.broadcasted_iota(jnp.int32, (rows, rows), 0)
    source = lax.broadcasted_iota(jnp.int32, (rows, rows), 1)
    order = jnp.where(source == jnp.bitwise_xor(reverse(to, rows), position), 1.0, 0.0).astype(jnp.bfloat16)
    return jnp.dot(order, activation, preferred_element_type=jnp.float32).astype(jnp.bfloat16)


def down_kernel(mine, act_ref, weight_ref, *rest):
    depth = act_ref.shape[1]
    side = lax.axis_index("tensor")
    start = pl.multiple_of((side if mine else 1 - side) * depth, depth)
    part = jnp.dot(
        reorder(act_ref[...]), weight_ref[pl.ds(start, depth), :], preferred_element_type=jnp.float32
    )
    if mine:
        rest[0][...] = part
        return
    before, keep_ref, send_ref = rest
    total = before[...] + part
    half = total.shape[0] // 2
    keep_ref[...] = total[:half]
    send_ref[...] = total[half:]


def ring(devices):
    if devices > BEAMS:
        return list(range(BEAMS))
    return list(range(0, BEAMS, 2)) + list(range(BEAMS - 1, 0, -2))


def place_kernel(stride, order, gathered_ref, new_ref, parents_ref, lengths_ref, out_ref, row, sem):
    position = lax.axis_index("batch")
    request = lax.rem(position, stride)
    parent = parents_ref[0, position]
    place = jnp.int32(0)
    for k, beam in enumerate(order):
        place = jnp.where(parent == beam, k, place)
    place = jnp.where(lax.axis_index("tensor") == 1, BEAMS - 1 - place, place)
    copy = pltpu.make_async_copy(gathered_ref.at[place], row, sem)
    copy.start()
    slots = lax.broadcasted_iota(jnp.int32, row.shape[1:], 0)
    copy.wait()
    for kind in range(2):
        old = row[kind].astype(jnp.float32)
        new = new_ref[kind : kind + 1, :].astype(jnp.float32)
        out_ref[kind] = jnp.where(slots == lengths_ref[request], new, old).astype(jnp.bfloat16)


def place(stride, order, gathered, new_kv, parents, lengths):
    return pl.pallas_call(
        functools.partial(place_kernel, stride, order),
        out_shape=jax.ShapeDtypeStruct(gathered.shape[1:], gathered.dtype),
        in_specs=[ANY, VM, SM, SM],
        out_specs=VM,
        scratch_shapes=[pltpu.VMEM(gathered.shape[1:], gathered.dtype), pltpu.SemaphoreType.DMA],
        compiler_params=pltpu.CompilerParams(vmem_limit_bytes=8 * MIB),
    )(in_hbm(gathered), new_kv, parents, lengths)


def body(
    init_cache,
    memory,
    queries,
    new_kv,
    residual,
    out_weight,
    up_weight,
    down_weight,
    parents,
    lengths,
):
    devices = lax.axis_size("batch")
    stride = devices // BEAMS
    position = lax.axis_index("batch")
    request = position % stride
    width = queries.shape[-1]
    rows = parents.shape[1]
    columns = out_weight.shape[2]
    hidden_units = up_weight.shape[1]
    out_columns = down_weight.shape[1]
    f32, bf16 = jnp.float32, jnp.bfloat16
    shape = jax.ShapeDtypeStruct
    down_weight = pltpu.with_memory_space_constraint(down_weight, pltpu.VMEM)
    per = devices // PIECES
    chunks = []

    def load_up(count):
        def work(buffer, other):
            loaded = []
            for _ in range(count):
                first = (len(chunks) + len(loaded)) * per
                loaded.append(fetch_rows(in_hbm(up_weight), first, per, devices, buffer))
            other, loaded = pin(other, loaded)
            chunks.extend(loaded)
            return other

        return work

    def load_out(buffer, other):
        other, local["out"] = pin(other, fetch([in_hbm(out_weight)], buffer)[0])
        return other

    local = {}
    plan = [load_out, load_up(1), load_up(1), load_up(2), load_up(1), load_up(2), load_up(1)]

    def work(buffer, other):
        return plan.pop(0)(buffer, other) if plan else other

    query_other = hand(queries[0, 0], 1)
    sources = (queries[0, 0], init_cache[0], memory[0], new_kv[0, 0], residual)
    loaded = fetch([in_hbm(x) for x in sources], queries[0, 0])
    cache_other, memory_other, new_other = (hand(x, 1) for x in (init_cache[0], memory[0], new_kv[0, 0]))
    out_other = hand(out_weight, 1)
    query_other, loaded = pin(query_other, loaded)
    query, cache_row, memory_row, new_row, residual_row = loaded
    near, far = doubling(jnp.concatenate([query, query_other]), stride, devices, work)
    state_shapes = (
        shape((2, 2 * BEAMS, width), f32),
        shape((2, 2 * BEAMS, 2 * LANES), f32),
        shape((2, 2 * BEAMS, width + LANES), bf16),
    )
    num, state, pay = call(
        functools.partial(attend_kernel, stride),
        state_shapes,
        near,
        far,
        cache_row,
        memory_row,
        new_row,
        cache_other,
        memory_other,
        new_other,
        parents,
        lengths,
        specs=[VM] * 8 + [SM] * 2,
    )
    bit = stride
    while True:
        arrived = work(pay, lead_permute(pay, bit))
        bit *= 2
        if bit == devices:
            break
        num, state, pay = call(merge_kernel, state_shapes, num, state, arrived)
    attended = finish(num, state, arrived)
    if stride > 1:
        pair = doubling(attended[None], 1, stride, lambda buffer, other: other)
        wanted = reverse(jnp.bitwise_xor(jnp.arange(stride, dtype=jnp.int32), request), stride)
        stacked = jnp.concatenate(pair)[wanted].reshape(stride, 2, 2, BEAMS, width)
        attended = stacked.transpose(1, 2, 3, 0, 4).reshape(2, 2 * rows, width)

    mine = call(
        project_kernel,
        pltpu.VMEM((1, rows, columns), bf16),
        attended,
        local["out"],
        out_other,
        residual_row,
    )
    near, far = doubling(mine, 1, devices, work)
    while len(chunks) < PIECES:
        near = load_up(1)(near, near)
    hidden, activation = up(near, far, hand(near, 0), hand(far, 0), chunks, hidden_units)
    arrived = xor_permute(activation, "tensor", 1)
    before = call(
        functools.partial(down_kernel, True), shape((rows, out_columns), f32), activation, down_weight
    )
    keep, send = call(
        functools.partial(down_kernel, False),
        (shape((rows // 2, out_columns), f32),) * 2,
        arrived,
        down_weight,
        before,
    )
    bit = 1
    while True:
        total = keep + xor_permute(send, "batch", bit)
        bit *= 2
        if bit == devices:
            break
        half = total.shape[0] // 2
        keep, send = total[:half], total[half:]
    ffn_row = total.astype(bf16)

    order = ring(devices)
    groups = []
    for r in range(stride):
        groups.append([(beam * stride + r) * 2 for beam in order])
        groups.append([(beam * stride + r) * 2 + 1 for beam in reversed(order)])
    gathered = lax.all_gather(init_cache[0], ("batch", "tensor"), axis_index_groups=groups)
    cache = place(stride, order, gathered, new_row, parents, lengths)
    return (hidden[None], ffn_row[None], cache[None])


def solution(mesh):
    placed = (
        P(("grp", "batch"), None, None, "tensor"),
        P(("grp", "batch"), None, None, "tensor"),
        P(None, ("grp", "batch"), None, "tensor"),
        P(None, ("grp", "batch"), None, "tensor"),
        P(None, "grp", "batch"),
        P(None, "tensor", "batch"),
        P(None, ("batch", "tensor")),
        P("batch", "tensor"),
        P(None, "grp"),
        P("grp"),
    )
    return jax.shard_map(
        body,
        mesh=mesh,
        in_specs=placed,
        out_specs=(
            P(None, "grp", "batch"),
            P(None, ("grp", "batch"), "tensor"),
            P(("grp", "batch"), None, None, "tensor"),
        ),
        check_vma=False,
    )
```

```python
import functools
import math

import jax
import jax.numpy as jnp
from jax import lax
from jax.experimental import pallas as pl
from jax.experimental.pallas import tpu as pltpu
from jax.sharding import PartitionSpec as P

HD = 128
LANES = 128
SLOT = 16
BEAMS = 8
LOW = -1e30
MIB = 1024 * 1024
BUFFERS = 3
STEP_BYTES = 16 * MIB

VM = pl.BlockSpec(memory_space=pltpu.VMEM)
SM = pl.BlockSpec(memory_space=pltpu.SMEM)
ANY = pl.BlockSpec(memory_space=pl.ANY)


def xor_permute(value, axis, bit):
    total = lax.axis_size(axis)
    return lax.ppermute(value, axis, [(i, i ^ bit) for i in range(total)])


def reverse(index, size):
    bits = size.bit_length() - 1
    return sum(((index >> k) & 1) << (bits - 1 - k) for k in range(bits))


def doubling(buffer, first, last):
    bit = last
    while True:
        bit //= 2
        other = xor_permute(buffer, "batch", bit)
        if bit == first:
            return buffer, other
        buffer = jnp.concatenate([buffer, other])


def call(kernel, out, *args, specs=None, vmem=8, flops=0, moved=STEP_BYTES):
    return pl.pallas_call(
        kernel,
        out_shape=out,
        in_specs=specs or [VM] * len(args),
        out_specs=jax.tree.map(lambda _: VM, out),
        compiler_params=pltpu.CompilerParams(vmem_limit_bytes=vmem * MIB),
        cost_estimate=pl.CostEstimate(flops=flops, bytes_accessed=moved, transcendentals=0),
    )(*args)


def in_hbm(value):
    return pltpu.with_memory_space_constraint(value, pltpu.HBM)


def pin(value, loaded):
    return lax.optimization_barrier((value, loaded))


def start_all(copies):
    for copy in copies:
        copy.start()
    for copy in copies:
        copy.wait()


def fetch_kernel(count, *refs):
    sems = refs[-1]
    outs = refs[-1 - count : -1]
    copies = []
    for i in range(count):
        parts = refs[i].shape[0] if len(refs[i].shape) > 2 else 1
        for k in range(parts):
            source, target = (refs[i].at[k], outs[i].at[k]) if parts > 1 else (refs[i], outs[i])
            copies.append(pltpu.make_async_copy(source, target, sems.at[i, k]))
    start_all(copies)


def fetch(arrays, after):
    count = len(arrays)
    return pl.pallas_call(
        functools.partial(fetch_kernel, count),
        out_shape=[pltpu.VMEM(x.shape, x.dtype) for x in arrays],
        in_specs=[ANY] * (count + 1),
        out_specs=[VM] * count,
        scratch_shapes=[pltpu.SemaphoreType.DMA((count, 2))],
        compiler_params=pltpu.CompilerParams(vmem_limit_bytes=2 * MIB),
        cost_estimate=pl.CostEstimate(flops=0, bytes_accessed=2 * MIB, transcendentals=0),
    )(*arrays, after)


class Stream:
    def __init__(self, pieces, buffers, sems):
        self.pieces, self.buffers, self.sems = pieces, buffers, sems
        for k in range(min(BUFFERS, len(pieces))):
            self.copy(k).start()

    def copy(self, k):
        slot = k % BUFFERS
        return pltpu.make_async_copy(self.pieces[k], self.buffers.at[slot], self.sems.at[slot])

    def take(self, k, use):
        self.copy(k).wait()
        result = use(self.buffers[k % BUFFERS])
        if k + BUFFERS < len(self.pieces):
            self.copy(k + BUFFERS).start()
        return result


def stream_call(kernel, out, *args, weight, piece, extra=()):
    specs = [VM] * len(args) + [ANY] * (1 + len(extra))
    return pl.pallas_call(
        kernel,
        out_shape=out,
        in_specs=specs,
        out_specs=jax.tree.map(lambda _: VM, out),
        scratch_shapes=[pltpu.VMEM((BUFFERS, *piece), weight.dtype), pltpu.SemaphoreType.DMA((BUFFERS,))],
        compiler_params=pltpu.CompilerParams(vmem_limit_bytes=12 * MIB),
        cost_estimate=pl.CostEstimate(flops=0, bytes_accessed=weight.size * 2, transcendentals=0),
    )(*args, weight, *extra)


def split3(value):
    high = value.astype(jnp.bfloat16).astype(jnp.float32)
    rest = value - high
    middle = rest.astype(jnp.bfloat16).astype(jnp.float32)
    return high, middle, rest - middle


def export(num_ref, state_ref, pay_ref, peaks, totals):
    heads = num_ref.shape[1] // HD
    inverse = jnp.where(totals > 0.0, 1.0 / jnp.where(totals > 0.0, totals, 1.0), 0.0)
    for h in range(heads):
        cols = slice(h * HD, (h + 1) * HD)
        pay_ref[:, cols] = (num_ref[:, cols] * inverse[:, h : h + 1]).astype(jnp.bfloat16)
    state_ref[:, :LANES] = peaks
    state_ref[:, LANES:] = totals
    group = lax.broadcasted_iota(jnp.int32, peaks.shape, 1) // SLOT
    extra = jnp.zeros_like(peaks)
    for g, part in enumerate(split3(peaks) + split3(totals)):
        extra = jnp.where(group == g, pltpu.roll(part, g * SLOT, 1) if g else part, extra)
    pay_ref[:, heads * HD :] = extra.astype(jnp.bfloat16)


def attend_kernel(
    stride, near_ref, far_ref, cache_ref, memory_ref, new_ref, parents_ref, lengths_ref, num_ref, state_ref, pay_ref
):
    position = lax.axis_index("batch")
    own, request = position // stride, lax.rem(position, stride)
    length = lengths_ref[request]
    rows, width = num_ref.shape
    heads = width // HD
    past = cache_ref.shape[1]
    span = past + memory_ref.shape[1]
    f32, bf16 = jnp.float32, jnp.bfloat16

    to = lax.broadcasted_iota(jnp.int32, (rows, BEAMS), 0)
    source = lax.broadcasted_iota(jnp.int32, (rows, BEAMS), 1)

    def place_rows(piece_ref, first):
        beam = jnp.bitwise_xor(reverse(first + source // 2, BEAMS), own)
        order = jnp.where(to == (source % 2) * BEAMS + beam, 1.0, 0.0).astype(bf16)
        return jnp.dot(order, piece_ref[...], preferred_element_type=f32)

    query = (place_rows(near_ref, 0) + place_rows(far_ref, BEAMS // 2)).astype(bf16)

    row = lax.broadcasted_iota(jnp.int32, (rows, span), 0)
    slot = lax.broadcasted_iota(jnp.int32, (rows, span), 1)
    parent = jnp.zeros_like(row)
    for b in range(BEAMS):
        parent = jnp.where(row == b, parents_ref[0, b * stride + request], parent)
    in_past = ((slot < length) & (parent == own)) | ((slot == length) & (row == own))
    valid = jnp.where(row < BEAMS, jnp.where(in_past, 1, 0), jnp.where(slot >= past, 1, 0)) == 1
    fresh = lax.broadcasted_iota(jnp.int32, (past, HD), 0) == length
    lane = lax.broadcasted_iota(jnp.int32, (rows, LANES), 1)
    all_cols = [slice(h * HD, (h + 1) * HD) for h in range(heads)]

    def block(kind, cols):
        old = cache_ref[kind, :, cols].astype(f32)
        new = new_ref[kind : kind + 1, cols].astype(f32)
        merged = jnp.where(fresh, new, old).astype(bf16)
        return jnp.concatenate([merged, memory_ref[kind, :, cols]])

    scores = [
        lax.dot_general(
            query[:, cols], block(0, cols), (((1,), (1,)), ((), ())), preferred_element_type=f32
        )
        for cols in all_cols
    ]
    values = [block(1, cols) for cols in all_cols]
    scores = [jnp.where(valid, s * (1.0 / math.sqrt(HD)), LOW) for s in scores]
    tops = [jnp.max(s, axis=1, keepdims=True) for s in scores]
    weights = [jnp.where(valid, jnp.exp(s - t), 0.0) for s, t in zip(scores, tops)]
    sums = [jnp.sum(w, axis=1, keepdims=True) for w in weights]
    highs = [w.astype(bf16) for w in weights]
    lows = [(w - high.astype(f32)).astype(bf16) for w, high in zip(weights, highs)]
    both = [
        jnp.dot(jnp.concatenate([high, low]), v, preferred_element_type=f32)
        for high, low, v in zip(highs, lows, values)
    ]
    peaks = jnp.zeros((rows, LANES), f32)
    totals = jnp.zeros((rows, LANES), f32)
    for h, cols in enumerate(all_cols):
        num_ref[:, cols] = both[h][:rows] + both[h][rows:]
        peaks = jnp.where(lane == h, tops[h], peaks)
        totals = jnp.where(lane == h, sums[h], totals)
    export(num_ref, state_ref, pay_ref, peaks, totals)


def combine(num_ref, state_ref, pay_ref, out_ref):
    heads = num_ref.shape[1] // HD
    extra = pay_ref[:, heads * HD :].astype(jnp.float32)
    summed = extra + pltpu.roll(extra, LANES - SLOT, 1) + pltpu.roll(extra, LANES - 2 * SLOT, 1)
    other_total = pltpu.roll(summed, LANES - 3 * SLOT, 1)
    lane = lax.broadcasted_iota(jnp.int32, extra.shape, 1)
    used = lane < SLOT
    other_peak = jnp.where(used, summed, 0.0)
    other_total = jnp.where(used, other_total, 0.0)
    own_peak, own_total = state_ref[:, :LANES], state_ref[:, LANES:]
    peaks = jnp.maximum(own_peak, other_peak)
    own_factor = jnp.exp(own_peak - peaks)
    other_factor = jnp.exp(other_peak - peaks) * other_total
    totals = own_total * own_factor + other_factor
    for h in range(heads):
        cols = slice(h * HD, (h + 1) * HD)
        other = pay_ref[:, cols].astype(jnp.float32)
        out_ref[:, cols] = num_ref[:, cols] * own_factor[:, h : h + 1] + other * other_factor[:, h : h + 1]
    return peaks, totals


def merge_kernel(num_ref, state_ref, pay_ref, num_out, state_out, pay_out):
    peaks, totals = combine(num_ref, state_ref, pay_ref, num_out)
    export(num_out, state_out, pay_out, peaks, totals)


def finish_kernel(num_ref, state_ref, pay_ref, out_ref, num):
    _, totals = combine(num_ref, state_ref, pay_ref, num)
    for h in range(num.shape[1] // HD):
        cols = slice(h * HD, (h + 1) * HD)
        out_ref[:, cols] = (num[:, cols] / totals[:, h : h + 1]).astype(jnp.bfloat16)


def finish(num, state, pay):
    return pl.pallas_call(
        finish_kernel,
        out_shape=jax.ShapeDtypeStruct(num.shape, jnp.bfloat16),
        in_specs=[VM] * 3,
        out_specs=VM,
        scratch_shapes=[pltpu.VMEM(num.shape, jnp.float32)],
        compiler_params=pltpu.CompilerParams(vmem_limit_bytes=8 * MIB),
        cost_estimate=pl.CostEstimate(flops=0, bytes_accessed=STEP_BYTES, transcendentals=0),
    )(num, state, pay)


def project_kernel(attended_ref, weight_ref, out_ref):
    rows = out_ref.shape[0]
    first = jnp.dot(attended_ref[...], weight_ref[0], preferred_element_type=jnp.float32)
    second = jnp.dot(attended_ref[...], weight_ref[1], preferred_element_type=jnp.float32)
    out_ref[...] = first[:rows] + second[rows:]


def add_kernel(own_ref, other_ref, residual_ref, out_ref):
    total = residual_ref[0].astype(jnp.float32) + (own_ref[...] + other_ref[...])
    out_ref[0] = total.astype(jnp.bfloat16)


def up_kernel(last, hidden_ref, *refs):
    half, _, depth = hidden_ref.shape
    if last:
        before_ref, weight_ref, _, out_ref, buffers, sems = refs
    else:
        weight_ref, own_ref, out_ref, buffers, sems = refs
        own_ref[...] = hidden_ref[0]
    position = lax.axis_index("batch")
    pieces = []
    for j in range(half):
        index = reverse(j + half if last else j, 2 * half)
        start = pl.multiple_of(jnp.bitwise_xor(position, index) * depth, depth)
        pieces.append(weight_ref.at[pl.ds(start, depth), :])
    stream = Stream(pieces, buffers, sems)
    total = before_ref[...] if last else jnp.zeros(out_ref.shape, jnp.float32)
    for j in range(half):
        total = total + stream.take(
            j, lambda weight: jnp.dot(hidden_ref[j], weight, preferred_element_type=jnp.float32)
        )
    if last:
        total = (0.5 * total * (1.0 + lax.erf(total * math.sqrt(0.5)))).astype(jnp.bfloat16)
    out_ref[...] = total


def reorder(activation):
    rows = activation.shape[0]
    position = lax.axis_index("batch")
    to = lax.broadcasted_iota(jnp.int32, (rows, rows), 0)
    source = lax.broadcasted_iota(jnp.int32, (rows, rows), 1)
    order = jnp.where(source == jnp.bitwise_xor(reverse(to, rows), position), 1.0, 0.0).astype(jnp.bfloat16)
    return jnp.dot(order, activation, preferred_element_type=jnp.float32).astype(jnp.bfloat16)


def down_kernel(mine, act_ref, *refs):
    if mine:
        weight_ref, out_ref, buffers, sems = refs
    else:
        before_ref, weight_ref, keep_ref, send_ref, buffers, sems = refs
    depth = act_ref.shape[1]
    count = depth // buffers.shape[1]
    step = buffers.shape[1]
    side = lax.axis_index("tensor")
    base = (side if mine else 1 - side) * depth
    stream = Stream(
        [weight_ref.at[pl.ds(pl.multiple_of(base + k * step, step), step), :] for k in range(count)], buffers, sems
    )
    activation = reorder(act_ref[...])
    total = None if mine else before_ref[...]
    for k in range(count):
        block = activation[:, k * step : (k + 1) * step]
        part = stream.take(k, lambda weight: jnp.dot(block, weight, preferred_element_type=jnp.float32))
        total = part if total is None else total + part
    if mine:
        out_ref[...] = total
        return
    half = total.shape[0] // 2
    keep_ref[...] = total[:half]
    send_ref[...] = total[half:]


def ring(devices):
    if devices > BEAMS:
        return list(range(BEAMS))
    return list(range(0, BEAMS, 2)) + list(range(BEAMS - 1, 0, -2))


def place_kernel(stride, order, gathered_ref, new_ref, parents_ref, lengths_ref, out_ref, row, sem):
    position = lax.axis_index("batch")
    request = lax.rem(position, stride)
    parent = parents_ref[0, position]
    place = jnp.int32(0)
    for k, beam in enumerate(order):
        place = jnp.where(parent == beam, k, place)
    place = jnp.where(lax.axis_index("tensor") == 1, BEAMS - 1 - place, place)
    copy = pltpu.make_async_copy(gathered_ref.at[place], row, sem)
    copy.start()
    slots = lax.broadcasted_iota(jnp.int32, row.shape[1:], 0)
    copy.wait()
    for kind in range(2):
        old = row[kind].astype(jnp.float32)
        new = new_ref[kind : kind + 1, :].astype(jnp.float32)
        out_ref[kind] = jnp.where(slots == lengths_ref[request], new, old).astype(jnp.bfloat16)


def place(stride, order, gathered, new_kv, parents, lengths):
    return pl.pallas_call(
        functools.partial(place_kernel, stride, order),
        out_shape=jax.ShapeDtypeStruct(gathered.shape[1:], gathered.dtype),
        in_specs=[ANY, VM, SM, SM],
        out_specs=VM,
        scratch_shapes=[pltpu.VMEM(gathered.shape[1:], gathered.dtype), pltpu.SemaphoreType.DMA],
        compiler_params=pltpu.CompilerParams(vmem_limit_bytes=8 * MIB),
    )(in_hbm(gathered), new_kv, parents, lengths)


def body(
    init_cache,
    memory,
    queries,
    new_kv,
    residual,
    out_weight,
    up_weight,
    down_weight,
    parents,
    lengths,
):
    devices = lax.axis_size("batch")
    stride = devices // BEAMS
    position = lax.axis_index("batch")
    request = position % stride
    width = queries.shape[-1]
    rows = parents.shape[1]
    columns = out_weight.shape[2]
    hidden_units = up_weight.shape[1]
    out_columns = down_weight.shape[1]
    f32, bf16 = jnp.float32, jnp.bfloat16
    shape = jax.ShapeDtypeStruct
    up_weight = in_hbm(up_weight)
    sources = (queries[0, 0], init_cache[0], memory[0], new_kv[0, 0], residual)
    bit = devices // 2
    other = xor_permute(queries[0, 0], "batch", bit)
    loaded = fetch([in_hbm(x) for x in sources], queries[0, 0])
    other, (query, cache_row, memory_row, new_row, residual_row) = pin(other, loaded)
    query, far = doubling(jnp.concatenate([query, other]), stride, bit)
    state_shapes = (
        shape((2 * BEAMS, width), f32),
        shape((2 * BEAMS, 2 * LANES), f32),
        shape((2 * BEAMS, width + LANES), bf16),
    )
    num, state, pay = call(
        functools.partial(attend_kernel, stride),
        state_shapes,
        query,
        far,
        cache_row,
        memory_row,
        new_row,
        parents,
        lengths,
        specs=[VM] * 5 + [SM] * 2,
    )
    bit = stride
    while True:
        arrived = xor_permute(pay, "batch", bit)
        if bit == stride:
            arrived, (out_row,) = pin(arrived, fetch([in_hbm(out_weight)], pay))
        bit *= 2
        if bit == devices:
            break
        num, state, pay = call(merge_kernel, state_shapes, num, state, arrived)
    attended = finish(num, state, arrived)
    if stride > 1:
        stacked = jnp.concatenate(doubling(attended[None], 1, stride))
        wanted = reverse(jnp.bitwise_xor(jnp.arange(stride, dtype=jnp.int32), request), stride)
        stacked = stacked[wanted].reshape(stride, 2, BEAMS, width)
        attended = stacked.transpose(1, 2, 0, 3).reshape(2 * rows, width)

    partial = call(project_kernel, shape((rows, columns), f32), attended, out_row)
    other = xor_permute(partial, "tensor", 1)
    mine = call(add_kernel, pltpu.VMEM((1, rows, columns), bf16), partial, other, residual_row)
    near, far = doubling(mine, 1, devices)
    piece = (columns, hidden_units)
    hidden, first_half = stream_call(
        functools.partial(up_kernel, False),
        (shape((rows, columns), bf16), shape((rows, hidden_units), f32)),
        near,
        weight=up_weight,
        piece=piece,
    )
    far, first_half = pin(far, first_half)
    activation = stream_call(
        functools.partial(up_kernel, True),
        shape((rows, hidden_units), bf16),
        far,
        first_half,
        weight=up_weight,
        piece=piece,
        extra=(down_weight,),
    )
    arrived = xor_permute(activation, "tensor", 1)
    piece = (hidden_units // min(4, hidden_units // LANES or 1), out_columns)
    before = stream_call(
        functools.partial(down_kernel, True),
        shape((rows, out_columns), f32),
        activation,
        weight=down_weight,
        piece=piece,
    )
    keep, send = stream_call(
        functools.partial(down_kernel, False),
        (shape((rows // 2, out_columns), f32),) * 2,
        arrived,
        before,
        weight=down_weight,
        piece=piece,
    )
    bit = 1
    while True:
        total = keep + xor_permute(send, "batch", bit)
        bit *= 2
        if bit == devices:
            break
        half = total.shape[0] // 2
        keep, send = total[:half], total[half:]
    ffn_row = total.astype(bf16)

    order = ring(devices)
    groups = []
    for r in range(stride):
        groups.append([(beam * stride + r) * 2 for beam in order])
        groups.append([(beam * stride + r) * 2 + 1 for beam in reversed(order)])
    gathered = lax.all_gather(init_cache[0], ("batch", "tensor"), axis_index_groups=groups)
    cache = place(stride, order, gathered, new_row, parents, lengths)
    return (hidden[None], ffn_row[None], cache[None])


def solution(mesh):
    placed = (
        P(("grp", "batch"), None, None, "tensor"),
        P(("grp", "batch"), None, None, "tensor"),
        P(None, ("grp", "batch"), None, "tensor"),
        P(None, ("grp", "batch"), None, "tensor"),
        P(None, "grp", "batch"),
        P(None, "tensor", "batch"),
        P(None, ("batch", "tensor")),
        P("batch", "tensor"),
        P(None, "grp"),
        P("grp"),
    )
    return jax.shard_map(
        body,
        mesh=mesh,
        in_specs=placed,
        out_specs=(
            P(None, "grp", "batch"),
            P(None, ("grp", "batch"), "tensor"),
            P(("grp", "batch"), None, None, "tensor"),
        ),
        check_vma=False,
    )
```

```python
import functools
import math

import jax
import jax.numpy as jnp
from jax import lax
from jax.experimental import pallas as pl
from jax.experimental.pallas import tpu as pltpu
from jax.sharding import PartitionSpec as P

HD = 128
LANES = 128
SLOT = 16
BEAMS = 8
LOW = -1e30
MIB = 1024 * 1024
SPLIT = 2
STEP_BYTES = 16 * MIB

VM = pl.BlockSpec(memory_space=pltpu.VMEM)
SM = pl.BlockSpec(memory_space=pltpu.SMEM)
ANY = pl.BlockSpec(memory_space=pl.ANY)


def xor_permute(value, axis, bit):
    total = lax.axis_size(axis)
    return lax.ppermute(value, axis, [(i, i ^ bit) for i in range(total)])


def reverse(index, size):
    bits = size.bit_length() - 1
    return sum(((index >> k) & 1) << (bits - 1 - k) for k in range(bits))


def doubling(buffer, first, last):
    bit = last
    while True:
        bit //= 2
        other = xor_permute(buffer, "batch", bit)
        if bit == first:
            return buffer, other
        buffer = jnp.concatenate([buffer, other])


def call(kernel, out, *args, specs=None, vmem=8, flops=0, moved=STEP_BYTES):
    return pl.pallas_call(
        kernel,
        out_shape=out,
        in_specs=specs or [VM] * len(args),
        out_specs=jax.tree.map(lambda _: VM, out),
        compiler_params=pltpu.CompilerParams(vmem_limit_bytes=vmem * MIB),
        cost_estimate=pl.CostEstimate(flops=flops, bytes_accessed=moved, transcendentals=0),
    )(*args)


def in_hbm(value):
    return pltpu.with_memory_space_constraint(value, pltpu.HBM)


def pin(value, loaded):
    return lax.optimization_barrier((value, loaded))


def start_all(copies):
    for copy in copies:
        copy.start()
    for copy in copies:
        copy.wait()


def fetch_kernel(count, *refs):
    sems = refs[-1]
    outs = refs[-1 - count : -1]
    copies = []
    for i in range(count):
        parts = refs[i].shape[0] if len(refs[i].shape) > 2 else 1
        for k in range(parts):
            source, target = (refs[i].at[k], outs[i].at[k]) if parts > 1 else (refs[i], outs[i])
            copies.append(pltpu.make_async_copy(source, target, sems.at[i, k]))
    start_all(copies)


def fetch(arrays, after):
    count = len(arrays)
    return pl.pallas_call(
        functools.partial(fetch_kernel, count),
        out_shape=[pltpu.VMEM(x.shape, x.dtype) for x in arrays],
        in_specs=[ANY] * (count + 1),
        out_specs=[VM] * count,
        scratch_shapes=[pltpu.SemaphoreType.DMA((count, 2))],
        compiler_params=pltpu.CompilerParams(vmem_limit_bytes=2 * MIB),
        cost_estimate=pl.CostEstimate(flops=0, bytes_accessed=2 * MIB, transcendentals=0),
    )(*arrays, after)


class Stream:
    def __init__(self, pieces, buffers, sems):
        self.buffers = buffers
        self.copies = [
            pltpu.make_async_copy(piece, buffers.at[k], sems.at[k]) for k, piece in enumerate(pieces)
        ]
        for copy in self.copies:
            copy.start()

    def take(self, k):
        self.copies[k].wait()
        return self.buffers[k]


def stream_call(kernel, out, *args, weight, count, piece, extra=()):
    specs = [VM] * len(args) + [ANY] * (1 + len(extra))
    return pl.pallas_call(
        kernel,
        out_shape=out,
        in_specs=specs,
        out_specs=jax.tree.map(lambda _: VM, out),
        scratch_shapes=[pltpu.VMEM((count, *piece), weight.dtype), pltpu.SemaphoreType.DMA((count,))],
        compiler_params=pltpu.CompilerParams(vmem_limit_bytes=14 * MIB),
        cost_estimate=pl.CostEstimate(flops=0, bytes_accessed=weight.size * 2, transcendentals=0),
    )(*args, weight, *extra)


def split3(value):
    high = value.astype(jnp.bfloat16).astype(jnp.float32)
    rest = value - high
    middle = rest.astype(jnp.bfloat16).astype(jnp.float32)
    return high, middle, rest - middle


def export(num_ref, state_ref, pay_ref, peaks, totals):
    heads = num_ref.shape[1] // HD
    inverse = jnp.where(totals > 0.0, 1.0 / jnp.where(totals > 0.0, totals, 1.0), 0.0)
    for h in range(heads):
        cols = slice(h * HD, (h + 1) * HD)
        pay_ref[:, cols] = (num_ref[:, cols] * inverse[:, h : h + 1]).astype(jnp.bfloat16)
    state_ref[:, :LANES] = peaks
    state_ref[:, LANES:] = totals
    group = lax.broadcasted_iota(jnp.int32, peaks.shape, 1) // SLOT
    extra = jnp.zeros_like(peaks)
    for g, part in enumerate(split3(peaks) + split3(totals)):
        extra = jnp.where(group == g, pltpu.roll(part, g * SLOT, 1) if g else part, extra)
    pay_ref[:, heads * HD :] = extra.astype(jnp.bfloat16)


def attend_kernel(
    stride, near_ref, far_ref, cache_ref, memory_ref, new_ref, parents_ref, lengths_ref, num_ref, state_ref, pay_ref
):
    position = lax.axis_index("batch")
    own, request = position // stride, lax.rem(position, stride)
    length = lengths_ref[request]
    rows, width = num_ref.shape
    heads = width // HD
    past = cache_ref.shape[1]
    span = past + memory_ref.shape[1]
    f32, bf16 = jnp.float32, jnp.bfloat16

    to = lax.broadcasted_iota(jnp.int32, (rows, BEAMS), 0)
    source = lax.broadcasted_iota(jnp.int32, (rows, BEAMS), 1)

    def place_rows(piece_ref, first):
        beam = jnp.bitwise_xor(reverse(first + source // 2, BEAMS), own)
        order = jnp.where(to == (source % 2) * BEAMS + beam, 1.0, 0.0).astype(bf16)
        return jnp.dot(order, piece_ref[...], preferred_element_type=f32)

    query = (place_rows(near_ref, 0) + place_rows(far_ref, BEAMS // 2)).astype(bf16)

    row = lax.broadcasted_iota(jnp.int32, (rows, span), 0)
    slot = lax.broadcasted_iota(jnp.int32, (rows, span), 1)
    parent = jnp.zeros_like(row)
    for b in range(BEAMS):
        parent = jnp.where(row == b, parents_ref[0, b * stride + request], parent)
    in_past = ((slot < length) & (parent == own)) | ((slot == length) & (row == own))
    valid = jnp.where(row < BEAMS, jnp.where(in_past, 1, 0), jnp.where(slot >= past, 1, 0)) == 1
    fresh = lax.broadcasted_iota(jnp.int32, (past, HD), 0) == length
    lane = lax.broadcasted_iota(jnp.int32, (rows, LANES), 1)
    all_cols = [slice(h * HD, (h + 1) * HD) for h in range(heads)]

    def block(kind, cols):
        old = cache_ref[kind, :, cols].astype(f32)
        new = new_ref[kind : kind + 1, cols].astype(f32)
        merged = jnp.where(fresh, new, old).astype(bf16)
        return jnp.concatenate([merged, memory_ref[kind, :, cols]])

    scores = [
        lax.dot_general(
            query[:, cols], block(0, cols), (((1,), (1,)), ((), ())), preferred_element_type=f32
        )
        for cols in all_cols
    ]
    values = [block(1, cols) for cols in all_cols]
    scores = [jnp.where(valid, s * (1.0 / math.sqrt(HD)), LOW) for s in scores]
    tops = [jnp.max(s, axis=1, keepdims=True) for s in scores]
    weights = [jnp.where(valid, jnp.exp(s - t), 0.0) for s, t in zip(scores, tops)]
    sums = [jnp.sum(w, axis=1, keepdims=True) for w in weights]
    highs = [w.astype(bf16) for w in weights]
    lows = [(w - high.astype(f32)).astype(bf16) for w, high in zip(weights, highs)]
    both = [
        jnp.dot(jnp.concatenate([high, low]), v, preferred_element_type=f32)
        for high, low, v in zip(highs, lows, values)
    ]
    peaks = jnp.zeros((rows, LANES), f32)
    totals = jnp.zeros((rows, LANES), f32)
    for h, cols in enumerate(all_cols):
        num_ref[:, cols] = both[h][:rows] + both[h][rows:]
        peaks = jnp.where(lane == h, tops[h], peaks)
        totals = jnp.where(lane == h, sums[h], totals)
    export(num_ref, state_ref, pay_ref, peaks, totals)


def combine(num_ref, state_ref, pay_ref, out_ref):
    heads = num_ref.shape[1] // HD
    extra = pay_ref[:, heads * HD :].astype(jnp.float32)
    summed = extra + pltpu.roll(extra, LANES - SLOT, 1) + pltpu.roll(extra, LANES - 2 * SLOT, 1)
    other_total = pltpu.roll(summed, LANES - 3 * SLOT, 1)
    lane = lax.broadcasted_iota(jnp.int32, extra.shape, 1)
    used = lane < SLOT
    other_peak = jnp.where(used, summed, 0.0)
    other_total = jnp.where(used, other_total, 0.0)
    own_peak, own_total = state_ref[:, :LANES], state_ref[:, LANES:]
    peaks = jnp.maximum(own_peak, other_peak)
    own_factor = jnp.exp(own_peak - peaks)
    other_factor = jnp.exp(other_peak - peaks) * other_total
    totals = own_total * own_factor + other_factor
    for h in range(heads):
        cols = slice(h * HD, (h + 1) * HD)
        other = pay_ref[:, cols].astype(jnp.float32)
        out_ref[:, cols] = num_ref[:, cols] * own_factor[:, h : h + 1] + other * other_factor[:, h : h + 1]
    return peaks, totals


def merge_kernel(num_ref, state_ref, pay_ref, num_out, state_out, pay_out):
    peaks, totals = combine(num_ref, state_ref, pay_ref, num_out)
    export(num_out, state_out, pay_out, peaks, totals)


def finish_kernel(num_ref, state_ref, pay_ref, out_ref, num):
    _, totals = combine(num_ref, state_ref, pay_ref, num)
    for h in range(num.shape[1] // HD):
        cols = slice(h * HD, (h + 1) * HD)
        out_ref[:, cols] = (num[:, cols] / totals[:, h : h + 1]).astype(jnp.bfloat16)


def finish(num, state, pay):
    return pl.pallas_call(
        finish_kernel,
        out_shape=jax.ShapeDtypeStruct(num.shape, jnp.bfloat16),
        in_specs=[VM] * 3,
        out_specs=VM,
        scratch_shapes=[pltpu.VMEM(num.shape, jnp.float32)],
        compiler_params=pltpu.CompilerParams(vmem_limit_bytes=8 * MIB),
        cost_estimate=pl.CostEstimate(flops=0, bytes_accessed=STEP_BYTES, transcendentals=0),
    )(num, state, pay)


def project_kernel(attended_ref, weight_ref, out_ref):
    rows = out_ref.shape[0]
    first = jnp.dot(attended_ref[...], weight_ref[0], preferred_element_type=jnp.float32)
    second = jnp.dot(attended_ref[...], weight_ref[1], preferred_element_type=jnp.float32)
    out_ref[...] = first[:rows] + second[rows:]


def add_kernel(own_ref, other_ref, residual_ref, out_ref):
    total = residual_ref[0].astype(jnp.float32) + (own_ref[...] + other_ref[...])
    out_ref[0] = total.astype(jnp.bfloat16)


def up_kernel(last, hidden_ref, *refs):
    half, _, depth = hidden_ref.shape
    if last:
        before_ref, weight_ref, _, out_ref, buffers, sems = refs
    else:
        weight_ref, own_ref, out_ref, buffers, sems = refs
        own_ref[...] = hidden_ref[0]
    position = lax.axis_index("batch")
    split = buffers.shape[0] // half
    step = depth // split
    pieces = []
    for j in range(half):
        index = reverse(j + half if last else j, 2 * half)
        start = jnp.bitwise_xor(position, index) * depth
        for k in range(split):
            pieces.append(weight_ref.at[pl.ds(pl.multiple_of(start + k * step, step), step), :])
    stream = Stream(pieces, buffers, sems)
    total = before_ref[...] if last else jnp.zeros(out_ref.shape, jnp.float32)
    for j in range(half):
        for k in range(split):
            block = hidden_ref[j][:, k * step : (k + 1) * step]
            total = total + jnp.dot(block, stream.take(j * split + k), preferred_element_type=jnp.float32)
    if last:
        total = (0.5 * total * (1.0 + lax.erf(total * math.sqrt(0.5)))).astype(jnp.bfloat16)
    out_ref[...] = total


def reorder(activation):
    rows = activation.shape[0]
    position = lax.axis_index("batch")
    to = lax.broadcasted_iota(jnp.int32, (rows, rows), 0)
    source = lax.broadcasted_iota(jnp.int32, (rows, rows), 1)
    order = jnp.where(source == jnp.bitwise_xor(reverse(to, rows), position), 1.0, 0.0).astype(jnp.bfloat16)
    return jnp.dot(order, activation, preferred_element_type=jnp.float32).astype(jnp.bfloat16)


def down_kernel(mine, act_ref, weight_ref, *rest):
    depth = act_ref.shape[1]
    side = lax.axis_index("tensor")
    start = pl.multiple_of((side if mine else 1 - side) * depth, depth)
    part = jnp.dot(
        reorder(act_ref[...]), weight_ref[pl.ds(start, depth), :], preferred_element_type=jnp.float32
    )
    if mine:
        rest[0][...] = part
        return
    before, keep_ref, send_ref = rest
    total = before[...] + part
    half = total.shape[0] // 2
    keep_ref[...] = total[:half]
    send_ref[...] = total[half:]


def ring(devices):
    if devices > BEAMS:
        return list(range(BEAMS))
    return list(range(0, BEAMS, 2)) + list(range(BEAMS - 1, 0, -2))


def place_kernel(stride, order, gathered_ref, new_ref, parents_ref, lengths_ref, out_ref, row, sem):
    position = lax.axis_index("batch")
    request = lax.rem(position, stride)
    parent = parents_ref[0, position]
    place = jnp.int32(0)
    for k, beam in enumerate(order):
        place = jnp.where(parent == beam, k, place)
    place = jnp.where(lax.axis_index("tensor") == 1, BEAMS - 1 - place, place)
    copy = pltpu.make_async_copy(gathered_ref.at[place], row, sem)
    copy.start()
    slots = lax.broadcasted_iota(jnp.int32, row.shape[1:], 0)
    copy.wait()
    for kind in range(2):
        old = row[kind].astype(jnp.float32)
        new = new_ref[kind : kind + 1, :].astype(jnp.float32)
        out_ref[kind] = jnp.where(slots == lengths_ref[request], new, old).astype(jnp.bfloat16)


def place(stride, order, gathered, new_kv, parents, lengths):
    return pl.pallas_call(
        functools.partial(place_kernel, stride, order),
        out_shape=jax.ShapeDtypeStruct(gathered.shape[1:], gathered.dtype),
        in_specs=[ANY, VM, SM, SM],
        out_specs=VM,
        scratch_shapes=[pltpu.VMEM(gathered.shape[1:], gathered.dtype), pltpu.SemaphoreType.DMA],
        compiler_params=pltpu.CompilerParams(vmem_limit_bytes=8 * MIB),
    )(in_hbm(gathered), new_kv, parents, lengths)


def body(
    init_cache,
    memory,
    queries,
    new_kv,
    residual,
    out_weight,
    up_weight,
    down_weight,
    parents,
    lengths,
):
    devices = lax.axis_size("batch")
    stride = devices // BEAMS
    position = lax.axis_index("batch")
    request = position % stride
    width = queries.shape[-1]
    rows = parents.shape[1]
    columns = out_weight.shape[2]
    hidden_units = up_weight.shape[1]
    out_columns = down_weight.shape[1]
    f32, bf16 = jnp.float32, jnp.bfloat16
    shape = jax.ShapeDtypeStruct
    up_weight = in_hbm(up_weight)
    down_weight = pltpu.with_memory_space_constraint(down_weight, pltpu.VMEM)
    sources = (queries[0, 0], init_cache[0], memory[0], new_kv[0, 0], residual)
    bit = devices // 2
    other = xor_permute(queries[0, 0], "batch", bit)
    loaded = fetch([in_hbm(x) for x in sources], queries[0, 0])
    other, (query, cache_row, memory_row, new_row, residual_row) = pin(other, loaded)
    query, far = doubling(jnp.concatenate([query, other]), stride, bit)
    state_shapes = (
        shape((2 * BEAMS, width), f32),
        shape((2 * BEAMS, 2 * LANES), f32),
        shape((2 * BEAMS, width + LANES), bf16),
    )
    num, state, pay = call(
        functools.partial(attend_kernel, stride),
        state_shapes,
        query,
        far,
        cache_row,
        memory_row,
        new_row,
        parents,
        lengths,
        specs=[VM] * 5 + [SM] * 2,
    )
    bit = stride
    while True:
        arrived = xor_permute(pay, "batch", bit)
        if bit == stride:
            arrived, (out_row,) = pin(arrived, fetch([in_hbm(out_weight)], pay))
        bit *= 2
        if bit == devices:
            break
        num, state, pay = call(merge_kernel, state_shapes, num, state, arrived)
    attended = finish(num, state, arrived)
    if stride > 1:
        stacked = jnp.concatenate(doubling(attended[None], 1, stride))
        wanted = reverse(jnp.bitwise_xor(jnp.arange(stride, dtype=jnp.int32), request), stride)
        stacked = stacked[wanted].reshape(stride, 2, BEAMS, width)
        attended = stacked.transpose(1, 2, 0, 3).reshape(2 * rows, width)

    partial = call(project_kernel, shape((rows, columns), f32), attended, out_row)
    other = xor_permute(partial, "tensor", 1)
    mine = call(add_kernel, pltpu.VMEM((1, rows, columns), bf16), partial, other, residual_row)
    near, far = doubling(mine, 1, devices)
    split = SPLIT if columns % (SPLIT * LANES) == 0 else 1
    count, piece = devices // 2 * split, (columns // split, hidden_units)
    hidden, first_half = stream_call(
        functools.partial(up_kernel, False),
        (shape((rows, columns), bf16), shape((rows, hidden_units), f32)),
        near,
        weight=up_weight,
        count=count,
        piece=piece,
    )
    far, first_half = pin(far, first_half)
    activation = stream_call(
        functools.partial(up_kernel, True),
        shape((rows, hidden_units), bf16),
        far,
        first_half,
        weight=up_weight,
        count=count,
        piece=piece,
        extra=(down_weight,),
    )
    arrived = xor_permute(activation, "tensor", 1)
    before = call(
        functools.partial(down_kernel, True), shape((rows, out_columns), f32), activation, down_weight
    )
    keep, send = call(
        functools.partial(down_kernel, False),
        (shape((rows // 2, out_columns), f32),) * 2,
        arrived,
        down_weight,
        before,
    )
    order = ring(devices)
    groups = []
    for r in range(stride):
        groups.append([(beam * stride + r) * 2 for beam in order])
        groups.append([(beam * stride + r) * 2 + 1 for beam in reversed(order)])
    gathered = lax.all_gather(init_cache[0], ("batch", "tensor"), axis_index_groups=groups)
    bit = 1
    while True:
        arrived = xor_permute(send, "batch", bit)
        bit *= 2
        if bit == devices:
            break
        total = keep + arrived
        half = total.shape[0] // 2
        keep, send = total[:half], total[half:]
    cache = place(stride, order, gathered, new_row, parents, lengths)
    arrived, cache = pin(arrived, cache)
    ffn_row = (keep + arrived).astype(bf16)
    return (hidden[None], ffn_row[None], cache[None])


def solution(mesh):
    placed = (
        P(("grp", "batch"), None, None, "tensor"),
        P(("grp", "batch"), None, None, "tensor"),
        P(None, ("grp", "batch"), None, "tensor"),
        P(None, ("grp", "batch"), None, "tensor"),
        P(None, "grp", "batch"),
        P(None, "tensor", "batch"),
        P(None, ("batch", "tensor")),
        P("batch", "tensor"),
        P(None, "grp"),
        P("grp"),
    )
    return jax.shard_map(
        body,
        mesh=mesh,
        in_specs=placed,
        out_specs=(
            P(None, "grp", "batch"),
            P(None, ("grp", "batch"), "tensor"),
            P(("grp", "batch"), None, None, "tensor"),
        ),
        check_vma=False,
    )
```

```python
import functools
import math

import jax
import jax.numpy as jnp
from jax import lax
from jax.experimental import pallas as pl
from jax.experimental.pallas import tpu as pltpu
from jax.sharding import PartitionSpec as P

HD = 128
LANES = 128
SLOT = 16
BEAMS = 8
LOW = -1e30
MIB = 1024 * 1024
STEP_FLOPS = 1_000_000_000

VM = pl.BlockSpec(memory_space=pltpu.VMEM)
SM = pl.BlockSpec(memory_space=pltpu.SMEM)
ANY = pl.BlockSpec(memory_space=pl.ANY)


def xor_permute(value, axis, bit):
    total = lax.axis_size(axis)
    return lax.ppermute(value, axis, [(i, i ^ bit) for i in range(total)])


def cross_permute(value, bit):
    pairs = [(2 * i + t, 2 * (i ^ bit) + 1 - t) for i in range(lax.axis_size("batch")) for t in range(2)]
    return lax.ppermute(value, ("batch", "tensor"), pairs)


def reverse(index, size):
    bits = size.bit_length() - 1
    return sum(((index >> k) & 1) << (bits - 1 - k) for k in range(bits))


def doubling(buffer, first, last, cross=False):
    bit = last
    while True:
        bit //= 2
        other = cross_permute(buffer, bit) if cross else xor_permute(buffer, "batch", bit)
        if bit == first:
            return buffer, other
        buffer = jnp.concatenate([buffer, other])


def drop(kernel, first, count, *refs):
    kernel(*refs[:first], *refs[first + count :])


def call(kernel, out, *args, specs=None, hold=(), vmem=8, flops=STEP_FLOPS, moved=0):
    first = len(args)
    return pl.pallas_call(
        functools.partial(drop, kernel, first, len(hold)),
        out_shape=out,
        in_specs=(specs or [VM] * first) + [ANY] * len(hold),
        out_specs=jax.tree.map(lambda _: VM, out),
        compiler_params=pltpu.CompilerParams(vmem_limit_bytes=vmem * MIB),
        cost_estimate=pl.CostEstimate(flops=flops, bytes_accessed=moved, transcendentals=0),
    )(*args, *hold)


def in_hbm(value):
    return pltpu.with_memory_space_constraint(value, pltpu.HBM)


def pin(value, loaded):
    return lax.optimization_barrier((value, loaded))


def start_all(copies):
    for copy in copies:
        copy.start()
    for copy in copies:
        copy.wait()


def fetch_kernel(count, *refs):
    sems = refs[-1]
    outs = refs[-1 - count : -1]
    copies = []
    for i in range(count):
        parts = refs[i].shape[0] if len(refs[i].shape) > 2 else 1
        for k in range(parts):
            source, target = (refs[i].at[k], outs[i].at[k]) if parts > 1 else (refs[i], outs[i])
            copies.append(pltpu.make_async_copy(source, target, sems.at[i, k]))
    start_all(copies)


def fetch(arrays, after):
    count = len(arrays)
    return pl.pallas_call(
        functools.partial(fetch_kernel, count),
        out_shape=[pltpu.VMEM(x.shape, x.dtype) for x in arrays],
        in_specs=[ANY] * (count + 1),
        out_specs=[VM] * count,
        scratch_shapes=[pltpu.SemaphoreType.DMA((count, 2))],
        compiler_params=pltpu.CompilerParams(vmem_limit_bytes=2 * MIB),
        cost_estimate=pl.CostEstimate(flops=0, bytes_accessed=2 * MIB, transcendentals=0),
    )(*arrays, after)


def split3(value):
    high = value.astype(jnp.bfloat16).astype(jnp.float32)
    rest = value - high
    middle = rest.astype(jnp.bfloat16).astype(jnp.float32)
    return high, middle, rest - middle


def export(num_ref, state_ref, pay_ref, peaks, totals):
    heads = num_ref.shape[1] // HD
    inverse = jnp.where(totals > 0.0, 1.0 / jnp.where(totals > 0.0, totals, 1.0), 0.0)
    for h in range(heads):
        cols = slice(h * HD, (h + 1) * HD)
        pay_ref[:, cols] = (num_ref[:, cols] * inverse[:, h : h + 1]).astype(jnp.bfloat16)
    state_ref[:, :LANES] = peaks
    state_ref[:, LANES:] = totals
    group = lax.broadcasted_iota(jnp.int32, peaks.shape, 1) // SLOT
    extra = jnp.zeros_like(peaks)
    for g, part in enumerate(split3(peaks) + split3(totals)):
        extra = jnp.where(group == g, pltpu.roll(part, g * SLOT, 1) if g else part, extra)
    pay_ref[:, heads * HD :] = extra.astype(jnp.bfloat16)


def attend_kernel(
    stride, near_ref, far_ref, cache_ref, memory_ref, new_ref, parents_ref, lengths_ref, num_ref, state_ref, pay_ref
):
    position = lax.axis_index("batch")
    own, request = position // stride, lax.rem(position, stride)
    length = lengths_ref[request]
    rows, width = num_ref.shape
    heads = width // HD
    past = cache_ref.shape[1]
    span = past + memory_ref.shape[1]
    f32, bf16 = jnp.float32, jnp.bfloat16

    to = lax.broadcasted_iota(jnp.int32, (rows, BEAMS), 0)
    source = lax.broadcasted_iota(jnp.int32, (rows, BEAMS), 1)

    def place_rows(piece_ref, first):
        beam = jnp.bitwise_xor(reverse(first + source // 2, BEAMS), own)
        order = jnp.where(to == (source % 2) * BEAMS + beam, 1.0, 0.0).astype(bf16)
        return jnp.dot(order, piece_ref[...], preferred_element_type=f32)

    query = (place_rows(near_ref, 0) + place_rows(far_ref, BEAMS // 2)).astype(bf16)

    row = lax.broadcasted_iota(jnp.int32, (rows, span), 0)
    slot = lax.broadcasted_iota(jnp.int32, (rows, span), 1)
    parent = jnp.zeros_like(row)
    for b in range(BEAMS):
        parent = jnp.where(row == b, parents_ref[0, b * stride + request], parent)
    in_past = ((slot < length) & (parent == own)) | ((slot == length) & (row == own))
    valid = jnp.where(row < BEAMS, jnp.where(in_past, 1, 0), jnp.where(slot >= past, 1, 0)) == 1
    fresh = lax.broadcasted_iota(jnp.int32, (past, HD), 0) == length
    lane = lax.broadcasted_iota(jnp.int32, (rows, LANES), 1)
    all_cols = [slice(h * HD, (h + 1) * HD) for h in range(heads)]

    def block(kind, cols):
        old = cache_ref[kind, :, cols].astype(f32)
        new = new_ref[kind : kind + 1, cols].astype(f32)
        merged = jnp.where(fresh, new, old).astype(bf16)
        return jnp.concatenate([merged, memory_ref[kind, :, cols]])

    scores = [
        lax.dot_general(
            query[:, cols], block(0, cols), (((1,), (1,)), ((), ())), preferred_element_type=f32
        )
        for cols in all_cols
    ]
    values = [block(1, cols) for cols in all_cols]
    scores = [jnp.where(valid, s * (1.0 / math.sqrt(HD)), LOW) for s in scores]
    tops = [jnp.max(s, axis=1, keepdims=True) for s in scores]
    weights = [jnp.where(valid, jnp.exp(s - t), 0.0) for s, t in zip(scores, tops)]
    sums = [jnp.sum(w, axis=1, keepdims=True) for w in weights]
    highs = [w.astype(bf16) for w in weights]
    lows = [(w - high.astype(f32)).astype(bf16) for w, high in zip(weights, highs)]
    both = [
        jnp.dot(jnp.concatenate([high, low]), v, preferred_element_type=f32)
        for high, low, v in zip(highs, lows, values)
    ]
    peaks = jnp.zeros((rows, LANES), f32)
    totals = jnp.zeros((rows, LANES), f32)
    for h, cols in enumerate(all_cols):
        num_ref[:, cols] = both[h][:rows] + both[h][rows:]
        peaks = jnp.where(lane == h, tops[h], peaks)
        totals = jnp.where(lane == h, sums[h], totals)
    export(num_ref, state_ref, pay_ref, peaks, totals)


def combine(num_ref, state_ref, pay_ref, out_ref):
    heads = num_ref.shape[1] // HD
    extra = pay_ref[:, heads * HD :].astype(jnp.float32)
    summed = extra + pltpu.roll(extra, LANES - SLOT, 1) + pltpu.roll(extra, LANES - 2 * SLOT, 1)
    other_total = pltpu.roll(summed, LANES - 3 * SLOT, 1)
    lane = lax.broadcasted_iota(jnp.int32, extra.shape, 1)
    used = lane < SLOT
    other_peak = jnp.where(used, summed, 0.0)
    other_total = jnp.where(used, other_total, 0.0)
    own_peak, own_total = state_ref[:, :LANES], state_ref[:, LANES:]
    peaks = jnp.maximum(own_peak, other_peak)
    own_factor = jnp.exp(own_peak - peaks)
    other_factor = jnp.exp(other_peak - peaks) * other_total
    totals = own_total * own_factor + other_factor
    for h in range(heads):
        cols = slice(h * HD, (h + 1) * HD)
        other = pay_ref[:, cols].astype(jnp.float32)
        out_ref[:, cols] = num_ref[:, cols] * own_factor[:, h : h + 1] + other * other_factor[:, h : h + 1]
    return peaks, totals


def merge_kernel(num_ref, state_ref, pay_ref, num_out, state_out, pay_out):
    peaks, totals = combine(num_ref, state_ref, pay_ref, num_out)
    export(num_out, state_out, pay_out, peaks, totals)


def finish_kernel(num_ref, state_ref, pay_ref, out_ref, num):
    _, totals = combine(num_ref, state_ref, pay_ref, num)
    for h in range(num.shape[1] // HD):
        cols = slice(h * HD, (h + 1) * HD)
        out_ref[:, cols] = (num[:, cols] / totals[:, h : h + 1]).astype(jnp.bfloat16)


def finish(num, state, pay):
    return pl.pallas_call(
        finish_kernel,
        out_shape=jax.ShapeDtypeStruct(num.shape, jnp.bfloat16),
        in_specs=[VM] * 3,
        out_specs=VM,
        scratch_shapes=[pltpu.VMEM(num.shape, jnp.float32)],
        compiler_params=pltpu.CompilerParams(vmem_limit_bytes=8 * MIB),
        cost_estimate=pl.CostEstimate(flops=STEP_FLOPS, bytes_accessed=0, transcendentals=0),
    )(num, state, pay)


def project_kernel(attended_ref, weight_ref, out_ref):
    rows = out_ref.shape[0]
    first = jnp.dot(attended_ref[...], weight_ref[0], preferred_element_type=jnp.float32)
    second = jnp.dot(attended_ref[...], weight_ref[1], preferred_element_type=jnp.float32)
    out_ref[...] = first[:rows] + second[rows:]


def add_kernel(own_ref, other_ref, residual_ref, out_ref):
    total = residual_ref[0].astype(jnp.float32) + (own_ref[...] + other_ref[...])
    out_ref[0] = total.astype(jnp.bfloat16)


def up_kernel(near_ref, far_ref, weight_ref, hidden_ref, out_ref):
    half, _, depth = near_ref.shape
    position = lax.axis_index("batch")
    hidden_ref[...] = near_ref[0]
    total = jnp.zeros(out_ref.shape, jnp.float32)
    for j in range(2 * half):
        block = near_ref[j] if j < half else far_ref[j - half]
        start = pl.multiple_of(jnp.bitwise_xor(position, reverse(j, 2 * half)) * depth, depth)
        total = total + jnp.dot(block, weight_ref[pl.ds(start, depth), :], preferred_element_type=jnp.float32)
    out_ref[...] = (0.5 * total * (1.0 + lax.erf(total * math.sqrt(0.5)))).astype(jnp.bfloat16)


def reorder(activation):
    rows = activation.shape[0]
    position = lax.axis_index("batch")
    to = lax.broadcasted_iota(jnp.int32, (rows, rows), 0)
    source = lax.broadcasted_iota(jnp.int32, (rows, rows), 1)
    order = jnp.where(source == jnp.bitwise_xor(reverse(to, rows), position), 1.0, 0.0).astype(jnp.bfloat16)
    return jnp.dot(order, activation, preferred_element_type=jnp.float32).astype(jnp.bfloat16)


def down_kernel(mine, act_ref, weight_ref, *rest):
    depth = act_ref.shape[1]
    side = lax.axis_index("tensor")
    start = pl.multiple_of((side if mine else 1 - side) * depth, depth)
    part = jnp.dot(
        reorder(act_ref[...]), weight_ref[pl.ds(start, depth), :], preferred_element_type=jnp.float32
    )
    if mine:
        rest[0][...] = part
        return
    before, keep_ref, send_ref = rest
    total = before[...] + part
    half = total.shape[0] // 2
    keep_ref[...] = total[:half]
    send_ref[...] = total[half:]


def ring(devices):
    if devices > BEAMS:
        return list(range(BEAMS))
    return list(range(0, BEAMS, 2)) + list(range(BEAMS - 1, 0, -2))


def place_kernel(stride, order, gathered_ref, new_ref, parents_ref, lengths_ref, out_ref, row, sem):
    position = lax.axis_index("batch")
    request = lax.rem(position, stride)
    parent = parents_ref[0, position]
    place = jnp.int32(0)
    for k, beam in enumerate(order):
        place = jnp.where(parent == beam, k, place)
    place = jnp.where(lax.axis_index("tensor") == 1, BEAMS - 1 - place, place)
    copy = pltpu.make_async_copy(gathered_ref.at[place], row, sem)
    copy.start()
    slots = lax.broadcasted_iota(jnp.int32, row.shape[1:], 0)
    copy.wait()
    for kind in range(2):
        old = row[kind].astype(jnp.float32)
        new = new_ref[kind : kind + 1, :].astype(jnp.float32)
        out_ref[kind] = jnp.where(slots == lengths_ref[request], new, old).astype(jnp.bfloat16)


def place(stride, order, gathered, new_kv, parents, lengths):
    return pl.pallas_call(
        functools.partial(place_kernel, stride, order),
        out_shape=jax.ShapeDtypeStruct(gathered.shape[1:], gathered.dtype),
        in_specs=[ANY, VM, SM, SM],
        out_specs=VM,
        scratch_shapes=[pltpu.VMEM(gathered.shape[1:], gathered.dtype), pltpu.SemaphoreType.DMA],
        compiler_params=pltpu.CompilerParams(vmem_limit_bytes=8 * MIB),
    )(in_hbm(gathered), new_kv, parents, lengths)


def body(
    init_cache,
    memory,
    queries,
    new_kv,
    residual,
    out_weight,
    up_weight,
    down_weight,
    parents,
    lengths,
):
    devices = lax.axis_size("batch")
    stride = devices // BEAMS
    position = lax.axis_index("batch")
    request = position % stride
    width = queries.shape[-1]
    rows = parents.shape[1]
    columns = out_weight.shape[2]
    hidden_units = up_weight.shape[1]
    out_columns = down_weight.shape[1]
    f32, bf16 = jnp.float32, jnp.bfloat16
    shape = jax.ShapeDtypeStruct
    down_weight = pltpu.with_memory_space_constraint(down_weight, pltpu.VMEM)
    up_weight = pltpu.with_memory_space_constraint(up_weight, pltpu.VMEM)
    sources = (queries[0, 0], init_cache[0], memory[0], new_kv[0, 0], residual)
    bit = devices // 2
    other = xor_permute(queries[0, 0], "batch", bit)
    loaded = fetch([in_hbm(x) for x in sources], queries[0, 0])
    other, (query, cache_row, memory_row, new_row, residual_row) = pin(other, loaded)
    query, far = doubling(jnp.concatenate([query, other]), stride, bit)
    far, (out_row,) = pin(far, fetch([in_hbm(out_weight)], query))
    state_shapes = (
        shape((2 * BEAMS, width), f32),
        shape((2 * BEAMS, 2 * LANES), f32),
        shape((2 * BEAMS, width + LANES), bf16),
    )
    num, state, pay = call(
        functools.partial(attend_kernel, stride),
        state_shapes,
        query,
        far,
        cache_row,
        memory_row,
        new_row,
        parents,
        lengths,
        specs=[VM] * 5 + [SM] * 2,
        hold=(),
    )
    bit = stride
    while True:
        arrived = xor_permute(pay, "batch", bit)
        bit *= 2
        if bit == devices:
            break
        num, state, pay = call(merge_kernel, state_shapes, num, state, arrived, hold=())
    attended = finish(num, state, arrived)
    if stride > 1:
        stacked = jnp.concatenate(doubling(attended[None], 1, stride))
        wanted = reverse(jnp.bitwise_xor(jnp.arange(stride, dtype=jnp.int32), request), stride)
        stacked = stacked[wanted].reshape(stride, 2, BEAMS, width)
        attended = stacked.transpose(1, 2, 0, 3).reshape(2 * rows, width)

    partial = call(project_kernel, shape((rows, columns), f32), attended, out_row, hold=())
    other = xor_permute(partial, "tensor", 1)
    mine = call(add_kernel, pltpu.VMEM((1, rows, columns), bf16), partial, other, residual_row, hold=())
    near, far = doubling(mine, 1, devices, cross=True)
    hidden, activation = call(
        up_kernel,
        (shape((rows, columns), bf16), shape((rows, hidden_units), bf16)),
        near,
        far,
        up_weight,
        hold=(),
    )
    arrived = xor_permute(activation, "tensor", 1)
    before = call(
        functools.partial(down_kernel, True), shape((rows, out_columns), f32), activation, down_weight, hold=()
    )
    keep, send = call(
        functools.partial(down_kernel, False),
        (shape((rows // 2, out_columns), f32),) * 2,
        arrived,
        down_weight,
        before,
    )
    order = ring(devices)
    groups = []
    for r in range(stride):
        groups.append([(beam * stride + r) * 2 for beam in order])
        groups.append([(beam * stride + r) * 2 + 1 for beam in reversed(order)])
    gathered = lax.all_gather(init_cache[0], ("batch", "tensor"), axis_index_groups=groups)
    bit = 1
    while True:
        arrived = xor_permute(send, "batch", bit)
        bit *= 2
        if bit == devices:
            break
        total = keep + arrived
        half = total.shape[0] // 2
        keep, send = total[:half], total[half:]
    cache = place(stride, order, gathered, new_row, parents, lengths)
    arrived, cache = pin(arrived, cache)
    ffn_row = (keep + arrived).astype(bf16)
    return (hidden[None], ffn_row[None], cache[None])


def solution(mesh):
    placed = (
        P(("grp", "batch"), None, None, "tensor"),
        P(("grp", "batch"), None, None, "tensor"),
        P(None, ("grp", "batch"), None, "tensor"),
        P(None, ("grp", "batch"), None, "tensor"),
        P(None, "grp", "batch"),
        P(None, "tensor", "batch"),
        P(None, ("batch", "tensor")),
        P("batch", "tensor"),
        P(None, "grp"),
        P("grp"),
    )
    return jax.shard_map(
        body,
        mesh=mesh,
        in_specs=placed,
        out_specs=(
            P(None, "grp", "batch"),
            P(None, ("grp", "batch"), "tensor"),
            P(("grp", "batch"), None, None, "tensor"),
        ),
        check_vma=False,
    )
```

```python
import functools
import math

import jax
import jax.numpy as jnp
from jax import lax
from jax.experimental import pallas as pl
from jax.experimental.pallas import tpu as pltpu
from jax.sharding import PartitionSpec as P

HD = 128
LANES = 128
SLOT = 16
BEAMS = 8
LOW = -1e30
MIB = 1024 * 1024
STEP_FLOPS = 1_000_000_000

VM = pl.BlockSpec(memory_space=pltpu.VMEM)
SM = pl.BlockSpec(memory_space=pltpu.SMEM)
ANY = pl.BlockSpec(memory_space=pl.ANY)


def xor_permute(value, axis, bit):
    total = lax.axis_size(axis)
    return lax.ppermute(value, axis, [(i, i ^ bit) for i in range(total)])


def cross_permute(value, bit):
    pairs = [(2 * i + t, 2 * (i ^ bit) + 1 - t) for i in range(lax.axis_size("batch")) for t in range(2)]
    return lax.ppermute(value, ("batch", "tensor"), pairs)


def reverse(index, size):
    bits = size.bit_length() - 1
    return sum(((index >> k) & 1) << (bits - 1 - k) for k in range(bits))


def doubling(buffer, first, last, cross=False):
    bit = last
    while True:
        bit //= 2
        other = cross_permute(buffer, bit) if cross else xor_permute(buffer, "batch", bit)
        if bit == first:
            return buffer, other
        buffer = jnp.concatenate([buffer, other])


def drop(kernel, first, count, *refs):
    kernel(*refs[:first], *refs[first + count :])


def call(kernel, out, *args, specs=None, hold=(), vmem=8, flops=STEP_FLOPS, moved=0):
    first = len(args)
    return pl.pallas_call(
        functools.partial(drop, kernel, first, len(hold)),
        out_shape=out,
        in_specs=(specs or [VM] * first) + [ANY] * len(hold),
        out_specs=jax.tree.map(lambda _: VM, out),
        compiler_params=pltpu.CompilerParams(vmem_limit_bytes=vmem * MIB),
        cost_estimate=pl.CostEstimate(flops=flops, bytes_accessed=moved, transcendentals=0),
    )(*args, *hold)


def in_hbm(value):
    return pltpu.with_memory_space_constraint(value, pltpu.HBM)


def pin(value, loaded):
    return lax.optimization_barrier((value, loaded))


def start_all(copies):
    for copy in copies:
        copy.start()
    for copy in copies:
        copy.wait()


def fetch_kernel(count, *refs):
    sems = refs[-1]
    outs = refs[-1 - count : -1]
    copies = []
    for i in range(count):
        parts = refs[i].shape[0] if len(refs[i].shape) > 2 else 1
        for k in range(parts):
            source, target = (refs[i].at[k], outs[i].at[k]) if parts > 1 else (refs[i], outs[i])
            copies.append(pltpu.make_async_copy(source, target, sems.at[i, k]))
    start_all(copies)


def fetch(arrays, after):
    count = len(arrays)
    return pl.pallas_call(
        functools.partial(fetch_kernel, count),
        out_shape=[pltpu.VMEM(x.shape, x.dtype) for x in arrays],
        in_specs=[ANY] * (count + 1),
        out_specs=[VM] * count,
        scratch_shapes=[pltpu.SemaphoreType.DMA((count, 2))],
        compiler_params=pltpu.CompilerParams(vmem_limit_bytes=2 * MIB),
        cost_estimate=pl.CostEstimate(flops=0, bytes_accessed=2 * MIB, transcendentals=0),
    )(*arrays, after)


def split3(value):
    high = value.astype(jnp.bfloat16).astype(jnp.float32)
    rest = value - high
    middle = rest.astype(jnp.bfloat16).astype(jnp.float32)
    return high, middle, rest - middle


def export(num_ref, state_ref, pay_ref, peaks, totals):
    heads = num_ref.shape[1] // HD
    inverse = jnp.where(totals > 0.0, 1.0 / jnp.where(totals > 0.0, totals, 1.0), 0.0)
    for h in range(heads):
        cols = slice(h * HD, (h + 1) * HD)
        pay_ref[:, cols] = (num_ref[:, cols] * inverse[:, h : h + 1]).astype(jnp.bfloat16)
    state_ref[:, :LANES] = peaks
    state_ref[:, LANES:] = totals
    group = lax.broadcasted_iota(jnp.int32, peaks.shape, 1) // SLOT
    extra = jnp.zeros_like(peaks)
    for g, part in enumerate(split3(peaks) + split3(totals)):
        extra = jnp.where(group == g, pltpu.roll(part, g * SLOT, 1) if g else part, extra)
    pay_ref[:, heads * HD :] = extra.astype(jnp.bfloat16)


def attend_kernel(
    stride, near_ref, far_ref, cache_ref, memory_ref, new_ref, parents_ref, lengths_ref, num_ref, state_ref, pay_ref
):
    position = lax.axis_index("batch")
    own, request = position // stride, lax.rem(position, stride)
    length = lengths_ref[request]
    rows, width = num_ref.shape
    heads = width // HD
    past = cache_ref.shape[1]
    span = past + memory_ref.shape[1]
    f32, bf16 = jnp.float32, jnp.bfloat16

    to = lax.broadcasted_iota(jnp.int32, (rows, BEAMS), 0)
    source = lax.broadcasted_iota(jnp.int32, (rows, BEAMS), 1)

    def place_rows(piece_ref, first):
        beam = jnp.bitwise_xor(reverse(first + source // 2, BEAMS), own)
        order = jnp.where(to == (source % 2) * BEAMS + beam, 1.0, 0.0).astype(bf16)
        return jnp.dot(order, piece_ref[...], preferred_element_type=f32)

    query = (place_rows(near_ref, 0) + place_rows(far_ref, BEAMS // 2)).astype(bf16)

    row = lax.broadcasted_iota(jnp.int32, (rows, span), 0)
    slot = lax.broadcasted_iota(jnp.int32, (rows, span), 1)
    parent = jnp.zeros_like(row)
    for b in range(BEAMS):
        parent = jnp.where(row == b, parents_ref[0, b * stride + request], parent)
    in_past = ((slot < length) & (parent == own)) | ((slot == length) & (row == own))
    valid = jnp.where(row < BEAMS, jnp.where(in_past, 1, 0), jnp.where(slot >= past, 1, 0)) == 1
    fresh = lax.broadcasted_iota(jnp.int32, (past, HD), 0) == length
    lane = lax.broadcasted_iota(jnp.int32, (rows, LANES), 1)
    all_cols = [slice(h * HD, (h + 1) * HD) for h in range(heads)]

    def block(kind, cols):
        old = cache_ref[kind, :, cols].astype(f32)
        new = new_ref[kind : kind + 1, cols].astype(f32)
        merged = jnp.where(fresh, new, old).astype(bf16)
        return jnp.concatenate([merged, memory_ref[kind, :, cols]])

    scores = [
        lax.dot_general(
            query[:, cols], block(0, cols), (((1,), (1,)), ((), ())), preferred_element_type=f32
        )
        for cols in all_cols
    ]
    values = [block(1, cols) for cols in all_cols]
    scores = [jnp.where(valid, s * (1.0 / math.sqrt(HD)), LOW) for s in scores]
    tops = [jnp.max(s, axis=1, keepdims=True) for s in scores]
    weights = [jnp.where(valid, jnp.exp(s - t), 0.0) for s, t in zip(scores, tops)]
    sums = [jnp.sum(w, axis=1, keepdims=True) for w in weights]
    highs = [w.astype(bf16) for w in weights]
    lows = [(w - high.astype(f32)).astype(bf16) for w, high in zip(weights, highs)]
    both = [
        jnp.dot(jnp.concatenate([high, low]), v, preferred_element_type=f32)
        for high, low, v in zip(highs, lows, values)
    ]
    peaks = jnp.zeros((rows, LANES), f32)
    totals = jnp.zeros((rows, LANES), f32)
    for h, cols in enumerate(all_cols):
        num_ref[:, cols] = both[h][:rows] + both[h][rows:]
        peaks = jnp.where(lane == h, tops[h], peaks)
        totals = jnp.where(lane == h, sums[h], totals)
    export(num_ref, state_ref, pay_ref, peaks, totals)


def combine(num_ref, state_ref, pay_ref, out_ref):
    heads = num_ref.shape[1] // HD
    extra = pay_ref[:, heads * HD :].astype(jnp.float32)
    summed = extra + pltpu.roll(extra, LANES - SLOT, 1) + pltpu.roll(extra, LANES - 2 * SLOT, 1)
    other_total = pltpu.roll(summed, LANES - 3 * SLOT, 1)
    lane = lax.broadcasted_iota(jnp.int32, extra.shape, 1)
    used = lane < SLOT
    other_peak = jnp.where(used, summed, 0.0)
    other_total = jnp.where(used, other_total, 0.0)
    own_peak, own_total = state_ref[:, :LANES], state_ref[:, LANES:]
    peaks = jnp.maximum(own_peak, other_peak)
    own_factor = jnp.exp(own_peak - peaks)
    other_factor = jnp.exp(other_peak - peaks) * other_total
    totals = own_total * own_factor + other_factor
    for h in range(heads):
        cols = slice(h * HD, (h + 1) * HD)
        other = pay_ref[:, cols].astype(jnp.float32)
        out_ref[:, cols] = num_ref[:, cols] * own_factor[:, h : h + 1] + other * other_factor[:, h : h + 1]
    return peaks, totals


def merge_kernel(num_ref, state_ref, pay_ref, num_out, state_out, pay_out):
    peaks, totals = combine(num_ref, state_ref, pay_ref, num_out)
    export(num_out, state_out, pay_out, peaks, totals)


def finish_kernel(num_ref, state_ref, pay_ref, out_ref, num):
    _, totals = combine(num_ref, state_ref, pay_ref, num)
    for h in range(num.shape[1] // HD):
        cols = slice(h * HD, (h + 1) * HD)
        out_ref[:, cols] = (num[:, cols] / totals[:, h : h + 1]).astype(jnp.bfloat16)


def finish(num, state, pay):
    return pl.pallas_call(
        finish_kernel,
        out_shape=jax.ShapeDtypeStruct(num.shape, jnp.bfloat16),
        in_specs=[VM] * 3,
        out_specs=VM,
        scratch_shapes=[pltpu.VMEM(num.shape, jnp.float32)],
        compiler_params=pltpu.CompilerParams(vmem_limit_bytes=8 * MIB),
        cost_estimate=pl.CostEstimate(flops=STEP_FLOPS, bytes_accessed=0, transcendentals=0),
    )(num, state, pay)


def project_kernel(attended_ref, weight_ref, out_ref):
    rows = out_ref.shape[0]
    first = jnp.dot(attended_ref[...], weight_ref[0], preferred_element_type=jnp.float32)
    second = jnp.dot(attended_ref[...], weight_ref[1], preferred_element_type=jnp.float32)
    out_ref[...] = first[:rows] + second[rows:]


def add_kernel(own_ref, other_ref, residual_ref, out_ref):
    total = residual_ref[0].astype(jnp.float32) + (own_ref[...] + other_ref[...])
    out_ref[0] = total.astype(jnp.bfloat16)


def up_kernel(near_ref, far_ref, weight_ref, hidden_ref, out_ref):
    half, _, depth = near_ref.shape
    position = lax.axis_index("batch")
    hidden_ref[...] = near_ref[0]
    total = jnp.zeros(out_ref.shape, jnp.float32)
    for j in range(2 * half):
        block = near_ref[j] if j < half else far_ref[j - half]
        start = pl.multiple_of(jnp.bitwise_xor(position, reverse(j, 2 * half)) * depth, depth)
        total = total + jnp.dot(block, weight_ref[pl.ds(start, depth), :], preferred_element_type=jnp.float32)
    out_ref[...] = (0.5 * total * (1.0 + lax.erf(total * math.sqrt(0.5)))).astype(jnp.bfloat16)


def reorder(activation):
    rows = activation.shape[0]
    position = lax.axis_index("batch")
    to = lax.broadcasted_iota(jnp.int32, (rows, rows), 0)
    source = lax.broadcasted_iota(jnp.int32, (rows, rows), 1)
    order = jnp.where(source == jnp.bitwise_xor(reverse(to, rows), position), 1.0, 0.0).astype(jnp.bfloat16)
    return jnp.dot(order, activation, preferred_element_type=jnp.float32).astype(jnp.bfloat16)


def down_kernel(mine, act_ref, weight_ref, *rest):
    depth = act_ref.shape[1]
    side = lax.axis_index("tensor")
    start = pl.multiple_of((side if mine else 1 - side) * depth, depth)
    part = jnp.dot(
        reorder(act_ref[...]), weight_ref[pl.ds(start, depth), :], preferred_element_type=jnp.float32
    )
    if mine:
        rest[0][...] = part
        return
    before, keep_ref, send_ref = rest
    total = before[...] + part
    half = total.shape[0] // 2
    keep_ref[...] = total[:half]
    send_ref[...] = total[half:]


def ring(devices):
    if devices > BEAMS:
        return list(range(BEAMS))
    return list(range(0, BEAMS, 2)) + list(range(BEAMS - 1, 0, -2))


def place_kernel(stride, order, keys_ref, values_ref, new_ref, parents_ref, lengths_ref, out_ref, row, sems):
    position = lax.axis_index("batch")
    request = lax.rem(position, stride)
    parent = parents_ref[0, position]
    forward = jnp.int32(0)
    for k, beam in enumerate(order):
        forward = jnp.where(parent == beam, k, forward)
    backward = BEAMS - 1 - forward
    first = lax.axis_index("tensor") == 0
    copies = [
        pltpu.make_async_copy(keys_ref.at[jnp.where(first, forward, backward)], row.at[0], sems.at[0]),
        pltpu.make_async_copy(values_ref.at[jnp.where(first, backward, forward)], row.at[1], sems.at[1]),
    ]
    start_all(copies)
    slots = lax.broadcasted_iota(jnp.int32, row.shape[1:], 0)
    for kind in range(2):
        old = row[kind].astype(jnp.float32)
        new = new_ref[kind : kind + 1, :].astype(jnp.float32)
        out_ref[kind] = jnp.where(slots == lengths_ref[request], new, old).astype(jnp.bfloat16)


def place(stride, order, keys, values, new_kv, parents, lengths):
    shape = (2, *keys.shape[1:])
    return pl.pallas_call(
        functools.partial(place_kernel, stride, order),
        out_shape=jax.ShapeDtypeStruct(shape, keys.dtype),
        in_specs=[ANY, ANY, VM, SM, SM],
        out_specs=VM,
        scratch_shapes=[pltpu.VMEM(shape, keys.dtype), pltpu.SemaphoreType.DMA((2,))],
        compiler_params=pltpu.CompilerParams(vmem_limit_bytes=8 * MIB),
    )(in_hbm(keys), in_hbm(values), new_kv, parents, lengths)


def body(
    init_cache,
    memory,
    queries,
    new_kv,
    residual,
    out_weight,
    up_weight,
    down_weight,
    parents,
    lengths,
):
    devices = lax.axis_size("batch")
    stride = devices // BEAMS
    position = lax.axis_index("batch")
    request = position % stride
    width = queries.shape[-1]
    rows = parents.shape[1]
    columns = out_weight.shape[2]
    hidden_units = up_weight.shape[1]
    out_columns = down_weight.shape[1]
    f32, bf16 = jnp.float32, jnp.bfloat16
    shape = jax.ShapeDtypeStruct
    down_weight = pltpu.with_memory_space_constraint(down_weight, pltpu.VMEM)
    up_weight = pltpu.with_memory_space_constraint(up_weight, pltpu.VMEM)
    sources = (queries[0, 0], init_cache[0], memory[0], new_kv[0, 0], residual)
    bit = devices // 2
    other = xor_permute(queries[0, 0], "batch", bit)
    loaded = fetch([in_hbm(x) for x in sources], queries[0, 0])
    other, (query, cache_row, memory_row, new_row, residual_row) = pin(other, loaded)
    query, far = doubling(jnp.concatenate([query, other]), stride, bit)
    far, (out_row,) = pin(far, fetch([in_hbm(out_weight)], query))
    state_shapes = (
        shape((2 * BEAMS, width), f32),
        shape((2 * BEAMS, 2 * LANES), f32),
        shape((2 * BEAMS, width + LANES), bf16),
    )
    num, state, pay = call(
        functools.partial(attend_kernel, stride),
        state_shapes,
        query,
        far,
        cache_row,
        memory_row,
        new_row,
        parents,
        lengths,
        specs=[VM] * 5 + [SM] * 2,
        hold=(),
    )
    bit = stride
    while True:
        arrived = xor_permute(pay, "batch", bit)
        bit *= 2
        if bit == devices:
            break
        num, state, pay = call(merge_kernel, state_shapes, num, state, arrived, hold=())
    attended = finish(num, state, arrived)
    if stride > 1:
        stacked = jnp.concatenate(doubling(attended[None], 1, stride))
        wanted = reverse(jnp.bitwise_xor(jnp.arange(stride, dtype=jnp.int32), request), stride)
        stacked = stacked[wanted].reshape(stride, 2, BEAMS, width)
        attended = stacked.transpose(1, 2, 0, 3).reshape(2 * rows, width)

    partial = call(project_kernel, shape((rows, columns), f32), attended, out_row, hold=())
    other = xor_permute(partial, "tensor", 1)
    mine = call(add_kernel, pltpu.VMEM((1, rows, columns), bf16), partial, other, residual_row, hold=())
    near, far = doubling(mine, 1, devices, cross=True)
    hidden, activation = call(
        up_kernel,
        (shape((rows, columns), bf16), shape((rows, hidden_units), bf16)),
        near,
        far,
        up_weight,
        hold=(),
    )
    arrived = xor_permute(activation, "tensor", 1)
    before = call(
        functools.partial(down_kernel, True), shape((rows, out_columns), f32), activation, down_weight, hold=()
    )
    keep, send = call(
        functools.partial(down_kernel, False),
        (shape((rows // 2, out_columns), f32),) * 2,
        arrived,
        down_weight,
        before,
    )
    order = ring(devices)
    groups = []
    for r in range(stride):
        groups.append([(beam * stride + r) * 2 for beam in order])
        groups.append([(beam * stride + r) * 2 + 1 for beam in reversed(order)])
    opposite = [group[::-1] for group in groups]
    keys = lax.all_gather(init_cache[0, 0], ("batch", "tensor"), axis_index_groups=groups)
    values = lax.all_gather(init_cache[0, 1], ("batch", "tensor"), axis_index_groups=opposite)
    bit = 1
    while True:
        arrived = xor_permute(send, "batch", bit)
        bit *= 2
        if bit == devices:
            break
        total = keep + arrived
        half = total.shape[0] // 2
        keep, send = total[:half], total[half:]
    cache = place(stride, order, keys, values, new_row, parents, lengths)
    arrived, cache = pin(arrived, cache)
    ffn_row = (keep + arrived).astype(bf16)
    return (hidden[None], ffn_row[None], cache[None])


def solution(mesh):
    placed = (
        P(("grp", "batch"), None, None, "tensor"),
        P(("grp", "batch"), None, None, "tensor"),
        P(None, ("grp", "batch"), None, "tensor"),
        P(None, ("grp", "batch"), None, "tensor"),
        P(None, "grp", "batch"),
        P(None, "tensor", "batch"),
        P(None, ("batch", "tensor")),
        P("batch", "tensor"),
        P(None, "grp"),
        P("grp"),
    )
    return jax.shard_map(
        body,
        mesh=mesh,
        in_specs=placed,
        out_specs=(
            P(None, "grp", "batch"),
            P(None, ("grp", "batch"), "tensor"),
            P(("grp", "batch"), None, None, "tensor"),
        ),
        check_vma=False,
    )
```

```python
import functools
import math

import jax
import jax.numpy as jnp
from jax import lax
from jax.experimental import pallas as pl
from jax.experimental.pallas import tpu as pltpu
from jax.sharding import PartitionSpec as P

HD = 128
LANES = 128
SLOT = 16
BEAMS = 8
LOW = -1e30
MIB = 1024 * 1024
STEP_FLOPS = 1_000_000_000

VM = pl.BlockSpec(memory_space=pltpu.VMEM)
SM = pl.BlockSpec(memory_space=pltpu.SMEM)
ANY = pl.BlockSpec(memory_space=pl.ANY)


def xor_permute(value, axis, bit):
    total = lax.axis_size(axis)
    return lax.ppermute(value, axis, [(i, i ^ bit) for i in range(total)])


def cross_permute(value, bit):
    pairs = [(2 * i + t, 2 * (i ^ bit) + 1 - t) for i in range(lax.axis_size("batch")) for t in range(2)]
    return lax.ppermute(value, ("batch", "tensor"), pairs)


def reverse(index, size):
    bits = size.bit_length() - 1
    return sum(((index >> k) & 1) << (bits - 1 - k) for k in range(bits))


def doubling(buffer, first, last, cross=False):
    bit = last
    while True:
        bit //= 2
        other = cross_permute(buffer, bit) if cross else xor_permute(buffer, "batch", bit)
        if bit == first:
            return buffer, other
        buffer = jnp.concatenate([buffer, other])


def drop(kernel, first, count, *refs):
    kernel(*refs[:first], *refs[first + count :])


def call(kernel, out, *args, specs=None, hold=(), vmem=8, flops=STEP_FLOPS, moved=0):
    first = len(args)
    return pl.pallas_call(
        functools.partial(drop, kernel, first, len(hold)),
        out_shape=out,
        in_specs=(specs or [VM] * first) + [ANY] * len(hold),
        out_specs=jax.tree.map(lambda _: VM, out),
        compiler_params=pltpu.CompilerParams(vmem_limit_bytes=vmem * MIB),
        cost_estimate=pl.CostEstimate(flops=flops, bytes_accessed=moved, transcendentals=0),
    )(*args, *hold)


def in_hbm(value):
    return pltpu.with_memory_space_constraint(value, pltpu.HBM)


def pin(value, loaded):
    return lax.optimization_barrier((value, loaded))


def start_all(copies):
    for copy in copies:
        copy.start()
    for copy in copies:
        copy.wait()


def fetch_kernel(count, *refs):
    sems = refs[-1]
    outs = refs[-1 - count : -1]
    copies = []
    for i in range(count):
        parts = refs[i].shape[0] if len(refs[i].shape) > 2 else 1
        for k in range(parts):
            source, target = (refs[i].at[k], outs[i].at[k]) if parts > 1 else (refs[i], outs[i])
            copies.append(pltpu.make_async_copy(source, target, sems.at[i, k]))
    start_all(copies)


def fetch(arrays, after):
    count = len(arrays)
    return pl.pallas_call(
        functools.partial(fetch_kernel, count),
        out_shape=[pltpu.VMEM(x.shape, x.dtype) for x in arrays],
        in_specs=[ANY] * (count + 1),
        out_specs=[VM] * count,
        scratch_shapes=[pltpu.SemaphoreType.DMA((count, 2))],
        compiler_params=pltpu.CompilerParams(vmem_limit_bytes=2 * MIB),
        cost_estimate=pl.CostEstimate(flops=0, bytes_accessed=2 * MIB, transcendentals=0),
    )(*arrays, after)


def split3(value):
    high = value.astype(jnp.bfloat16).astype(jnp.float32)
    rest = value - high
    middle = rest.astype(jnp.bfloat16).astype(jnp.float32)
    return high, middle, rest - middle


def export(num_ref, state_ref, pay_ref, peaks, totals):
    heads = num_ref.shape[1] // HD
    inverse = jnp.where(totals > 0.0, 1.0 / jnp.where(totals > 0.0, totals, 1.0), 0.0)
    for h in range(heads):
        cols = slice(h * HD, (h + 1) * HD)
        pay_ref[:, cols] = (num_ref[:, cols] * inverse[:, h : h + 1]).astype(jnp.bfloat16)
    state_ref[:, :LANES] = peaks
    state_ref[:, LANES:] = totals
    group = lax.broadcasted_iota(jnp.int32, peaks.shape, 1) // SLOT
    extra = jnp.zeros_like(peaks)
    for g, part in enumerate(split3(peaks) + split3(totals)):
        extra = jnp.where(group == g, pltpu.roll(part, g * SLOT, 1) if g else part, extra)
    pay_ref[:, heads * HD :] = extra.astype(jnp.bfloat16)


def attend_kernel(
    stride, near_ref, far_ref, cache_ref, memory_ref, new_ref, parents_ref, lengths_ref, num_ref, state_ref, pay_ref
):
    position = lax.axis_index("batch")
    own, request = position // stride, lax.rem(position, stride)
    length = lengths_ref[request]
    rows, width = num_ref.shape
    heads = width // HD
    past = cache_ref.shape[1]
    span = past + memory_ref.shape[1]
    f32, bf16 = jnp.float32, jnp.bfloat16

    to = lax.broadcasted_iota(jnp.int32, (rows, BEAMS), 0)
    source = lax.broadcasted_iota(jnp.int32, (rows, BEAMS), 1)

    def place_rows(piece_ref, first):
        beam = jnp.bitwise_xor(reverse(first + source // 2, BEAMS), own)
        order = jnp.where(to == (source % 2) * BEAMS + beam, 1.0, 0.0).astype(bf16)
        return jnp.dot(order, piece_ref[...], preferred_element_type=f32)

    query = (place_rows(near_ref, 0) + place_rows(far_ref, BEAMS // 2)).astype(bf16)

    row = lax.broadcasted_iota(jnp.int32, (rows, span), 0)
    slot = lax.broadcasted_iota(jnp.int32, (rows, span), 1)
    parent = jnp.zeros_like(row)
    for b in range(BEAMS):
        parent = jnp.where(row == b, parents_ref[0, b * stride + request], parent)
    in_past = ((slot < length) & (parent == own)) | ((slot == length) & (row == own))
    valid = jnp.where(row < BEAMS, jnp.where(in_past, 1, 0), jnp.where(slot >= past, 1, 0)) == 1
    fresh = lax.broadcasted_iota(jnp.int32, (past, HD), 0) == length
    lane = lax.broadcasted_iota(jnp.int32, (rows, LANES), 1)
    all_cols = [slice(h * HD, (h + 1) * HD) for h in range(heads)]

    def block(kind, cols):
        old = cache_ref[kind, :, cols].astype(f32)
        new = new_ref[kind : kind + 1, cols].astype(f32)
        merged = jnp.where(fresh, new, old).astype(bf16)
        return jnp.concatenate([merged, memory_ref[kind, :, cols]])

    scores = [
        lax.dot_general(
            query[:, cols], block(0, cols), (((1,), (1,)), ((), ())), preferred_element_type=f32
        )
        for cols in all_cols
    ]
    values = [block(1, cols) for cols in all_cols]
    scores = [jnp.where(valid, s * (1.0 / math.sqrt(HD)), LOW) for s in scores]
    tops = [jnp.max(s, axis=1, keepdims=True) for s in scores]
    weights = [jnp.where(valid, jnp.exp(s - t), 0.0) for s, t in zip(scores, tops)]
    sums = [jnp.sum(w, axis=1, keepdims=True) for w in weights]
    highs = [w.astype(bf16) for w in weights]
    lows = [(w - high.astype(f32)).astype(bf16) for w, high in zip(weights, highs)]
    both = [
        jnp.dot(jnp.concatenate([high, low]), v, preferred_element_type=f32)
        for high, low, v in zip(highs, lows, values)
    ]
    peaks = jnp.zeros((rows, LANES), f32)
    totals = jnp.zeros((rows, LANES), f32)
    for h, cols in enumerate(all_cols):
        num_ref[:, cols] = both[h][:rows] + both[h][rows:]
        peaks = jnp.where(lane == h, tops[h], peaks)
        totals = jnp.where(lane == h, sums[h], totals)
    export(num_ref, state_ref, pay_ref, peaks, totals)


def combine(num_ref, state_ref, pay_ref, out_ref):
    heads = num_ref.shape[1] // HD
    extra = pay_ref[:, heads * HD :].astype(jnp.float32)
    summed = extra + pltpu.roll(extra, LANES - SLOT, 1) + pltpu.roll(extra, LANES - 2 * SLOT, 1)
    other_total = pltpu.roll(summed, LANES - 3 * SLOT, 1)
    lane = lax.broadcasted_iota(jnp.int32, extra.shape, 1)
    used = lane < SLOT
    other_peak = jnp.where(used, summed, 0.0)
    other_total = jnp.where(used, other_total, 0.0)
    own_peak, own_total = state_ref[:, :LANES], state_ref[:, LANES:]
    peaks = jnp.maximum(own_peak, other_peak)
    own_factor = jnp.exp(own_peak - peaks)
    other_factor = jnp.exp(other_peak - peaks) * other_total
    totals = own_total * own_factor + other_factor
    for h in range(heads):
        cols = slice(h * HD, (h + 1) * HD)
        other = pay_ref[:, cols].astype(jnp.float32)
        out_ref[:, cols] = num_ref[:, cols] * own_factor[:, h : h + 1] + other * other_factor[:, h : h + 1]
    return peaks, totals


def merge_kernel(num_ref, state_ref, pay_ref, num_out, state_out, pay_out):
    peaks, totals = combine(num_ref, state_ref, pay_ref, num_out)
    export(num_out, state_out, pay_out, peaks, totals)


def finish_kernel(num_ref, state_ref, pay_ref, out_ref, num):
    _, totals = combine(num_ref, state_ref, pay_ref, num)
    for h in range(num.shape[1] // HD):
        cols = slice(h * HD, (h + 1) * HD)
        out_ref[:, cols] = (num[:, cols] / totals[:, h : h + 1]).astype(jnp.bfloat16)


def finish(num, state, pay):
    return pl.pallas_call(
        finish_kernel,
        out_shape=jax.ShapeDtypeStruct(num.shape, jnp.bfloat16),
        in_specs=[VM] * 3,
        out_specs=VM,
        scratch_shapes=[pltpu.VMEM(num.shape, jnp.float32)],
        compiler_params=pltpu.CompilerParams(vmem_limit_bytes=8 * MIB),
        cost_estimate=pl.CostEstimate(flops=STEP_FLOPS, bytes_accessed=0, transcendentals=0),
    )(num, state, pay)


def project_kernel(attended_ref, weight_ref, out_ref):
    rows = out_ref.shape[0]
    first = jnp.dot(attended_ref[...], weight_ref[0], preferred_element_type=jnp.float32)
    second = jnp.dot(attended_ref[...], weight_ref[1], preferred_element_type=jnp.float32)
    out_ref[...] = first[:rows] + second[rows:]


def finish_project_kernel(num_ref, state_ref, pay_ref, weight_ref, out_ref, num, attended):
    finish_kernel(num_ref, state_ref, pay_ref, attended, num)
    project_kernel(attended, weight_ref, out_ref)


def finish_project(num, state, pay, weight):
    rows, columns = num.shape[0] // 2, weight.shape[2]
    return pl.pallas_call(
        finish_project_kernel,
        out_shape=jax.ShapeDtypeStruct((rows, columns), jnp.float32),
        in_specs=[VM] * 4,
        out_specs=VM,
        scratch_shapes=[pltpu.VMEM(num.shape, jnp.float32), pltpu.VMEM(num.shape, jnp.bfloat16)],
        compiler_params=pltpu.CompilerParams(vmem_limit_bytes=8 * MIB),
        cost_estimate=pl.CostEstimate(flops=2 * STEP_FLOPS, bytes_accessed=0, transcendentals=0),
    )(num, state, pay, weight)


def add_kernel(own_ref, other_ref, residual_ref, out_ref):
    total = residual_ref[0].astype(jnp.float32) + (own_ref[...] + other_ref[...])
    out_ref[0] = total.astype(jnp.bfloat16)


def up_kernel(near_ref, far_ref, weight_ref, hidden_ref, out_ref):
    half, _, depth = near_ref.shape
    position = lax.axis_index("batch")
    hidden_ref[...] = near_ref[0]
    total = jnp.zeros(out_ref.shape, jnp.float32)
    for j in range(2 * half):
        block = near_ref[j] if j < half else far_ref[j - half]
        start = pl.multiple_of(jnp.bitwise_xor(position, reverse(j, 2 * half)) * depth, depth)
        total = total + jnp.dot(block, weight_ref[pl.ds(start, depth), :], preferred_element_type=jnp.float32)
    out_ref[...] = (0.5 * total * (1.0 + lax.erf(total * math.sqrt(0.5)))).astype(jnp.bfloat16)


def reorder(activation):
    rows = activation.shape[0]
    position = lax.axis_index("batch")
    to = lax.broadcasted_iota(jnp.int32, (rows, rows), 0)
    source = lax.broadcasted_iota(jnp.int32, (rows, rows), 1)
    order = jnp.where(source == jnp.bitwise_xor(reverse(to, rows), position), 1.0, 0.0).astype(jnp.bfloat16)
    return jnp.dot(order, activation, preferred_element_type=jnp.float32).astype(jnp.bfloat16)


def down_kernel(mine, act_ref, weight_ref, *rest):
    depth = act_ref.shape[1]
    side = lax.axis_index("tensor")
    start = pl.multiple_of((side if mine else 1 - side) * depth, depth)
    part = jnp.dot(
        reorder(act_ref[...]), weight_ref[pl.ds(start, depth), :], preferred_element_type=jnp.float32
    )
    if mine:
        rest[0][...] = part
        return
    before, keep_ref, send_ref = rest
    total = before[...] + part
    half = total.shape[0] // 2
    keep_ref[...] = total[:half]
    send_ref[...] = total[half:]


def ring(devices):
    if devices > BEAMS:
        return list(range(BEAMS))
    return list(range(0, BEAMS, 2)) + list(range(BEAMS - 1, 0, -2))


def place_kernel(stride, order, gathered_ref, new_ref, parents_ref, lengths_ref, out_ref, row, sem):
    position = lax.axis_index("batch")
    request = lax.rem(position, stride)
    parent = parents_ref[0, position]
    place = jnp.int32(0)
    for k, beam in enumerate(order):
        place = jnp.where(parent == beam, k, place)
    place = jnp.where(lax.axis_index("tensor") == 1, BEAMS - 1 - place, place)
    copy = pltpu.make_async_copy(gathered_ref.at[place], row, sem)
    copy.start()
    slots = lax.broadcasted_iota(jnp.int32, row.shape[1:], 0)
    copy.wait()
    for kind in range(2):
        old = row[kind].astype(jnp.float32)
        new = new_ref[kind : kind + 1, :].astype(jnp.float32)
        out_ref[kind] = jnp.where(slots == lengths_ref[request], new, old).astype(jnp.bfloat16)


def place(stride, order, gathered, new_kv, parents, lengths):
    return pl.pallas_call(
        functools.partial(place_kernel, stride, order),
        out_shape=jax.ShapeDtypeStruct(gathered.shape[1:], gathered.dtype),
        in_specs=[ANY, VM, SM, SM],
        out_specs=VM,
        scratch_shapes=[pltpu.VMEM(gathered.shape[1:], gathered.dtype), pltpu.SemaphoreType.DMA],
        compiler_params=pltpu.CompilerParams(vmem_limit_bytes=8 * MIB),
    )(in_hbm(gathered), new_kv, parents, lengths)


def body(
    init_cache,
    memory,
    queries,
    new_kv,
    residual,
    out_weight,
    up_weight,
    down_weight,
    parents,
    lengths,
):
    devices = lax.axis_size("batch")
    stride = devices // BEAMS
    position = lax.axis_index("batch")
    request = position % stride
    width = queries.shape[-1]
    rows = parents.shape[1]
    columns = out_weight.shape[2]
    hidden_units = up_weight.shape[1]
    out_columns = down_weight.shape[1]
    f32, bf16 = jnp.float32, jnp.bfloat16
    shape = jax.ShapeDtypeStruct
    down_weight = pltpu.with_memory_space_constraint(down_weight, pltpu.VMEM)
    up_weight = pltpu.with_memory_space_constraint(up_weight, pltpu.VMEM)
    sources = (queries[0, 0], init_cache[0], memory[0], new_kv[0, 0], residual)
    bit = devices // 2
    other = xor_permute(queries[0, 0], "batch", bit)
    loaded = fetch([in_hbm(x) for x in sources], queries[0, 0])
    other, (query, cache_row, memory_row, new_row, residual_row) = pin(other, loaded)
    query, far = doubling(jnp.concatenate([query, other]), stride, bit)
    far, (out_row,) = pin(far, fetch([in_hbm(out_weight)], query))
    state_shapes = (
        shape((2 * BEAMS, width), f32),
        shape((2 * BEAMS, 2 * LANES), f32),
        shape((2 * BEAMS, width + LANES), bf16),
    )
    num, state, pay = call(
        functools.partial(attend_kernel, stride),
        state_shapes,
        query,
        far,
        cache_row,
        memory_row,
        new_row,
        parents,
        lengths,
        specs=[VM] * 5 + [SM] * 2,
        hold=(),
    )
    bit = stride
    while True:
        arrived = xor_permute(pay, "batch", bit)
        bit *= 2
        if bit == devices:
            break
        num, state, pay = call(merge_kernel, state_shapes, num, state, arrived, hold=())
    if stride == 1:
        partial = finish_project(num, state, arrived, out_row)
    else:
        attended = finish(num, state, arrived)
        stacked = jnp.concatenate(doubling(attended[None], 1, stride))
        wanted = reverse(jnp.bitwise_xor(jnp.arange(stride, dtype=jnp.int32), request), stride)
        stacked = stacked[wanted].reshape(stride, 2, BEAMS, width)
        attended = stacked.transpose(1, 2, 0, 3).reshape(2 * rows, width)
        partial = call(project_kernel, shape((rows, columns), f32), attended, out_row)
    other = xor_permute(partial, "tensor", 1)
    mine = call(add_kernel, pltpu.VMEM((1, rows, columns), bf16), partial, other, residual_row, hold=())
    near, far = doubling(mine, 1, devices, cross=True)
    hidden, activation = call(
        up_kernel,
        (shape((rows, columns), bf16), shape((rows, hidden_units), bf16)),
        near,
        far,
        up_weight,
        hold=(),
    )
    arrived = xor_permute(activation, "tensor", 1)
    before = call(
        functools.partial(down_kernel, True), shape((rows, out_columns), f32), activation, down_weight, hold=()
    )
    keep, send = call(
        functools.partial(down_kernel, False),
        (shape((rows // 2, out_columns), f32),) * 2,
        arrived,
        down_weight,
        before,
    )
    order = ring(devices)
    groups = []
    for r in range(stride):
        groups.append([(beam * stride + r) * 2 for beam in order])
        groups.append([(beam * stride + r) * 2 + 1 for beam in reversed(order)])
    gathered = lax.all_gather(init_cache[0], ("batch", "tensor"), axis_index_groups=groups)
    bit = 1
    while True:
        arrived = xor_permute(send, "batch", bit)
        bit *= 2
        if 2 * bit == devices:
            cache = place(stride, order, gathered, new_row, parents, lengths)
            arrived, cache = pin(arrived, cache)
        total = keep + arrived
        if bit == devices:
            break
        half = total.shape[0] // 2
        keep, send = total[:half], total[half:]
    ffn_row = total.astype(bf16)
    return (hidden[None], ffn_row[None], cache[None])


def solution(mesh):
    placed = (
        P(("grp", "batch"), None, None, "tensor"),
        P(("grp", "batch"), None, None, "tensor"),
        P(None, ("grp", "batch"), None, "tensor"),
        P(None, ("grp", "batch"), None, "tensor"),
        P(None, "grp", "batch"),
        P(None, "tensor", "batch"),
        P(None, ("batch", "tensor")),
        P("batch", "tensor"),
        P(None, "grp"),
        P("grp"),
    )
    return jax.shard_map(
        body,
        mesh=mesh,
        in_specs=placed,
        out_specs=(
            P(None, "grp", "batch"),
            P(None, ("grp", "batch"), "tensor"),
            P(("grp", "batch"), None, None, "tensor"),
        ),
        check_vma=False,
    )
```

```python
import functools
import math

import jax
import jax.numpy as jnp
from jax import lax
from jax.experimental import pallas as pl
from jax.experimental.pallas import tpu as pltpu
from jax.sharding import PartitionSpec as P

HD = 128
LANES = 128
SLOT = 16
BEAMS = 8
LOW = -1e30
MIB = 1024 * 1024
STEP_FLOPS = 1_000_000_000

VM = pl.BlockSpec(memory_space=pltpu.VMEM)
SM = pl.BlockSpec(memory_space=pltpu.SMEM)
ANY = pl.BlockSpec(memory_space=pl.ANY)


def xor_permute(value, axis, bit):
    total = lax.axis_size(axis)
    return lax.ppermute(value, axis, [(i, i ^ bit) for i in range(total)])


def cross_permute(value, bit):
    pairs = [(2 * i + t, 2 * (i ^ bit) + 1 - t) for i in range(lax.axis_size("batch")) for t in range(2)]
    return lax.ppermute(value, ("batch", "tensor"), pairs)


def reverse(index, size):
    bits = size.bit_length() - 1
    return sum(((index >> k) & 1) << (bits - 1 - k) for k in range(bits))


def doubling(buffer, first, last, cross=False):
    bit = last
    while True:
        bit //= 2
        other = cross_permute(buffer, bit) if cross else xor_permute(buffer, "batch", bit)
        if bit == first:
            return buffer, other
        buffer = jnp.concatenate([buffer, other])


def drop(kernel, first, count, *refs):
    kernel(*refs[:first], *refs[first + count :])


def call(kernel, out, *args, specs=None, hold=(), vmem=8, flops=STEP_FLOPS, moved=0):
    first = len(args)
    return pl.pallas_call(
        functools.partial(drop, kernel, first, len(hold)),
        out_shape=out,
        in_specs=(specs or [VM] * first) + [ANY] * len(hold),
        out_specs=jax.tree.map(lambda _: VM, out),
        compiler_params=pltpu.CompilerParams(vmem_limit_bytes=vmem * MIB),
        cost_estimate=pl.CostEstimate(flops=flops, bytes_accessed=moved, transcendentals=0),
    )(*args, *hold)


def in_hbm(value):
    return pltpu.with_memory_space_constraint(value, pltpu.HBM)


def pin(value, loaded):
    return lax.optimization_barrier((value, loaded))


def start_all(copies):
    for copy in copies:
        copy.start()
    for copy in copies:
        copy.wait()


def fetch_kernel(count, *refs):
    sems = refs[-1]
    outs = refs[-1 - count : -1]
    copies = []
    for i in range(count):
        parts = refs[i].shape[0] if len(refs[i].shape) > 2 else 1
        for k in range(parts):
            source, target = (refs[i].at[k], outs[i].at[k]) if parts > 1 else (refs[i], outs[i])
            copies.append(pltpu.make_async_copy(source, target, sems.at[i, k]))
    start_all(copies)


def fetch(arrays, after):
    count = len(arrays)
    return pl.pallas_call(
        functools.partial(fetch_kernel, count),
        out_shape=[pltpu.VMEM(x.shape, x.dtype) for x in arrays],
        in_specs=[ANY] * (count + 1),
        out_specs=[VM] * count,
        scratch_shapes=[pltpu.SemaphoreType.DMA((count, 2))],
        compiler_params=pltpu.CompilerParams(vmem_limit_bytes=2 * MIB),
        cost_estimate=pl.CostEstimate(flops=0, bytes_accessed=2 * MIB, transcendentals=0),
    )(*arrays, after)


def split3(value):
    high = value.astype(jnp.bfloat16).astype(jnp.float32)
    rest = value - high
    middle = rest.astype(jnp.bfloat16).astype(jnp.float32)
    return high, middle, rest - middle


def export(num_ref, state_ref, pay_ref, peaks, totals):
    heads = num_ref.shape[1] // HD
    inverse = jnp.where(totals > 0.0, 1.0 / jnp.where(totals > 0.0, totals, 1.0), 0.0)
    for h in range(heads):
        cols = slice(h * HD, (h + 1) * HD)
        pay_ref[:, cols] = (num_ref[:, cols] * inverse[:, h : h + 1]).astype(jnp.bfloat16)
    state_ref[:, :LANES] = peaks
    state_ref[:, LANES:] = totals
    group = lax.broadcasted_iota(jnp.int32, peaks.shape, 1) // SLOT
    extra = jnp.zeros_like(peaks)
    for g, part in enumerate(split3(peaks) + split3(totals)):
        extra = jnp.where(group == g, pltpu.roll(part, g * SLOT, 1) if g else part, extra)
    pay_ref[:, heads * HD :] = extra.astype(jnp.bfloat16)


def attend_kernel(
    stride, near_ref, far_ref, cache_ref, memory_ref, new_ref, parents_ref, lengths_ref, num_ref, state_ref, pay_ref
):
    position = lax.axis_index("batch")
    own, request = position // stride, lax.rem(position, stride)
    length = lengths_ref[request]
    rows, width = num_ref.shape
    heads = width // HD
    past = cache_ref.shape[1]
    span = past + memory_ref.shape[1]
    f32, bf16 = jnp.float32, jnp.bfloat16

    to = lax.broadcasted_iota(jnp.int32, (rows, BEAMS), 0)
    source = lax.broadcasted_iota(jnp.int32, (rows, BEAMS), 1)

    def place_rows(piece_ref, first):
        beam = jnp.bitwise_xor(reverse(first + source // 2, BEAMS), own)
        order = jnp.where(to == (source % 2) * BEAMS + beam, 1.0, 0.0).astype(bf16)
        return jnp.dot(order, piece_ref[...], preferred_element_type=f32)

    query = (place_rows(near_ref, 0) + place_rows(far_ref, BEAMS // 2)).astype(bf16)

    row = lax.broadcasted_iota(jnp.int32, (rows, span), 0)
    slot = lax.broadcasted_iota(jnp.int32, (rows, span), 1)
    parent = jnp.zeros_like(row)
    for b in range(BEAMS):
        parent = jnp.where(row == b, parents_ref[0, b * stride + request], parent)
    in_past = ((slot < length) & (parent == own)) | ((slot == length) & (row == own))
    valid = jnp.where(row < BEAMS, jnp.where(in_past, 1, 0), jnp.where(slot >= past, 1, 0)) == 1
    fresh = lax.broadcasted_iota(jnp.int32, (past, HD), 0) == length
    lane = lax.broadcasted_iota(jnp.int32, (rows, LANES), 1)
    all_cols = [slice(h * HD, (h + 1) * HD) for h in range(heads)]

    def block(kind, cols):
        old = cache_ref[kind, :, cols].astype(f32)
        new = new_ref[kind : kind + 1, cols].astype(f32)
        merged = jnp.where(fresh, new, old).astype(bf16)
        return jnp.concatenate([merged, memory_ref[kind, :, cols]])

    scores = [
        lax.dot_general(
            query[:, cols], block(0, cols), (((1,), (1,)), ((), ())), preferred_element_type=f32
        )
        for cols in all_cols
    ]
    values = [block(1, cols) for cols in all_cols]
    scores = [jnp.where(valid, s * (1.0 / math.sqrt(HD)), LOW) for s in scores]
    tops = [jnp.max(s, axis=1, keepdims=True) for s in scores]
    weights = [jnp.where(valid, jnp.exp(s - t), 0.0) for s, t in zip(scores, tops)]
    sums = [jnp.sum(w, axis=1, keepdims=True) for w in weights]
    highs = [w.astype(bf16) for w in weights]
    lows = [(w - high.astype(f32)).astype(bf16) for w, high in zip(weights, highs)]
    both = [
        jnp.dot(jnp.concatenate([high, low]), v, preferred_element_type=f32)
        for high, low, v in zip(highs, lows, values)
    ]
    peaks = jnp.zeros((rows, LANES), f32)
    totals = jnp.zeros((rows, LANES), f32)
    for h, cols in enumerate(all_cols):
        num_ref[:, cols] = both[h][:rows] + both[h][rows:]
        peaks = jnp.where(lane == h, tops[h], peaks)
        totals = jnp.where(lane == h, sums[h], totals)
    export(num_ref, state_ref, pay_ref, peaks, totals)


def combine(num_ref, state_ref, pay_ref, out_ref):
    heads = num_ref.shape[1] // HD
    extra = pay_ref[:, heads * HD :].astype(jnp.float32)
    summed = extra + pltpu.roll(extra, LANES - SLOT, 1) + pltpu.roll(extra, LANES - 2 * SLOT, 1)
    other_total = pltpu.roll(summed, LANES - 3 * SLOT, 1)
    lane = lax.broadcasted_iota(jnp.int32, extra.shape, 1)
    used = lane < SLOT
    other_peak = jnp.where(used, summed, 0.0)
    other_total = jnp.where(used, other_total, 0.0)
    own_peak, own_total = state_ref[:, :LANES], state_ref[:, LANES:]
    peaks = jnp.maximum(own_peak, other_peak)
    own_factor = jnp.exp(own_peak - peaks)
    other_factor = jnp.exp(other_peak - peaks) * other_total
    totals = own_total * own_factor + other_factor
    for h in range(heads):
        cols = slice(h * HD, (h + 1) * HD)
        other = pay_ref[:, cols].astype(jnp.float32)
        out_ref[:, cols] = num_ref[:, cols] * own_factor[:, h : h + 1] + other * other_factor[:, h : h + 1]
    return peaks, totals


def merge_kernel(num_ref, state_ref, pay_ref, num_out, state_out, pay_out):
    peaks, totals = combine(num_ref, state_ref, pay_ref, num_out)
    export(num_out, state_out, pay_out, peaks, totals)


def finish_kernel(num_ref, state_ref, pay_ref, out_ref, num):
    _, totals = combine(num_ref, state_ref, pay_ref, num)
    for h in range(num.shape[1] // HD):
        cols = slice(h * HD, (h + 1) * HD)
        out_ref[:, cols] = (num[:, cols] / totals[:, h : h + 1]).astype(jnp.bfloat16)


def finish(num, state, pay):
    return pl.pallas_call(
        finish_kernel,
        out_shape=jax.ShapeDtypeStruct(num.shape, jnp.bfloat16),
        in_specs=[VM] * 3,
        out_specs=VM,
        scratch_shapes=[pltpu.VMEM(num.shape, jnp.float32)],
        compiler_params=pltpu.CompilerParams(vmem_limit_bytes=8 * MIB),
        cost_estimate=pl.CostEstimate(flops=STEP_FLOPS, bytes_accessed=0, transcendentals=0),
    )(num, state, pay)


def project_kernel(attended_ref, weight_ref, out_ref):
    rows = out_ref.shape[0]
    first = jnp.dot(attended_ref[...], weight_ref[0], preferred_element_type=jnp.float32)
    second = jnp.dot(attended_ref[...], weight_ref[1], preferred_element_type=jnp.float32)
    out_ref[...] = first[:rows] + second[rows:]


def finish_project_kernel(num_ref, state_ref, pay_ref, weight_ref, out_ref, num, attended):
    finish_kernel(num_ref, state_ref, pay_ref, attended, num)
    project_kernel(attended, weight_ref, out_ref)


def finish_project(num, state, pay, weight):
    rows, columns = num.shape[0] // 2, weight.shape[2]
    return pl.pallas_call(
        finish_project_kernel,
        out_shape=jax.ShapeDtypeStruct((rows, columns), jnp.float32),
        in_specs=[VM] * 4,
        out_specs=VM,
        scratch_shapes=[pltpu.VMEM(num.shape, jnp.float32), pltpu.VMEM(num.shape, jnp.bfloat16)],
        compiler_params=pltpu.CompilerParams(vmem_limit_bytes=8 * MIB),
        cost_estimate=pl.CostEstimate(flops=2 * STEP_FLOPS, bytes_accessed=0, transcendentals=0),
    )(num, state, pay, weight)


def add_kernel(own_ref, other_ref, residual_ref, out_ref):
    total = residual_ref[0].astype(jnp.float32) + (own_ref[...] + other_ref[...])
    out_ref[0] = total.astype(jnp.bfloat16)


def up_kernel(near_ref, far_ref, weight_ref, hidden_ref, out_ref):
    half, _, depth = near_ref.shape
    position = lax.axis_index("batch")
    hidden_ref[...] = near_ref[0]
    total = jnp.zeros(out_ref.shape, jnp.float32)
    for j in range(2 * half):
        block = near_ref[j] if j < half else far_ref[j - half]
        start = pl.multiple_of(jnp.bitwise_xor(position, reverse(j, 2 * half)) * depth, depth)
        total = total + jnp.dot(block, weight_ref[pl.ds(start, depth), :], preferred_element_type=jnp.float32)
    out_ref[...] = (0.5 * total * (1.0 + lax.erf(total * math.sqrt(0.5)))).astype(jnp.bfloat16)


def reorder(activation):
    rows = activation.shape[0]
    position = lax.axis_index("batch")
    to = lax.broadcasted_iota(jnp.int32, (rows, rows), 0)
    source = lax.broadcasted_iota(jnp.int32, (rows, rows), 1)
    order = jnp.where(source == jnp.bitwise_xor(reverse(to, rows), position), 1.0, 0.0).astype(jnp.bfloat16)
    return jnp.dot(order, activation, preferred_element_type=jnp.float32).astype(jnp.bfloat16)


def down_kernel(mine, act_ref, weight_ref, *rest):
    depth = act_ref.shape[1]
    side = lax.axis_index("tensor")
    start = pl.multiple_of((side if mine else 1 - side) * depth, depth)
    part = jnp.dot(
        reorder(act_ref[...]), weight_ref[pl.ds(start, depth), :], preferred_element_type=jnp.float32
    )
    if mine:
        rest[0][...] = part
        return
    before, keep_ref, send_ref = rest
    total = before[...] + part
    half = total.shape[0] // 2
    keep_ref[...] = total[:half]
    send_ref[...] = total[half:]


def pick(wanted, near, refs, use):
    apart = jnp.bitwise_xor(wanted, near)
    found = jnp.int32(0)
    for k, offset in enumerate((0, 4, 1, 5)):
        found = jnp.where(apart == offset, k, found)
    for k, ref in enumerate(refs):
        pl.when(found == k)(functools.partial(use, ref))


def select_kernel(stride, own_ref, far_ref, side_ref, both_ref, parents_ref, out_ref):
    position = lax.axis_index("batch")
    wanted = parents_ref[0, jnp.bitwise_xor(position, 2 * stride)]

    def use(ref):
        out_ref[...] = ref[...]

    pick(wanted, position // stride, (own_ref, far_ref, side_ref, both_ref), use)


def place_kernel(stride, own_ref, far_ref, side_ref, both_ref, sent_ref, new_ref, parents_ref, lengths_ref, out_ref):
    position = lax.axis_index("batch")
    beam, request = position // stride, lax.rem(position, stride)
    parent = parents_ref[0, position]
    slots = lax.broadcasted_iota(jnp.int32, out_ref.shape[1:], 0)

    def use(ref):
        for kind in range(2):
            old = ref[kind].astype(jnp.float32)
            new = new_ref[kind : kind + 1, :].astype(jnp.float32)
            out_ref[kind] = jnp.where(slots == lengths_ref[request], new, old).astype(jnp.bfloat16)

    held = (jnp.bitwise_xor(parent, beam) // 2) % 2 == 0
    pl.when(held)(lambda: pick(parent, beam, (own_ref, far_ref, side_ref, both_ref), use))
    pl.when(jnp.logical_not(held))(lambda: use(sent_ref))


def body(
    init_cache,
    memory,
    queries,
    new_kv,
    residual,
    out_weight,
    up_weight,
    down_weight,
    parents,
    lengths,
):
    devices = lax.axis_size("batch")
    stride = devices // BEAMS
    position = lax.axis_index("batch")
    request = position % stride
    width = queries.shape[-1]
    rows = parents.shape[1]
    columns = out_weight.shape[2]
    hidden_units = up_weight.shape[1]
    out_columns = down_weight.shape[1]
    f32, bf16 = jnp.float32, jnp.bfloat16
    shape = jax.ShapeDtypeStruct
    down_weight = pltpu.with_memory_space_constraint(down_weight, pltpu.VMEM)
    up_weight = pltpu.with_memory_space_constraint(up_weight, pltpu.VMEM)
    sources = (queries[0, 0], init_cache[0], memory[0], new_kv[0, 0], residual)
    bit = devices // 2
    other = xor_permute(queries[0, 0], "batch", bit)
    far_row = xor_permute(init_cache[0], "batch", 4 * stride)
    side_row = xor_permute(init_cache[0], "batch", stride)
    loaded = fetch([in_hbm(x) for x in sources], queries[0, 0])
    other, (query, cache_row, memory_row, new_row, residual_row) = pin(other, loaded)
    query, far = doubling(jnp.concatenate([query, other]), stride, bit)
    far, (out_row,) = pin(far, fetch([in_hbm(out_weight)], query))
    state_shapes = (
        shape((2 * BEAMS, width), f32),
        shape((2 * BEAMS, 2 * LANES), f32),
        shape((2 * BEAMS, width + LANES), bf16),
    )
    num, state, pay = call(
        functools.partial(attend_kernel, stride),
        state_shapes,
        query,
        far,
        cache_row,
        memory_row,
        new_row,
        parents,
        lengths,
        specs=[VM] * 5 + [SM] * 2,
        hold=(side_row,),
    )
    bit = stride
    while True:
        arrived = xor_permute(pay, "batch", bit)
        bit *= 2
        if bit == devices:
            break
        num, state, pay = call(merge_kernel, state_shapes, num, state, arrived)
        if bit == 2 * stride:
            both_row = xor_permute(pin(far_row, num)[0], "batch", stride)
    if stride == 1:
        partial = finish_project(num, state, arrived, out_row)
    else:
        attended = finish(num, state, arrived)
        stacked = jnp.concatenate(doubling(attended[None], 1, stride))
        wanted = reverse(jnp.bitwise_xor(jnp.arange(stride, dtype=jnp.int32), request), stride)
        stacked = stacked[wanted].reshape(stride, 2, BEAMS, width)
        attended = stacked.transpose(1, 2, 0, 3).reshape(2 * rows, width)
        partial = call(project_kernel, shape((rows, columns), f32), attended, out_row)
    other = xor_permute(partial, "tensor", 1)
    rows_held = (cache_row, far_row, side_row, pin(both_row, partial)[0])
    sent_row = call(
        functools.partial(select_kernel, stride),
        shape(cache_row.shape, bf16),
        *rows_held,
        parents,
        specs=[VM] * 4 + [SM],
    )
    sent_row = xor_permute(sent_row, "batch", 2 * stride)
    mine = call(add_kernel, pltpu.VMEM((1, rows, columns), bf16), partial, other, residual_row, hold=())
    near, far = doubling(mine, 1, devices, cross=True)
    hidden, activation = call(
        up_kernel,
        (shape((rows, columns), bf16), shape((rows, hidden_units), bf16)),
        near,
        far,
        up_weight,
        hold=(),
    )
    arrived = xor_permute(activation, "tensor", 1)
    before = call(
        functools.partial(down_kernel, True), shape((rows, out_columns), f32), activation, down_weight, hold=()
    )
    keep, send = call(
        functools.partial(down_kernel, False),
        (shape((rows // 2, out_columns), f32),) * 2,
        arrived,
        down_weight,
        before,
    )
    bit = 1
    while True:
        arrived = xor_permute(send, "batch", bit)
        bit *= 2
        if 2 * bit == devices:
            cache = call(
                functools.partial(place_kernel, stride),
                shape(cache_row.shape, bf16),
                *rows_held,
                sent_row,
                new_row,
                parents,
                lengths,
                specs=[VM] * 6 + [SM] * 2,
            )
            arrived, cache = pin(arrived, cache)
        total = keep + arrived
        if bit == devices:
            break
        half = total.shape[0] // 2
        keep, send = total[:half], total[half:]
    ffn_row = total.astype(bf16)
    return (hidden[None], ffn_row[None], cache[None])


def solution(mesh):
    placed = (
        P(("grp", "batch"), None, None, "tensor"),
        P(("grp", "batch"), None, None, "tensor"),
        P(None, ("grp", "batch"), None, "tensor"),
        P(None, ("grp", "batch"), None, "tensor"),
        P(None, "grp", "batch"),
        P(None, "tensor", "batch"),
        P(None, ("batch", "tensor")),
        P("batch", "tensor"),
        P(None, "grp"),
        P("grp"),
    )
    return jax.shard_map(
        body,
        mesh=mesh,
        in_specs=placed,
        out_specs=(
            P(None, "grp", "batch"),
            P(None, ("grp", "batch"), "tensor"),
            P(("grp", "batch"), None, None, "tensor"),
        ),
        check_vma=False,
    )
```

```python
import functools
import math

import jax
import jax.numpy as jnp
from jax import lax
from jax.experimental import pallas as pl
from jax.experimental.pallas import tpu as pltpu
from jax.sharding import PartitionSpec as P

HD = 128
LANES = 128
SLOT = 16
BEAMS = 8
LOW = -1e30
MIB = 1024 * 1024
STEP_FLOPS = 1_000_000_000

VM = pl.BlockSpec(memory_space=pltpu.VMEM)
SM = pl.BlockSpec(memory_space=pltpu.SMEM)
ANY = pl.BlockSpec(memory_space=pl.ANY)


def xor_permute(value, axis, bit):
    total = lax.axis_size(axis)
    return lax.ppermute(value, axis, [(i, i ^ bit) for i in range(total)])


def cross_permute(value, bit):
    pairs = [(2 * i + t, 2 * (i ^ bit) + 1 - t) for i in range(lax.axis_size("batch")) for t in range(2)]
    return lax.ppermute(value, ("batch", "tensor"), pairs)


def reverse(index, size):
    bits = size.bit_length() - 1
    return sum(((index >> k) & 1) << (bits - 1 - k) for k in range(bits))


def doubling(buffer, first, last, cross=False):
    bit = last
    while True:
        bit //= 2
        other = cross_permute(buffer, bit) if cross else xor_permute(buffer, "batch", bit)
        if bit == first:
            return buffer, other
        buffer = jnp.concatenate([buffer, other])


def drop(kernel, first, count, *refs):
    kernel(*refs[:first], *refs[first + count :])


def call(kernel, out, *args, specs=None, hold=(), vmem=8, flops=STEP_FLOPS, moved=0):
    first = len(args)
    return pl.pallas_call(
        functools.partial(drop, kernel, first, len(hold)),
        out_shape=out,
        in_specs=(specs or [VM] * first) + [ANY] * len(hold),
        out_specs=jax.tree.map(lambda _: VM, out),
        compiler_params=pltpu.CompilerParams(vmem_limit_bytes=vmem * MIB),
        cost_estimate=pl.CostEstimate(flops=flops, bytes_accessed=moved, transcendentals=0),
    )(*args, *hold)


def in_hbm(value):
    return pltpu.with_memory_space_constraint(value, pltpu.HBM)


def pin(value, loaded):
    return lax.optimization_barrier((value, loaded))


def start_all(copies):
    for copy in copies:
        copy.start()
    for copy in copies:
        copy.wait()


def fetch_kernel(count, *refs):
    sems = refs[-1]
    outs = refs[-1 - count : -1]
    copies = []
    for i in range(count):
        parts = refs[i].shape[0] if len(refs[i].shape) > 2 else 1
        for k in range(parts):
            source, target = (refs[i].at[k], outs[i].at[k]) if parts > 1 else (refs[i], outs[i])
            copies.append(pltpu.make_async_copy(source, target, sems.at[i, k]))
    start_all(copies)


def fetch(arrays, after):
    count = len(arrays)
    return pl.pallas_call(
        functools.partial(fetch_kernel, count),
        out_shape=[pltpu.VMEM(x.shape, x.dtype) for x in arrays],
        in_specs=[ANY] * (count + 1),
        out_specs=[VM] * count,
        scratch_shapes=[pltpu.SemaphoreType.DMA((count, 2))],
        compiler_params=pltpu.CompilerParams(vmem_limit_bytes=2 * MIB),
        cost_estimate=pl.CostEstimate(flops=0, bytes_accessed=2 * MIB, transcendentals=0),
    )(*arrays, after)


def split3(value):
    high = value.astype(jnp.bfloat16).astype(jnp.float32)
    rest = value - high
    middle = rest.astype(jnp.bfloat16).astype(jnp.float32)
    return high, middle, rest - middle


def export(num_ref, state_ref, pay_ref, peaks, totals):
    heads = num_ref.shape[1] // HD
    inverse = jnp.where(totals > 0.0, 1.0 / jnp.where(totals > 0.0, totals, 1.0), 0.0)
    for h in range(heads):
        cols = slice(h * HD, (h + 1) * HD)
        pay_ref[:, cols] = (num_ref[:, cols] * inverse[:, h : h + 1]).astype(jnp.bfloat16)
    state_ref[:, :LANES] = peaks
    state_ref[:, LANES:] = totals
    group = lax.broadcasted_iota(jnp.int32, peaks.shape, 1) // SLOT
    extra = jnp.zeros_like(peaks)
    for g, part in enumerate(split3(peaks) + split3(totals)):
        extra = jnp.where(group == g, pltpu.roll(part, g * SLOT, 1) if g else part, extra)
    pay_ref[:, heads * HD :] = extra.astype(jnp.bfloat16)


def attend_kernel(
    stride, near_ref, far_ref, cache_ref, memory_ref, new_ref, parents_ref, lengths_ref, num_ref, state_ref, pay_ref
):
    position = lax.axis_index("batch")
    own, request = position // stride, lax.rem(position, stride)
    length = lengths_ref[request]
    rows, width = num_ref.shape
    heads = width // HD
    past = cache_ref.shape[1]
    span = past + memory_ref.shape[1]
    f32, bf16 = jnp.float32, jnp.bfloat16

    to = lax.broadcasted_iota(jnp.int32, (rows, BEAMS), 0)
    source = lax.broadcasted_iota(jnp.int32, (rows, BEAMS), 1)

    def place_rows(piece_ref, first):
        beam = jnp.bitwise_xor(reverse(first + source // 2, BEAMS), own)
        order = jnp.where(to == (source % 2) * BEAMS + beam, 1.0, 0.0).astype(bf16)
        return jnp.dot(order, piece_ref[...], preferred_element_type=f32)

    query = (place_rows(near_ref, 0) + place_rows(far_ref, BEAMS // 2)).astype(bf16)

    row = lax.broadcasted_iota(jnp.int32, (rows, span), 0)
    slot = lax.broadcasted_iota(jnp.int32, (rows, span), 1)
    parent = jnp.zeros_like(row)
    for b in range(BEAMS):
        parent = jnp.where(row == b, parents_ref[0, b * stride + request], parent)
    in_past = ((slot < length) & (parent == own)) | ((slot == length) & (row == own))
    valid = jnp.where(row < BEAMS, jnp.where(in_past, 1, 0), jnp.where(slot >= past, 1, 0)) == 1
    fresh = lax.broadcasted_iota(jnp.int32, (past, HD), 0) == length
    lane = lax.broadcasted_iota(jnp.int32, (rows, LANES), 1)
    all_cols = [slice(h * HD, (h + 1) * HD) for h in range(heads)]

    def block(kind, cols):
        old = cache_ref[kind, :, cols].astype(f32)
        new = new_ref[kind : kind + 1, cols].astype(f32)
        merged = jnp.where(fresh, new, old).astype(bf16)
        return jnp.concatenate([merged, memory_ref[kind, :, cols]])

    scores = [
        lax.dot_general(
            query[:, cols], block(0, cols), (((1,), (1,)), ((), ())), preferred_element_type=f32
        )
        for cols in all_cols
    ]
    values = [block(1, cols) for cols in all_cols]
    scores = [jnp.where(valid, s * (1.0 / math.sqrt(HD)), LOW) for s in scores]
    tops = [jnp.max(s, axis=1, keepdims=True) for s in scores]
    weights = [jnp.where(valid, jnp.exp(s - t), 0.0) for s, t in zip(scores, tops)]
    sums = [jnp.sum(w, axis=1, keepdims=True) for w in weights]
    highs = [w.astype(bf16) for w in weights]
    lows = [(w - high.astype(f32)).astype(bf16) for w, high in zip(weights, highs)]
    both = [
        jnp.dot(jnp.concatenate([high, low]), v, preferred_element_type=f32)
        for high, low, v in zip(highs, lows, values)
    ]
    peaks = jnp.zeros((rows, LANES), f32)
    totals = jnp.zeros((rows, LANES), f32)
    for h, cols in enumerate(all_cols):
        num_ref[:, cols] = both[h][:rows] + both[h][rows:]
        peaks = jnp.where(lane == h, tops[h], peaks)
        totals = jnp.where(lane == h, sums[h], totals)
    export(num_ref, state_ref, pay_ref, peaks, totals)


def combine(num_ref, state_ref, pay_ref, out_ref):
    heads = num_ref.shape[1] // HD
    extra = pay_ref[:, heads * HD :].astype(jnp.float32)
    summed = extra + pltpu.roll(extra, LANES - SLOT, 1) + pltpu.roll(extra, LANES - 2 * SLOT, 1)
    other_total = pltpu.roll(summed, LANES - 3 * SLOT, 1)
    lane = lax.broadcasted_iota(jnp.int32, extra.shape, 1)
    used = lane < SLOT
    other_peak = jnp.where(used, summed, 0.0)
    other_total = jnp.where(used, other_total, 0.0)
    own_peak, own_total = state_ref[:, :LANES], state_ref[:, LANES:]
    peaks = jnp.maximum(own_peak, other_peak)
    own_factor = jnp.exp(own_peak - peaks)
    other_factor = jnp.exp(other_peak - peaks) * other_total
    totals = own_total * own_factor + other_factor
    for h in range(heads):
        cols = slice(h * HD, (h + 1) * HD)
        other = pay_ref[:, cols].astype(jnp.float32)
        out_ref[:, cols] = num_ref[:, cols] * own_factor[:, h : h + 1] + other * other_factor[:, h : h + 1]
    return peaks, totals


def merge_kernel(num_ref, state_ref, pay_ref, num_out, state_out, pay_out):
    peaks, totals = combine(num_ref, state_ref, pay_ref, num_out)
    export(num_out, state_out, pay_out, peaks, totals)


def finish_kernel(num_ref, state_ref, pay_ref, out_ref, num):
    _, totals = combine(num_ref, state_ref, pay_ref, num)
    for h in range(num.shape[1] // HD):
        cols = slice(h * HD, (h + 1) * HD)
        out_ref[:, cols] = (num[:, cols] / totals[:, h : h + 1]).astype(jnp.bfloat16)


def finish(num, state, pay):
    return pl.pallas_call(
        finish_kernel,
        out_shape=jax.ShapeDtypeStruct(num.shape, jnp.bfloat16),
        in_specs=[VM] * 3,
        out_specs=VM,
        scratch_shapes=[pltpu.VMEM(num.shape, jnp.float32)],
        compiler_params=pltpu.CompilerParams(vmem_limit_bytes=8 * MIB),
        cost_estimate=pl.CostEstimate(flops=STEP_FLOPS, bytes_accessed=0, transcendentals=0),
    )(num, state, pay)


def project_kernel(attended_ref, weight_ref, out_ref):
    rows = out_ref.shape[0]
    first = jnp.dot(attended_ref[...], weight_ref[0], preferred_element_type=jnp.float32)
    second = jnp.dot(attended_ref[...], weight_ref[1], preferred_element_type=jnp.float32)
    out_ref[...] = first[:rows] + second[rows:]


def finish_project_kernel(num_ref, state_ref, pay_ref, weight_ref, out_ref, num, attended):
    finish_kernel(num_ref, state_ref, pay_ref, attended, num)
    project_kernel(attended, weight_ref, out_ref)


def finish_project(num, state, pay, weight):
    rows, columns = num.shape[0] // 2, weight.shape[2]
    return pl.pallas_call(
        finish_project_kernel,
        out_shape=jax.ShapeDtypeStruct((rows, columns), jnp.float32),
        in_specs=[VM] * 4,
        out_specs=VM,
        scratch_shapes=[pltpu.VMEM(num.shape, jnp.float32), pltpu.VMEM(num.shape, jnp.bfloat16)],
        compiler_params=pltpu.CompilerParams(vmem_limit_bytes=8 * MIB),
        cost_estimate=pl.CostEstimate(flops=2 * STEP_FLOPS, bytes_accessed=0, transcendentals=0),
    )(num, state, pay, weight)


def add_kernel(own_ref, other_ref, residual_ref, out_ref):
    total = residual_ref[0].astype(jnp.float32) + (own_ref[...] + other_ref[...])
    out_ref[0] = total.astype(jnp.bfloat16)


def up_kernel(near_ref, far_ref, weight_ref, hidden_ref, out_ref):
    half, _, depth = near_ref.shape
    position = lax.axis_index("batch")
    hidden_ref[...] = near_ref[0]
    total = jnp.zeros(out_ref.shape, jnp.float32)
    for j in range(2 * half):
        block = near_ref[j] if j < half else far_ref[j - half]
        start = pl.multiple_of(jnp.bitwise_xor(position, reverse(j, 2 * half)) * depth, depth)
        total = total + jnp.dot(block, weight_ref[pl.ds(start, depth), :], preferred_element_type=jnp.float32)
    out_ref[...] = (0.5 * total * (1.0 + lax.erf(total * math.sqrt(0.5)))).astype(jnp.bfloat16)


def reorder(activation):
    rows = activation.shape[0]
    position = lax.axis_index("batch")
    to = lax.broadcasted_iota(jnp.int32, (rows, rows), 0)
    source = lax.broadcasted_iota(jnp.int32, (rows, rows), 1)
    order = jnp.where(source == jnp.bitwise_xor(reverse(to, rows), position), 1.0, 0.0).astype(jnp.bfloat16)
    return jnp.dot(order, activation, preferred_element_type=jnp.float32).astype(jnp.bfloat16)


def down_kernel(mine, act_ref, weight_ref, *rest):
    depth = act_ref.shape[1]
    side = lax.axis_index("tensor")
    start = pl.multiple_of((side if mine else 1 - side) * depth, depth)
    part = jnp.dot(
        reorder(act_ref[...]), weight_ref[pl.ds(start, depth), :], preferred_element_type=jnp.float32
    )
    if mine:
        rest[0][...] = part
        return
    before, keep_ref, send_ref = rest
    total = before[...] + part
    half = total.shape[0] // 2
    keep_ref[...] = total[:half]
    send_ref[...] = total[half:]


def pick(wanted, near, refs, use):
    apart = jnp.bitwise_xor(wanted, near)
    found = jnp.int32(0)
    for k, offset in enumerate((0, 4, 1, 5)):
        found = jnp.where(apart == offset, k, found)
    for k, ref in enumerate(refs):
        pl.when(found == k)(functools.partial(use, ref))


def select_kernel(stride, own_ref, far_ref, side_ref, both_ref, parents_ref, out_ref):
    position = lax.axis_index("batch")
    wanted = parents_ref[0, jnp.bitwise_xor(position, 2 * stride)]

    def use(ref):
        out_ref[...] = ref[...]

    pick(wanted, position // stride, (own_ref, far_ref, side_ref, both_ref), use)


def place_kernel(stride, own_ref, far_ref, side_ref, both_ref, sent_ref, new_ref, parents_ref, lengths_ref, out_ref):
    position = lax.axis_index("batch")
    beam, request = position // stride, lax.rem(position, stride)
    parent = parents_ref[0, position]
    slots = lax.broadcasted_iota(jnp.int32, out_ref.shape[1:], 0)

    def use(ref):
        for kind in range(2):
            old = ref[kind].astype(jnp.float32)
            new = new_ref[kind : kind + 1, :].astype(jnp.float32)
            out_ref[kind] = jnp.where(slots == lengths_ref[request], new, old).astype(jnp.bfloat16)

    held = (jnp.bitwise_xor(parent, beam) // 2) % 2 == 0
    pl.when(held)(lambda: pick(parent, beam, (own_ref, far_ref, side_ref, both_ref), use))
    pl.when(jnp.logical_not(held))(lambda: use(sent_ref))


def body(
    init_cache,
    memory,
    queries,
    new_kv,
    residual,
    out_weight,
    up_weight,
    down_weight,
    parents,
    lengths,
):
    devices = lax.axis_size("batch")
    stride = devices // BEAMS
    position = lax.axis_index("batch")
    request = position % stride
    width = queries.shape[-1]
    rows = parents.shape[1]
    columns = out_weight.shape[2]
    hidden_units = up_weight.shape[1]
    out_columns = down_weight.shape[1]
    f32, bf16 = jnp.float32, jnp.bfloat16
    shape = jax.ShapeDtypeStruct
    down_weight = pltpu.with_memory_space_constraint(down_weight, pltpu.VMEM)
    up_weight = pltpu.with_memory_space_constraint(up_weight, pltpu.VMEM)
    sources = (queries[0, 0], init_cache[0], memory[0], new_kv[0, 0], residual)
    bit = devices // 2
    other = xor_permute(queries[0, 0], "batch", bit)
    far_row = xor_permute(init_cache[0], "batch", 4 * stride)
    side_row = xor_permute(init_cache[0], "batch", stride)
    loaded = fetch([in_hbm(x) for x in sources], queries[0, 0])
    other, (query, cache_row, memory_row, new_row, residual_row) = pin(other, loaded)
    query, far = doubling(jnp.concatenate([query, other]), stride, bit)
    far, (out_row,) = pin(far, fetch([in_hbm(out_weight)], query))
    state_shapes = (
        shape((2 * BEAMS, width), f32),
        shape((2 * BEAMS, 2 * LANES), f32),
        shape((2 * BEAMS, width + LANES), bf16),
    )
    num, state, pay = call(
        functools.partial(attend_kernel, stride),
        state_shapes,
        query,
        far,
        cache_row,
        memory_row,
        new_row,
        parents,
        lengths,
        specs=[VM] * 5 + [SM] * 2,
        hold=(side_row,),
    )
    bit = stride
    while True:
        arrived = xor_permute(pay, "batch", bit)
        bit *= 2
        if bit == devices:
            break
        hold = (far_row,) if bit == 4 * stride else ()
        num, state, pay = call(merge_kernel, state_shapes, num, state, arrived, hold=hold)
        if bit == 2 * stride:
            both_row = xor_permute(pin(far_row, num)[0], "batch", stride)
    if stride == 1:
        partial = finish_project(num, state, arrived, out_row)
    else:
        attended = finish(num, state, arrived)
        stacked = jnp.concatenate(doubling(attended[None], 1, stride))
        wanted = reverse(jnp.bitwise_xor(jnp.arange(stride, dtype=jnp.int32), request), stride)
        stacked = stacked[wanted].reshape(stride, 2, BEAMS, width)
        attended = stacked.transpose(1, 2, 0, 3).reshape(2 * rows, width)
        partial = call(project_kernel, shape((rows, columns), f32), attended, out_row)
    other = xor_permute(partial, "tensor", 1)
    rows_held = (cache_row, far_row, side_row, pin(both_row, partial)[0])
    sent_row = call(
        functools.partial(select_kernel, stride),
        shape(cache_row.shape, bf16),
        *rows_held,
        parents,
        specs=[VM] * 4 + [SM],
    )
    sent_row = xor_permute(sent_row, "batch", 2 * stride)
    mine = call(add_kernel, pltpu.VMEM((1, rows, columns), bf16), partial, other, residual_row, hold=())
    near, far = doubling(mine, 1, devices, cross=True)
    hidden, activation = call(
        up_kernel,
        (shape((rows, columns), bf16), shape((rows, hidden_units), bf16)),
        near,
        far,
        up_weight,
        hold=(),
    )
    arrived = xor_permute(activation, "tensor", 1)
    before = call(
        functools.partial(down_kernel, True), shape((rows, out_columns), f32), activation, down_weight, hold=()
    )
    keep, send = call(
        functools.partial(down_kernel, False),
        (shape((rows // 2, out_columns), f32),) * 2,
        arrived,
        down_weight,
        before,
    )
    bit = 1
    while True:
        arrived = xor_permute(send, "batch", bit)
        bit *= 2
        if 2 * bit == devices:
            cache = call(
                functools.partial(place_kernel, stride),
                shape(cache_row.shape, bf16),
                *rows_held,
                sent_row,
                new_row,
                parents,
                lengths,
                specs=[VM] * 6 + [SM] * 2,
            )
            arrived, cache = pin(arrived, cache)
        total = keep + arrived
        if bit == devices:
            break
        half = total.shape[0] // 2
        keep, send = total[:half], total[half:]
    ffn_row = total.astype(bf16)
    return (hidden[None], ffn_row[None], cache[None])


def solution(mesh):
    placed = (
        P(("grp", "batch"), None, None, "tensor"),
        P(("grp", "batch"), None, None, "tensor"),
        P(None, ("grp", "batch"), None, "tensor"),
        P(None, ("grp", "batch"), None, "tensor"),
        P(None, "grp", "batch"),
        P(None, "tensor", "batch"),
        P(None, ("batch", "tensor")),
        P("batch", "tensor"),
        P(None, "grp"),
        P("grp"),
    )
    return jax.shard_map(
        body,
        mesh=mesh,
        in_specs=placed,
        out_specs=(
            P(None, "grp", "batch"),
            P(None, ("grp", "batch"), "tensor"),
            P(("grp", "batch"), None, None, "tensor"),
        ),
        check_vma=False,
    )
```

```python
import functools
import math

import jax
import jax.numpy as jnp
from jax import lax
from jax.experimental import pallas as pl
from jax.experimental.pallas import tpu as pltpu
from jax.sharding import PartitionSpec as P

HD = 128
LANES = 128
SLOT = 16
BEAMS = 8
LOW = -1e30
MIB = 1024 * 1024
STEP_FLOPS = 1_000_000_000

VM = pl.BlockSpec(memory_space=pltpu.VMEM)
SM = pl.BlockSpec(memory_space=pltpu.SMEM)
ANY = pl.BlockSpec(memory_space=pl.ANY)


def xor_permute(value, axis, bit):
    total = lax.axis_size(axis)
    return lax.ppermute(value, axis, [(i, i ^ bit) for i in range(total)])


def cross_permute(value, bit):
    pairs = [(2 * i + t, 2 * (i ^ bit) + 1 - t) for i in range(lax.axis_size("batch")) for t in range(2)]
    return lax.ppermute(value, ("batch", "tensor"), pairs)


def reverse(index, size):
    bits = size.bit_length() - 1
    return sum(((index >> k) & 1) << (bits - 1 - k) for k in range(bits))


def doubling(buffer, first, last, cross=False):
    bit = last
    while True:
        bit //= 2
        other = cross_permute(buffer, bit) if cross else xor_permute(buffer, "batch", bit)
        if bit == first:
            return buffer, other
        buffer = jnp.concatenate([buffer, other])


def drop(kernel, first, count, *refs):
    kernel(*refs[:first], *refs[first + count :])


def call(kernel, out, *args, specs=None, hold=(), vmem=8, flops=STEP_FLOPS, moved=0):
    first = len(args)
    return pl.pallas_call(
        functools.partial(drop, kernel, first, len(hold)),
        out_shape=out,
        in_specs=(specs or [VM] * first) + [ANY] * len(hold),
        out_specs=jax.tree.map(lambda _: VM, out),
        compiler_params=pltpu.CompilerParams(vmem_limit_bytes=vmem * MIB),
        cost_estimate=pl.CostEstimate(flops=flops, bytes_accessed=moved, transcendentals=0),
    )(*args, *hold)


def in_hbm(value):
    return pltpu.with_memory_space_constraint(value, pltpu.HBM)


def pin(value, loaded):
    return lax.optimization_barrier((value, loaded))


def start_all(copies):
    for copy in copies:
        copy.start()
    for copy in copies:
        copy.wait()


def fetch_kernel(count, *refs):
    sems = refs[-1]
    outs = refs[-1 - count : -1]
    copies = []
    for i in range(count):
        parts = refs[i].shape[0] if len(refs[i].shape) > 2 else 1
        for k in range(parts):
            source, target = (refs[i].at[k], outs[i].at[k]) if parts > 1 else (refs[i], outs[i])
            copies.append(pltpu.make_async_copy(source, target, sems.at[i, k]))
    start_all(copies)


def fetch(arrays, after):
    count = len(arrays)
    return pl.pallas_call(
        functools.partial(fetch_kernel, count),
        out_shape=[pltpu.VMEM(x.shape, x.dtype) for x in arrays],
        in_specs=[ANY] * (count + 1),
        out_specs=[VM] * count,
        scratch_shapes=[pltpu.SemaphoreType.DMA((count, 2))],
        compiler_params=pltpu.CompilerParams(vmem_limit_bytes=2 * MIB),
        cost_estimate=pl.CostEstimate(flops=0, bytes_accessed=2 * MIB, transcendentals=0),
    )(*arrays, after)


def split3(value):
    high = value.astype(jnp.bfloat16).astype(jnp.float32)
    rest = value - high
    middle = rest.astype(jnp.bfloat16).astype(jnp.float32)
    return high, middle, rest - middle


def export(num_ref, state_ref, pay_ref, peaks, totals):
    heads = num_ref.shape[1] // HD
    inverse = jnp.where(totals > 0.0, 1.0 / jnp.where(totals > 0.0, totals, 1.0), 0.0)
    for h in range(heads):
        cols = slice(h * HD, (h + 1) * HD)
        pay_ref[:, cols] = (num_ref[:, cols] * inverse[:, h : h + 1]).astype(jnp.bfloat16)
    state_ref[:, :LANES] = peaks
    state_ref[:, LANES:] = totals
    group = lax.broadcasted_iota(jnp.int32, peaks.shape, 1) // SLOT
    extra = jnp.zeros_like(peaks)
    for g, part in enumerate(split3(peaks) + split3(totals)):
        extra = jnp.where(group == g, pltpu.roll(part, g * SLOT, 1) if g else part, extra)
    pay_ref[:, heads * HD :] = extra.astype(jnp.bfloat16)


def attend_kernel(
    stride, near_ref, far_ref, cache_ref, memory_ref, new_ref, parents_ref, lengths_ref, num_ref, state_ref, pay_ref
):
    position = lax.axis_index("batch")
    own, request = position // stride, lax.rem(position, stride)
    length = lengths_ref[request]
    rows, width = num_ref.shape
    heads = width // HD
    past = cache_ref.shape[1]
    span = past + memory_ref.shape[1]
    f32, bf16 = jnp.float32, jnp.bfloat16

    to = lax.broadcasted_iota(jnp.int32, (rows, BEAMS), 0)
    source = lax.broadcasted_iota(jnp.int32, (rows, BEAMS), 1)

    def place_rows(piece_ref, first):
        beam = jnp.bitwise_xor(reverse(first + source // 2, BEAMS), own)
        order = jnp.where(to == (source % 2) * BEAMS + beam, 1.0, 0.0).astype(bf16)
        return jnp.dot(order, piece_ref[...], preferred_element_type=f32)

    query = (place_rows(near_ref, 0) + place_rows(far_ref, BEAMS // 2)).astype(bf16)

    row = lax.broadcasted_iota(jnp.int32, (rows, span), 0)
    slot = lax.broadcasted_iota(jnp.int32, (rows, span), 1)
    parent = jnp.zeros_like(row)
    for b in range(BEAMS):
        parent = jnp.where(row == b, parents_ref[0, b * stride + request], parent)
    in_past = ((slot < length) & (parent == own)) | ((slot == length) & (row == own))
    valid = jnp.where(row < BEAMS, jnp.where(in_past, 1, 0), jnp.where(slot >= past, 1, 0)) == 1
    fresh = lax.broadcasted_iota(jnp.int32, (past, HD), 0) == length
    lane = lax.broadcasted_iota(jnp.int32, (rows, LANES), 1)
    all_cols = [slice(h * HD, (h + 1) * HD) for h in range(heads)]

    def block(kind, cols):
        old = cache_ref[kind, :, cols].astype(f32)
        new = new_ref[kind : kind + 1, cols].astype(f32)
        merged = jnp.where(fresh, new, old).astype(bf16)
        return jnp.concatenate([merged, memory_ref[kind, :, cols]])

    scores = [
        lax.dot_general(
            query[:, cols], block(0, cols), (((1,), (1,)), ((), ())), preferred_element_type=f32
        )
        for cols in all_cols
    ]
    values = [block(1, cols) for cols in all_cols]
    scores = [jnp.where(valid, s * (1.0 / math.sqrt(HD)), LOW) for s in scores]
    tops = [jnp.max(s, axis=1, keepdims=True) for s in scores]
    weights = [jnp.where(valid, jnp.exp(s - t), 0.0) for s, t in zip(scores, tops)]
    sums = [jnp.sum(w, axis=1, keepdims=True) for w in weights]
    highs = [w.astype(bf16) for w in weights]
    lows = [(w - high.astype(f32)).astype(bf16) for w, high in zip(weights, highs)]
    both = [
        jnp.dot(jnp.concatenate([high, low]), v, preferred_element_type=f32)
        for high, low, v in zip(highs, lows, values)
    ]
    peaks = jnp.zeros((rows, LANES), f32)
    totals = jnp.zeros((rows, LANES), f32)
    for h, cols in enumerate(all_cols):
        num_ref[:, cols] = both[h][:rows] + both[h][rows:]
        peaks = jnp.where(lane == h, tops[h], peaks)
        totals = jnp.where(lane == h, sums[h], totals)
    export(num_ref, state_ref, pay_ref, peaks, totals)


def combine(num_ref, state_ref, pay_ref, out_ref):
    heads = num_ref.shape[1] // HD
    extra = pay_ref[:, heads * HD :].astype(jnp.float32)
    summed = extra + pltpu.roll(extra, LANES - SLOT, 1) + pltpu.roll(extra, LANES - 2 * SLOT, 1)
    other_total = pltpu.roll(summed, LANES - 3 * SLOT, 1)
    lane = lax.broadcasted_iota(jnp.int32, extra.shape, 1)
    used = lane < SLOT
    other_peak = jnp.where(used, summed, 0.0)
    other_total = jnp.where(used, other_total, 0.0)
    own_peak, own_total = state_ref[:, :LANES], state_ref[:, LANES:]
    peaks = jnp.maximum(own_peak, other_peak)
    own_factor = jnp.exp(own_peak - peaks)
    other_factor = jnp.exp(other_peak - peaks) * other_total
    totals = own_total * own_factor + other_factor
    for h in range(heads):
        cols = slice(h * HD, (h + 1) * HD)
        other = pay_ref[:, cols].astype(jnp.float32)
        out_ref[:, cols] = num_ref[:, cols] * own_factor[:, h : h + 1] + other * other_factor[:, h : h + 1]
    return peaks, totals


def merge_kernel(num_ref, state_ref, pay_ref, num_out, state_out, pay_out):
    peaks, totals = combine(num_ref, state_ref, pay_ref, num_out)
    export(num_out, state_out, pay_out, peaks, totals)


def finish_kernel(num_ref, state_ref, pay_ref, out_ref, num):
    _, totals = combine(num_ref, state_ref, pay_ref, num)
    for h in range(num.shape[1] // HD):
        cols = slice(h * HD, (h + 1) * HD)
        out_ref[:, cols] = (num[:, cols] / totals[:, h : h + 1]).astype(jnp.bfloat16)


def finish(num, state, pay):
    return pl.pallas_call(
        finish_kernel,
        out_shape=jax.ShapeDtypeStruct(num.shape, jnp.bfloat16),
        in_specs=[VM] * 3,
        out_specs=VM,
        scratch_shapes=[pltpu.VMEM(num.shape, jnp.float32)],
        compiler_params=pltpu.CompilerParams(vmem_limit_bytes=8 * MIB),
        cost_estimate=pl.CostEstimate(flops=STEP_FLOPS, bytes_accessed=0, transcendentals=0),
    )(num, state, pay)


def project_kernel(attended_ref, weight_ref, out_ref):
    rows = out_ref.shape[0]
    first = jnp.dot(attended_ref[...], weight_ref[0], preferred_element_type=jnp.float32)
    second = jnp.dot(attended_ref[...], weight_ref[1], preferred_element_type=jnp.float32)
    out_ref[...] = first[:rows] + second[rows:]


def finish_project_kernel(num_ref, state_ref, pay_ref, weight_ref, out_ref, num, attended):
    finish_kernel(num_ref, state_ref, pay_ref, attended, num)
    project_kernel(attended, weight_ref, out_ref)


def finish_project(num, state, pay, weight):
    rows, columns = num.shape[0] // 2, weight.shape[2]
    return pl.pallas_call(
        finish_project_kernel,
        out_shape=jax.ShapeDtypeStruct((rows, columns), jnp.float32),
        in_specs=[VM] * 4,
        out_specs=VM,
        scratch_shapes=[pltpu.VMEM(num.shape, jnp.float32), pltpu.VMEM(num.shape, jnp.bfloat16)],
        compiler_params=pltpu.CompilerParams(vmem_limit_bytes=8 * MIB),
        cost_estimate=pl.CostEstimate(flops=2 * STEP_FLOPS, bytes_accessed=0, transcendentals=0),
    )(num, state, pay, weight)


def add_kernel(own_ref, other_ref, residual_ref, out_ref):
    total = residual_ref[0].astype(jnp.float32) + (own_ref[...] + other_ref[...])
    out_ref[0] = total.astype(jnp.bfloat16)


def up_kernel(near_ref, far_ref, weight_ref, hidden_ref, out_ref):
    half, _, depth = near_ref.shape
    position = lax.axis_index("batch")
    hidden_ref[...] = near_ref[0]
    total = jnp.zeros(out_ref.shape, jnp.float32)
    for j in range(2 * half):
        block = near_ref[j] if j < half else far_ref[j - half]
        start = pl.multiple_of(jnp.bitwise_xor(position, reverse(j, 2 * half)) * depth, depth)
        total = total + jnp.dot(block, weight_ref[pl.ds(start, depth), :], preferred_element_type=jnp.float32)
    out_ref[...] = (0.5 * total * (1.0 + lax.erf(total * math.sqrt(0.5)))).astype(jnp.bfloat16)


def reorder(activation):
    rows = activation.shape[0]
    position = lax.axis_index("batch")
    to = lax.broadcasted_iota(jnp.int32, (rows, rows), 0)
    source = lax.broadcasted_iota(jnp.int32, (rows, rows), 1)
    order = jnp.where(source == jnp.bitwise_xor(reverse(to, rows), position), 1.0, 0.0).astype(jnp.bfloat16)
    return jnp.dot(order, activation, preferred_element_type=jnp.float32).astype(jnp.bfloat16)


def down_kernel(mine, act_ref, weight_ref, *rest):
    depth = act_ref.shape[1]
    side = lax.axis_index("tensor")
    start = pl.multiple_of((side if mine else 1 - side) * depth, depth)
    part = jnp.dot(
        reorder(act_ref[...]), weight_ref[pl.ds(start, depth), :], preferred_element_type=jnp.float32
    )
    if mine:
        rest[0][...] = part
        return
    before, keep_ref, send_ref = rest
    total = before[...] + part
    half = total.shape[0] // 2
    keep_ref[...] = total[:half]
    send_ref[...] = total[half:]


def pick(wanted, near, refs, use):
    apart = jnp.bitwise_xor(wanted, near)
    found = jnp.int32(0)
    for k, offset in enumerate((0, 4, 1, 5)):
        found = jnp.where(apart == offset, k, found)
    for k, ref in enumerate(refs):
        pl.when(found == k)(functools.partial(use, ref))


def select_kernel(stride, own_ref, far_ref, side_ref, both_ref, parents_ref, out_ref):
    position = lax.axis_index("batch")
    wanted = parents_ref[0, jnp.bitwise_xor(position, 2 * stride)]

    def use(ref):
        out_ref[...] = ref[...]

    pick(wanted, position // stride, (own_ref, far_ref, side_ref, both_ref), use)


def place_kernel(stride, own_ref, far_ref, side_ref, both_ref, sent_ref, new_ref, parents_ref, lengths_ref, out_ref):
    position = lax.axis_index("batch")
    beam, request = position // stride, lax.rem(position, stride)
    parent = parents_ref[0, position]
    slots = lax.broadcasted_iota(jnp.int32, out_ref.shape[1:], 0)

    def use(ref):
        for kind in range(2):
            old = ref[kind].astype(jnp.float32)
            new = new_ref[kind : kind + 1, :].astype(jnp.float32)
            out_ref[kind] = jnp.where(slots == lengths_ref[request], new, old).astype(jnp.bfloat16)

    held = (jnp.bitwise_xor(parent, beam) // 2) % 2 == 0
    pl.when(held)(lambda: pick(parent, beam, (own_ref, far_ref, side_ref, both_ref), use))
    pl.when(jnp.logical_not(held))(lambda: use(sent_ref))


def body(
    init_cache,
    memory,
    queries,
    new_kv,
    residual,
    out_weight,
    up_weight,
    down_weight,
    parents,
    lengths,
):
    devices = lax.axis_size("batch")
    stride = devices // BEAMS
    position = lax.axis_index("batch")
    request = position % stride
    width = queries.shape[-1]
    rows = parents.shape[1]
    columns = out_weight.shape[2]
    hidden_units = up_weight.shape[1]
    out_columns = down_weight.shape[1]
    f32, bf16 = jnp.float32, jnp.bfloat16
    shape = jax.ShapeDtypeStruct
    down_weight = pltpu.with_memory_space_constraint(down_weight, pltpu.VMEM)
    up_weight = pltpu.with_memory_space_constraint(up_weight, pltpu.VMEM)
    sources = (queries[0, 0], init_cache[0], memory[0], new_kv[0, 0], residual)
    bit = devices // 2
    other = xor_permute(queries[0, 0], "batch", bit)
    far_row = xor_permute(init_cache[0], "batch", 4 * stride)
    side_row = xor_permute(init_cache[0], "batch", stride)
    loaded = fetch([in_hbm(x) for x in sources], queries[0, 0])
    other, (query, cache_row, memory_row, new_row, residual_row) = pin(other, loaded)
    query, far = doubling(jnp.concatenate([query, other]), stride, bit)
    far, (out_row,) = pin(far, fetch([in_hbm(out_weight)], query))
    state_shapes = (
        shape((2 * BEAMS, width), f32),
        shape((2 * BEAMS, 2 * LANES), f32),
        shape((2 * BEAMS, width + LANES), bf16),
    )
    num, state, pay = call(
        functools.partial(attend_kernel, stride),
        state_shapes,
        query,
        far,
        cache_row,
        memory_row,
        new_row,
        parents,
        lengths,
        specs=[VM] * 5 + [SM] * 2,
        hold=(side_row,),
    )
    bit = stride
    while True:
        arrived = xor_permute(pay, "batch", bit)
        bit *= 2
        if bit == devices:
            break
        hold = (far_row,) if bit == 2 * stride else ()
        num, state, pay = call(merge_kernel, state_shapes, num, state, arrived, hold=hold)
        if bit == 2 * stride:
            both_row = xor_permute(pin(far_row, num)[0], "batch", stride)
    if stride == 1:
        partial = finish_project(num, state, arrived, out_row)
    else:
        attended = finish(num, state, arrived)
        stacked = jnp.concatenate(doubling(attended[None], 1, stride))
        wanted = reverse(jnp.bitwise_xor(jnp.arange(stride, dtype=jnp.int32), request), stride)
        stacked = stacked[wanted].reshape(stride, 2, BEAMS, width)
        attended = stacked.transpose(1, 2, 0, 3).reshape(2 * rows, width)
        partial = call(project_kernel, shape((rows, columns), f32), attended, out_row)
    other = xor_permute(partial, "tensor", 1)
    rows_held = (cache_row, far_row, side_row, pin(both_row, partial)[0])
    sent_row = call(
        functools.partial(select_kernel, stride),
        shape(cache_row.shape, bf16),
        *rows_held,
        parents,
        specs=[VM] * 4 + [SM],
    )
    sent_row = xor_permute(sent_row, "batch", 2 * stride)
    mine = call(add_kernel, pltpu.VMEM((1, rows, columns), bf16), partial, other, residual_row, hold=())
    near, far = doubling(mine, 1, devices, cross=True)
    hidden, activation = call(
        up_kernel,
        (shape((rows, columns), bf16), shape((rows, hidden_units), bf16)),
        near,
        far,
        up_weight,
        hold=(),
    )
    arrived = xor_permute(activation, "tensor", 1)
    before = call(
        functools.partial(down_kernel, True), shape((rows, out_columns), f32), activation, down_weight, hold=()
    )
    keep, send = call(
        functools.partial(down_kernel, False),
        (shape((rows // 2, out_columns), f32),) * 2,
        arrived,
        down_weight,
        before,
    )
    bit = 1
    while True:
        arrived = xor_permute(send, "batch", bit)
        bit *= 2
        if 2 * bit == devices:
            cache = call(
                functools.partial(place_kernel, stride),
                shape(cache_row.shape, bf16),
                *rows_held,
                sent_row,
                new_row,
                parents,
                lengths,
                specs=[VM] * 6 + [SM] * 2,
            )
            arrived, cache = pin(arrived, cache)
        total = keep + arrived
        if bit == devices:
            break
        half = total.shape[0] // 2
        keep, send = total[:half], total[half:]
    ffn_row = total.astype(bf16)
    return (hidden[None], ffn_row[None], cache[None])


def solution(mesh):
    placed = (
        P(("grp", "batch"), None, None, "tensor"),
        P(("grp", "batch"), None, None, "tensor"),
        P(None, ("grp", "batch"), None, "tensor"),
        P(None, ("grp", "batch"), None, "tensor"),
        P(None, "grp", "batch"),
        P(None, "tensor", "batch"),
        P(None, ("batch", "tensor")),
        P("batch", "tensor"),
        P(None, "grp"),
        P("grp"),
    )
    return jax.shard_map(
        body,
        mesh=mesh,
        in_specs=placed,
        out_specs=(
            P(None, "grp", "batch"),
            P(None, ("grp", "batch"), "tensor"),
            P(("grp", "batch"), None, None, "tensor"),
        ),
        check_vma=False,
    )
```
